32 devices in a mesh: start: 2 (over core), pencil: 16 (over z, y, x).
Axes of the slice: x: 2, y: 2, z: 4, core: 2. Of those that a mesh axis runs over, the one named last changes fastest.
Arguments:
- template: bfloat16 [64, 64, 512], P('pencil', 'start'), parts along dimension 1, may hold values from -3.5 to 3.5
- reference_image: bfloat16 [64, 64, 512], P('pencil', 'start'), parts along dimension 1, may hold values from -3.5 to 3.5
- velocity: float32 [6, 64, 32, 512], P('start', 'pencil'), parts along dimension 0, may hold values from -4 to 4
- dep_owner: int32 [4, 4096], P('start', 'pencil'), parts along dimension 0, may hold values from 0 to 15, as said below
- dep_offset: int32 [4, 4096], P('start', 'pencil'), parts along dimension 0, may hold values from 0 to 255, as said below
- dep_weight: int32 [4, 4096], P('start', 'pencil'), parts along dimension 0, may hold values from 0 to 15
Outputs:
- warped: bfloat16 [64, 64, 512], P('pencil', 'start'), parts along dimension 1
- gradient: float32 [6, 64, 32, 512], P('start', 'pencil'), parts along dimension 0
The draws below stay inside these ranges and needn't reach their ends.
There are 2 independent parts, one for each index of `start`. The reference program is written for one: setup_inputs(seed, part) draws one part's arguments, and reference() takes and returns one part's arrays. A program takes and returns all parts, laid end to end along the dimension named above; each array names one. Nothing has to cross between parts.
Inputs may be any that keep to these rules, and one draw needn't show every extreme that they name: Device d holds blocks d * 256 to (d + 1) * 256 - 1. For a block of device d, dep_owner is (d + m) mod 16 with m one of -2, -1, 0, 1, so that its stencil rows lie on devices d - 2 to d + 2 (modulo 16). dep_offset = r P + g with P as in the reference program, g the block's own in-row number and r < 4; r >= 1 where m = -2.
All inputs are finite; a program needn't handle non-finite values.
Results may differ from the reference program's by a relative error of at most 0.012.
Values may be sent and summed in bfloat16 or wider, within the bound.
A program may use at most 192 MiB of HBM per device.

```python
import math
import jax
import jax.numpy as jnp
from jax import lax

ROWS = 4
NZ = 32
NY = 512
ZB = 2
SEG = 128
Q = 16
NX = 64
BLK_DEV = 256
N_PENCIL = 16


def rough_field(key):
    grid_field = jax.random.normal(key, (NX, NZ, NY), jnp.float32)
    return jnp.clip(grid_field, -3.5, 3.5).astype(jnp.bfloat16)


def draw_template(key, part):
    return rough_field(jax.random.fold_in(key, 3))


def draw_reference_image(key, part):
    return rough_field(jax.random.fold_in(key, 5))


def departures(key):
    owners = []
    offsets = []
    levels = []
    per_row = NZ // ZB * (NY // SEG)
    device_ids = jnp.arange(N_PENCIL, dtype=jnp.int32)[:, None]
    own_place = (jnp.arange(BLK_DEV, dtype=jnp.int32) % per_row)[None, :]
    for section_index in range(2):
        section_key = jax.random.fold_in(key, 17 + section_index)
        device_keys = jax.random.split(jax.random.fold_in(section_key, 2), N_PENCIL)
        block_order = jax.vmap(lambda device_key: jax.random.permutation(device_key, BLK_DEV))(device_keys)
        move = (block_order % 4).astype(jnp.int32) - 2
        block_owner = (device_ids + move + N_PENCIL) % N_PENCIL
        row_any = jax.random.randint(jax.random.fold_in(section_key, 4), (N_PENCIL, BLK_DEV), 0, ROWS)
        row_spill = jax.random.randint(jax.random.fold_in(section_key, 5), (N_PENCIL, BLK_DEV), 1, ROWS)
        start_row = jnp.where(move == -2, row_spill, row_any)
        offset = start_row * per_row + own_place
        weight_level = jax.random.randint(jax.random.fold_in(section_key, 8), (N_PENCIL, BLK_DEV), 0, Q)
        owners.append(block_owner.reshape(-1).astype(jnp.int32))
        offsets.append(offset.reshape(-1).astype(jnp.int32))
        levels.append(weight_level.reshape(-1).astype(jnp.int32))
    return (jnp.stack(owners), jnp.stack(offsets), jnp.stack(levels))


def draw_dep_owner(key, part):
    return departures(jax.random.fold_in(key, 11))[0]


def draw_dep_offset(key, part):
    return departures(jax.random.fold_in(key, 11))[1]


def draw_dep_weight(key, part):
    return departures(jax.random.fold_in(key, 11))[2]


def shard_levels(own_key, extent, cuts, smallest, high):
    loudness = 1.0
    for axis_at, shards_of in cuts:
        heights = jax.random.uniform(jax.random.fold_in(jax.random.fold_in(own_key, 6), axis_at), (shards_of,), jnp.float32, smallest / len(cuts), high / len(cuts))
        loudness = loudness * jnp.repeat(jnp.exp(heights), extent[axis_at] // shards_of).reshape((-1,) + (1,) * (len(extent) - 1 - axis_at))
    return loudness


def centred(own_key, extent, spread, reach, cuts=(), kind=jnp.bfloat16):
    drawn = jax.random.normal(own_key, extent, jnp.float32) * spread
    if len(cuts) > 0:
        drawn = shard_levels(own_key, extent, cuts, -0.22, 0.18) * drawn
    return jnp.clip(drawn, min=-reach, max=reach).astype(kind)


def setup_inputs(seed: int = 0, part: int = 0) -> dict:
    arg_keys = jax.random.split(jax.random.key(seed), 7)
    own_keys = jax.random.split(jax.random.fold_in(arg_keys[6], part), 7)
    return {
        "template": draw_template(jax.random.fold_in(jax.random.fold_in(arg_keys[6], part), 71), part),
        "reference_image": draw_reference_image(jax.random.fold_in(jax.random.fold_in(arg_keys[6], part), 71), part),
        "velocity": centred(own_keys[2], (3, NX, NZ, NY), 1.0, 4.0, ((1, 16),), jnp.float32),
        "dep_owner": draw_dep_owner(jax.random.fold_in(jax.random.fold_in(arg_keys[6], part), 71), part),
        "dep_offset": draw_dep_offset(jax.random.fold_in(jax.random.fold_in(arg_keys[6], part), 71), part),
        "dep_weight": draw_dep_weight(jax.random.fold_in(jax.random.fold_in(arg_keys[6], part), 71), part),
    }


h1_weight = 64.0
force_gain = 32.0


def dft_tables(length):
    series = jnp.arange(length, dtype=jnp.int32)
    product = (series[:, None] * series[None, :]) % length
    angles = product.astype(jnp.float32) * (2.0 * math.pi / length)
    return jnp.cos(angles).astype(jnp.bfloat16), jnp.sin(angles).astype(jnp.bfloat16)


def wave_numbers(length):
    series = jnp.arange(length, dtype=jnp.int32)
    signed = jnp.where(series < length // 2, series, series - length)
    signed = jnp.where(series == length // 2, 0, signed)
    return signed.astype(jnp.float32) * (2.0 * math.pi / length)


def cubic_table(levels):
    fraction = (jnp.arange(levels, dtype=jnp.float32) + 0.5) / levels
    node_left = -fraction * (fraction - 1.0) * (fraction - 2.0) / 6.0
    node_zero = (fraction + 1.0) * (fraction - 1.0) * (fraction - 2.0) / 2.0
    node_one = -(fraction + 1.0) * fraction * (fraction - 2.0) / 2.0
    node_two = (fraction + 1.0) * fraction * (fraction - 1.0) / 6.0
    return jnp.stack([node_left, node_zero, node_one, node_two], axis=1)


def transport(grid_field, block_owner, offset, weight_level, weight_table):
    z_groups = NZ // ZB
    y_groups = NY // SEG
    per_row = z_groups * y_groups
    blocks = grid_field.reshape(NX, z_groups, ZB, y_groups, SEG).transpose(0, 1, 3, 2, 4).reshape(NX * per_row, ZB, SEG)
    base_row = block_owner * ROWS + offset // per_row
    remainder = offset % per_row
    tap_rows = (base_row[:, None] + jnp.arange(4, dtype=jnp.int32)[None, :]) % NX
    picked = blocks[tap_rows * per_row + remainder[:, None]].astype(jnp.float32)
    weights = weight_table[weight_level]
    mixed = jnp.sum(weights[:, :, None, None] * picked, axis=1).astype(jnp.bfloat16)
    return mixed.reshape(NX, z_groups, y_groups, ZB, SEG).transpose(0, 1, 3, 2, 4).reshape(NX, NZ, NY)


def reference(template, reference_image, velocity, dep_owner, dep_offset, dep_weight):
    weight_table = cubic_table(Q)
    first_pass = transport(template, dep_owner[0], dep_offset[0], dep_weight[0], weight_table)
    warped = transport(first_pass, dep_owner[1], dep_offset[1], dep_weight[1], weight_table)
    warped_f = warped.astype(jnp.float32)
    residual = reference_image.astype(jnp.float32) - warped_f
    cos_y, sin_y = dft_tables(NY)
    cos_x, sin_x = dft_tables(NX)
    kvec_y = wave_numbers(NY)
    kvec_x = wave_numbers(NX)
    forward_y = jnp.concatenate([cos_y, -sin_y], axis=1)
    inverse_y = jnp.concatenate([cos_y, -sin_y], axis=0)
    forward_x = jnp.concatenate([cos_x, -sin_x], axis=0)
    inverse_x = jnp.concatenate([cos_x, -sin_x], axis=1)
    stack_x = jnp.concatenate([cos_x, sin_x], axis=0)

    spec_y = jnp.dot(warped.reshape(-1, NY), forward_y, preferred_element_type=jnp.float32)
    spec_y = spec_y.astype(jnp.bfloat16).astype(jnp.float32)
    coef_y = jnp.concatenate([-kvec_y * spec_y[:, NY:], kvec_y * spec_y[:, :NY]], axis=1).astype(jnp.bfloat16)
    slope_y = (jnp.dot(coef_y, inverse_y, preferred_element_type=jnp.float32) / NY).reshape(NX, NZ, NY)

    spec_x = jnp.dot(forward_x, warped.reshape(NX, NZ * NY), preferred_element_type=jnp.float32)
    coef_x = jnp.concatenate([-kvec_x[:, None] * spec_x[NX:], kvec_x[:, None] * spec_x[:NX]], axis=0).astype(jnp.bfloat16)
    slope_x = (jnp.dot(inverse_x, coef_x, preferred_element_type=jnp.float32) / NX).astype(jnp.bfloat16).reshape(NX, NZ, NY)

    slope_z = (jnp.roll(warped_f, -1, axis=1) - jnp.roll(warped_f, 1, axis=1)) * 0.5
    force = (jnp.stack([slope_x.astype(jnp.float32), slope_y, slope_z]) * residual[None]).astype(jnp.bfloat16)
    spec_f = jnp.dot(force.reshape(-1, NY), forward_y, preferred_element_type=jnp.float32)
    spec_f = spec_f.astype(jnp.bfloat16).reshape(3, NX, NZ, 2, NY)
    spectral_gain = force_gain / (NX * NY * (1.0 + h1_weight * (kvec_x[:, None] * kvec_x[:, None] + kvec_y[None, :] * kvec_y[None, :])))

    def smooth_component(component):
        halves = jnp.dot(stack_x, component.reshape(NX, -1), preferred_element_type=jnp.float32).reshape(2, NX, NZ, 2, NY)
        real_f = halves[0, :, :, 0] + halves[1, :, :, 1]
        imag_f = halves[0, :, :, 1] - halves[1, :, :, 0]
        scaled = jnp.stack([real_f * spectral_gain[:, None, :], imag_f * spectral_gain[:, None, :]], axis=2).astype(jnp.bfloat16)
        inverse_halves = jnp.dot(stack_x, scaled.reshape(NX, -1), preferred_element_type=jnp.float32).reshape(2, NX, NZ, 2, NY)
        real_b = inverse_halves[0, :, :, 0] - inverse_halves[1, :, :, 1]
        imag_b = inverse_halves[0, :, :, 1] + inverse_halves[1, :, :, 0]
        mixed = jnp.stack([real_b, imag_b], axis=2).astype(jnp.bfloat16)
        return jnp.dot(mixed.reshape(-1, 2 * NY), inverse_y, preferred_element_type=jnp.float32).reshape(NX, NZ, NY)

    smoothed = lax.map(smooth_component, spec_f)
    gradient = velocity + smoothed
    return warped, gradient
```

```python
import functools
import math

import jax
import jax.numpy as jnp
import numpy as np
from jax import lax
from jax.experimental import pallas as pl
from jax.experimental.pallas import tpu as pltpu
from jax.sharding import PartitionSpec as P

ZB = 2
SEG = 128
Q = 16


h1_weight = 64.0
force_gain = 32.0


def shifted(x, axis, by):
    length = lax.axis_size(axis)
    return lax.ppermute(x, axis, [(i, (i + by) % length) for i in range(length)])


def dft_tables(length):
    series = jnp.arange(length, dtype=jnp.int32)
    product = series[:, None] * series[None, :] % length
    angles = product.astype(jnp.float32) * (2.0 * math.pi / length)
    return (jnp.cos(angles).astype(jnp.bfloat16), jnp.sin(angles).astype(jnp.bfloat16))


def signed_waves(series, length):
    signed = jnp.where(series < length // 2, series, series - length)
    signed = jnp.where(series == length // 2, 0, signed)
    return signed.astype(jnp.float32) * (2.0 * math.pi / length)


def wave_numbers(length):
    return signed_waves(jnp.arange(length, dtype=jnp.int32), length)


def cubic_table(levels):
    fraction = (jnp.arange(levels, dtype=jnp.float32) + 0.5) / levels
    node_left = -fraction * (fraction - 1.0) * (fraction - 2.0) / 6.0
    node_zero = (fraction + 1.0) * (fraction - 1.0) * (fraction - 2.0) / 2.0
    node_one = -(fraction + 1.0) * fraction * (fraction - 2.0) / 2.0
    node_two = (fraction + 1.0) * fraction * (fraction - 1.0) / 6.0
    return jnp.stack([node_left, node_zero, node_one, node_two], axis=1)


def pick_weights(weight_level, weight_table):
    onehot = (
        weight_level[:, None] == jnp.arange(weight_table.shape[0], dtype=jnp.int32)[None, :]
    ).astype(jnp.float32)
    return jnp.dot(onehot, weight_table, precision=lax.Precision.HIGHEST)


def general(template, reference_image, velocity, dep_owner, dep_offset, dep_weight):
    peer_count = lax.axis_size("pencil")
    row_count, plane_count, y_count = template.shape
    full_rows = row_count * peer_count
    z_groups = plane_count // ZB
    y_groups = y_count // SEG
    per_row = z_groups * y_groups
    block_count = row_count * per_row
    cell_count = plane_count * y_count
    weight_table = cubic_table(Q)
    my_index = lax.axis_index("pencil")
    shaped = template.reshape(row_count, z_groups, ZB, y_groups, SEG)
    blocks = shaped.transpose(0, 1, 3, 2, 4).reshape(block_count, ZB * SEG)
    for section_index in range(2):
        pieces = []
        for distance in (2, 1, 0, -1, -2):
            if distance == 0:
                pieces.append(blocks)
            else:
                pieces.append(shifted(blocks, "pencil", distance))
        window = jnp.concatenate(pieces, axis=0)
        relative = (dep_owner[section_index] - my_index + peer_count) % peer_count
        move = jnp.where(relative >= peer_count - 2, relative - peer_count, relative)
        offset = dep_offset[section_index]
        start_row = offset // per_row
        place = offset % per_row
        tap_row = (
            (move[:, None] + 2) * row_count
            + start_row[:, None]
            + jnp.arange(4, dtype=jnp.int32)[None, :]
        )
        taps = window[tap_row * per_row + place[:, None]].astype(jnp.float32)
        weights = pick_weights(dep_weight[section_index], weight_table)
        blocks = jnp.sum(weights[:, :, None] * taps, axis=1).astype(jnp.bfloat16)
    shaped = blocks.reshape(row_count, z_groups, y_groups, ZB, SEG)
    warped = shaped.transpose(0, 1, 3, 2, 4).reshape(row_count, plane_count, y_count)
    warped_f = warped.astype(jnp.float32)
    residual = reference_image.astype(jnp.float32) - warped_f
    cos_y, sin_y = dft_tables(y_count)
    cos_x, sin_x = dft_tables(full_rows)
    kvec_y = wave_numbers(y_count)
    kvec_x = wave_numbers(full_rows)
    forward_y = jnp.concatenate([cos_y, -sin_y], axis=1)
    inverse_y = jnp.concatenate([cos_y, -sin_y], axis=0)
    forward_x = jnp.concatenate([cos_x, -sin_x], axis=0)
    inverse_x = jnp.concatenate([cos_x, -sin_x], axis=1)
    spec_y = jnp.dot(warped.reshape(-1, y_count), forward_y, preferred_element_type=jnp.float32)
    spec_y = spec_y.astype(jnp.bfloat16).astype(jnp.float32)
    coef_y = jnp.concatenate(
        [-kvec_y * spec_y[:, y_count:], kvec_y * spec_y[:, :y_count]], axis=1
    ).astype(jnp.bfloat16)
    slope_y = (jnp.dot(coef_y, inverse_y, preferred_element_type=jnp.float32) / y_count).reshape(
        row_count, plane_count, y_count
    )
    flat_warp = warped.reshape(1, row_count, cell_count)
    spec_x = jnp.einsum(
        "kx,ixm->ikm",
        forward_x,
        lax.all_to_all(flat_warp, "pencil", split_axis=2, concat_axis=1, tiled=True),
        preferred_element_type=jnp.float32,
    )
    coef_x = jnp.concatenate(
        [
            -kvec_x[None, :, None] * spec_x[:, full_rows:],
            kvec_x[None, :, None] * spec_x[:, :full_rows],
        ],
        axis=1,
    ).astype(jnp.bfloat16)
    slope = (
        jnp.einsum("xk,ikm->ixm", inverse_x, coef_x, preferred_element_type=jnp.float32) / full_rows
    ).astype(jnp.bfloat16)
    slope_x = lax.all_to_all(slope, "pencil", split_axis=1, concat_axis=2, tiled=True)
    slope_x = slope_x.reshape(row_count, plane_count, y_count)
    slope_z = (jnp.roll(warped_f, -1, axis=1) - jnp.roll(warped_f, 1, axis=1)) * 0.5
    force = (jnp.stack([slope_x.astype(jnp.float32), slope_y, slope_z]) * residual[None]).astype(
        jnp.bfloat16
    )
    force_lines = force.reshape(-1, y_count)
    spec_real = jnp.dot(force_lines, cos_y, preferred_element_type=jnp.float32).astype(jnp.bfloat16)
    spec_imag = jnp.dot(force_lines, -sin_y, preferred_element_type=jnp.float32).astype(
        jnp.bfloat16
    )
    spec_f = jnp.stack(
        [spec_real.reshape(3, row_count, cell_count), spec_imag.reshape(3, row_count, cell_count)],
        axis=1,
    )
    planes = lax.all_to_all(spec_f, "pencil", split_axis=3, concat_axis=2, tiled=True)
    local_cols = planes.shape[3]
    column_ids = my_index * local_cols + jnp.arange(local_cols, dtype=jnp.int32)
    kvec_local = signed_waves(column_ids % y_count, y_count)
    spectral_gain = force_gain / (
        full_rows
        * y_count
        * (
            1.0
            + h1_weight
            * (kvec_x[:, None] * kvec_x[:, None] + kvec_local[None, :] * kvec_local[None, :])
        )
    )
    cos_part = jnp.einsum("kx,chxm->chkm", cos_x, planes, preferred_element_type=jnp.float32)
    sin_part = jnp.einsum("kx,chxm->chkm", sin_x, planes, preferred_element_type=jnp.float32)
    real_f = cos_part[:, 0] + sin_part[:, 1]
    imag_f = cos_part[:, 1] - sin_part[:, 0]
    scale_grid = spectral_gain[None]
    scaled = jnp.stack([real_f * scale_grid, imag_f * scale_grid], axis=1).astype(jnp.bfloat16)
    cos_back = jnp.einsum("xk,chkm->chxm", cos_x, scaled, preferred_element_type=jnp.float32)
    sin_back = jnp.einsum("xk,chkm->chxm", sin_x, scaled, preferred_element_type=jnp.float32)
    real_b = cos_back[:, 0] - sin_back[:, 1]
    imag_b = cos_back[:, 1] + sin_back[:, 0]
    mixed = jnp.stack([real_b, imag_b], axis=1).astype(jnp.bfloat16)
    smoothed = lax.all_to_all(mixed, "pencil", split_axis=2, concat_axis=3, tiled=True)
    spatial = jnp.dot(
        smoothed[:, 0].reshape(-1, y_count), cos_y, preferred_element_type=jnp.float32
    )
    spatial = spatial - jnp.dot(
        smoothed[:, 1].reshape(-1, y_count), sin_y, preferred_element_type=jnp.float32
    )
    gradient = velocity + spatial.reshape(3, row_count, plane_count, y_count)
    return (warped, gradient)


def split_pair(values):
    high = values.astype(jnp.bfloat16)
    low = (values - np.asarray(high, np.float64)).astype(jnp.bfloat16)
    return [high, low]


def real_dft(length):
    half = length // 2
    waves = np.concatenate([np.arange(half + 1), np.arange(1, half)])
    angle = 2.0 * np.pi * ((np.arange(length)[:, None] * waves[None, :]) % length) / length
    table = np.where(np.arange(length)[None, :] <= half, np.cos(angle), np.sin(angle))
    factor = np.where((waves == 0) | (waves == half), 1.0, 2.0)
    k = np.where(waves == half, 0, waves) * (2.0 * np.pi / length)
    return table, (table * factor[None, :]).T, k


def derivative(length):
    series = np.arange(length)
    angle = 2.0 * np.pi * ((series[:, None] * series[None, :]) % length) / length
    cos, sin = np.cos(angle), np.sin(angle)
    k = np.where(series < length // 2, series, series - length)
    k = np.where(series == length // 2, 0, k) * (2.0 * np.pi / length)
    return ((sin * k) @ cos - (cos * k) @ sin) / length


@functools.lru_cache(None)
def tables(n, rows, planes, ny):
    nx = n * rows
    m = nx * ZB
    index = np.arange(m)
    line_x = index // (ZB * rows) * rows + index % rows
    line_z = index // rows % ZB
    wide = np.arange(2 * m)
    wide_dev = wide // (2 * ZB * rows)
    wide_half = wide // (ZB * rows) % 2
    wide_z = wide // rows % ZB
    wide_row = wide % rows
    slab = wide_half * m + wide_row * planes + wide_dev * ZB + wide_z
    line = wide_half * m + wide_dev * (ZB * rows) + wide_z * rows + wide_row
    eye = np.eye(2 * m)
    to_message = eye[slab]
    from_message = eye[slab].T
    line_message = eye[line]
    line_second = eye[line].T[m:]
    wide_x = np.where(wide_half == 0, wide_dev * rows + wide_row, 8 * nx)
    first_x = np.where(line_z[:, None] == wide_z[None, :], wide_x[None, :], 8 * nx)
    second_x = np.where(line_z[:, None] == line_z[None, :], line_x[None, :], 8 * nx)
    same_z = line_z[:, None] == line_z[None, :]
    dx = derivative(nx)[line_x[None, :], line_x[:, None]] * same_z
    dy = derivative(ny)
    plane_last = np.zeros((nx, m))
    plane_first = np.zeros((nx, m))
    plane_last[line_x[line_z == ZB - 1], index[line_z == ZB - 1]] = 1.0
    plane_first[line_x[line_z == 0], index[line_z == 0]] = 1.0
    dz = np.zeros((m, 2 * m))
    for r in range(m):
        x, z = line_x[r], line_z[r]
        for step, sign in ((1, 0.5), (-1, -0.5)):
            if z + step < 0:
                column = m + x
            elif z + step >= ZB:
                column = m + nx + x
            else:
                column = int(np.nonzero((line_x == x) & (line_z == z + step))[0][0])
            dz[r, column] += sign
    fx, bx, kx = real_dft(nx)
    fy, by, ky = real_dft(ny)
    out_z = index // nx
    out_k = index % nx
    forward = fx.T[out_k][:, line_x] * (out_z[:, None] == line_z[None, :])
    backward = bx.T[line_x][:, out_k] * (line_z[:, None] == out_z[None, :])
    gain = force_gain / (
        nx * ny * (1.0 + h1_weight * (kx[out_k][:, None] ** 2 + ky[None, :] ** 2))
    )
    per = ny // SEG
    groups = planes // ZB
    lanes = np.arange(rows * groups * per)
    lane_row = lanes // (groups * per)
    lane_group = lanes // per % groups
    code_mask = (lane_group[None, :] == (index // (ZB * rows))[:, None]) & (
        lane_row[None, :] == (index % rows)[:, None]
    )
    code_spread = np.zeros((4, lanes.size, 128))
    for j in range(4):
        code_spread[j, lanes, j * per + lanes % per] = 1.0
    b16 = lambda t: np.asarray(t, np.float64).astype(jnp.bfloat16)
    f32 = lambda t: np.asarray(t, np.float32)
    return (
        b16(to_message),
        b16(from_message),
        b16(line_message),
        b16(line_second),
        f32(first_x),
        f32(second_x),
        *split_pair(dx),
        *split_pair(dy),
        b16(np.concatenate([plane_last, plane_first])),
        b16(dz),
        b16(forward),
        b16(backward),
        b16(fy),
        b16(by),
        f32(gain),
        b16(code_mask),
        b16(code_spread),
    )


def dot(a, b):
    return jnp.dot(a, b, preferred_element_type=jnp.float32)


def body(
    n,
    template_ref,
    image_ref,
    velocity_ref,
    code_ref,
    to_message,
    from_message,
    line_message,
    line_second,
    first_x,
    second_x,
    dx_high,
    dx_low,
    dy_high,
    dy_low,
    planes_out,
    dz,
    forward_x,
    backward_x,
    forward_y,
    backward_y,
    gain,
    code_mask,
    code_spread,
    warped_ref,
    gradient_ref,
    code_send,
    code_recv,
    image_send,
    image_recv,
    halo_send,
    halo_recv,
    back_send,
    back_recv,
    code_sems,
    image_sems,
    halo_sems,
    back_sems,
):
    me = lax.axis_index("pencil")
    rows, planes, ny = template_ref.shape
    m = n * rows * ZB
    nx = n * rows
    per = ny // SEG
    half = ny // 2
    after = lax.rem(me + 1, n)
    before = lax.rem(me + n - 1, n)

    barrier = pltpu.get_barrier_semaphore()

    def greet(off, carry):
        pl.semaphore_signal(
            barrier,
            inc=1,
            device_id={"pencil": lax.rem(me + off, n)},
            device_id_type=pl.DeviceIdType.MESH,
        )
        return carry

    lax.fori_loop(1, n, greet, 0)

    def copy(send, recv, sems, off, slot):
        return pltpu.make_async_remote_copy(
            src_ref=send.at[lax.rem(me + off, n)],
            dst_ref=recv.at[slot],
            send_sem=sems.at[0, off],
            recv_sem=sems.at[1, off],
            device_id={"pencil": lax.rem(me + off, n)},
            device_id_type=pl.DeviceIdType.MESH,
        )

    def scatter(send, recv, sems):
        def step(off, carry):
            copy(send, recv, sems, off, me).start()
            return carry

        lax.fori_loop(1, n, step, 0)
        recv[me] = send[me]

    def collect(send, recv, sems):
        def step(off, carry):
            copy(send, recv, sems, off, lax.rem(me + n - off, n)).wait_recv()
            return carry

        lax.fori_loop(1, n, step, 0)

    def drain(send, recv, sems):
        def step(off, carry):
            copy(send, recv, sems, off, me).wait_send()
            return carry

        lax.fori_loop(1, n, step, 0)

    codes = jnp.zeros((m, 128), jnp.float32)
    for j in range(4):
        codes += dot(code_mask[...] * code_ref[j : j + 1, :], code_spread[j])
    code_send[...] = codes.reshape(n, ZB * rows, 128)
    both = jnp.concatenate(
        [template_ref[...].reshape(m, ny), image_ref[...].reshape(m, ny)], axis=0
    )
    image_send[...] = (
        dot(to_message[...], both).astype(jnp.bfloat16).reshape(n, 2 * ZB * rows, ny)
    )
    pl.semaphore_wait(barrier, n - 1)
    scatter(code_send, code_recv, code_sems)
    scatter(image_send, image_recv, image_sems)

    collect(code_send, code_recv, code_sems)
    code = code_recv[...].reshape(m, 128)
    t = (code + 0.5) / Q
    weights = (
        -t * (t - 1.0) * (t - 2.0) / 6.0,
        (t + 1.0) * (t - 1.0) * (t - 2.0) / 2.0,
        -(t + 1.0) * t * (t - 2.0) / 2.0,
        (t + 1.0) * t * (t - 1.0) / 6.0,
    )

    def stencil(section, group, place):
        at = section * per + group
        delta = place - code[:, at : at + 1]
        delta = jnp.where(delta < 0.0, delta + nx, delta)
        at = 2 * per + at
        taps = jnp.zeros_like(delta)
        for k in range(4):
            taps = jnp.where(delta == float(k), weights[k][:, at : at + 1], taps)
        high = taps.astype(jnp.bfloat16)
        low = (taps - high.astype(jnp.float32)).astype(jnp.bfloat16)
        return high, low

    first = [stencil(0, g, first_x[...]) for g in range(per)]
    collect(image_send, image_recv, image_sems)
    images = image_recv[...].reshape(2 * m, ny)
    warped = []
    for g in range(per):
        high, low = first[g]
        seg = images[:, g * SEG : (g + 1) * SEG]
        seg = (dot(high, seg) + dot(low, seg)).astype(jnp.bfloat16)
        high, low = stencil(1, g, second_x[...])
        warped.append((dot(high, seg) + dot(low, seg)).astype(jnp.bfloat16))
    warped = jnp.concatenate(warped, axis=1)

    halo_send[...] = dot(planes_out[...], warped).astype(jnp.bfloat16).reshape(2, nx, ny)
    halos = [
        pltpu.make_async_remote_copy(
            src_ref=halo_send.at[side],
            dst_ref=halo_recv.at[side],
            send_sem=halo_sems.at[0, side],
            recv_sem=halo_sems.at[1, side],
            device_id={"pencil": (after, before)[side]},
            device_id_type=pl.DeviceIdType.MESH,
        )
        for side in range(2)
    ]
    for halo in halos:
        halo.start()

    def send_back(slot, value):
        stacked = jnp.concatenate([value[:, :half], value[:, half:]], axis=0)
        message = dot(line_message[...], stacked).astype(jnp.bfloat16)
        back_send[slot] = message.reshape(n, 2 * ZB * rows, half)
        scatter(back_send.at[slot], back_recv.at[slot], back_sems.at[slot])

    send_back(0, warped)
    residual = dot(line_second[...], images) - warped.astype(jnp.float32)

    def smooth(slot, slope):
        force = (slope * residual).astype(jnp.bfloat16)
        spectrum = dot(force, forward_y[...]).astype(jnp.bfloat16)
        spectrum = (dot(forward_x[...], spectrum) * gain[...]).astype(jnp.bfloat16)
        spectrum = dot(backward_x[...], spectrum).astype(jnp.bfloat16)
        send_back(slot, dot(spectrum, backward_y[...]).astype(jnp.bfloat16))

    smooth(1, dot(dx_high[...], warped) + dot(dx_low[...], warped))
    smooth(2, dot(warped, dy_high[...]) + dot(warped, dy_low[...]))
    for halo in halos:
        halo.wait_recv()
    smooth(
        3, dot(dz[...], jnp.concatenate([warped, halo_recv[0], halo_recv[1]], axis=0))
    )

    for slot in range(4):
        collect(back_send.at[slot], back_recv.at[slot], back_sems.at[slot])
        home = dot(from_message[...], back_recv[slot].reshape(2 * m, half))
        home = jnp.concatenate([home[:m], home[m:]], axis=1).reshape(rows, planes, ny)
        if slot == 0:
            warped_ref[...] = home.astype(jnp.bfloat16)
        else:
            gradient_ref[slot - 1] = velocity_ref[slot - 1] + home

    drain(code_send, code_recv, code_sems)
    drain(image_send, image_recv, image_sems)
    for halo in halos:
        halo.wait_send()
    for slot in range(4):
        drain(back_send.at[slot], back_recv.at[slot], back_sems.at[slot])


def by_groups(template, reference_image, velocity, dep_owner, dep_offset, dep_weight):
    n = lax.axis_size("pencil")
    rows, planes, ny = template.shape
    per_row = planes // ZB * (ny // SEG)
    m = n * rows * ZB
    base = (dep_owner * rows + dep_offset // per_row) % (n * rows)
    codes = jnp.concatenate([base, dep_weight], axis=0).astype(jnp.bfloat16)
    constants = [jnp.asarray(t) for t in tables(n, rows, planes, ny)]
    vmem = pl.BlockSpec(memory_space=pltpu.VMEM)
    b16, f32 = jnp.bfloat16, jnp.float32
    return pl.pallas_call(
        functools.partial(body, n),
        out_shape=(
            jax.ShapeDtypeStruct(template.shape, b16),
            jax.ShapeDtypeStruct(velocity.shape, f32),
        ),
        in_specs=[vmem] * (4 + len(constants)),
        out_specs=(vmem, vmem),
        scratch_shapes=[
            pltpu.VMEM((n, ZB * rows, 128), f32),
            pltpu.VMEM((n, ZB * rows, 128), f32),
            pltpu.VMEM((n, 2 * ZB * rows, ny), b16),
            pltpu.VMEM((n, 2 * ZB * rows, ny), b16),
            pltpu.VMEM((2, n * rows, ny), b16),
            pltpu.VMEM((2, n * rows, ny), b16),
            pltpu.VMEM((4, n, 2 * ZB * rows, ny // 2), b16),
            pltpu.VMEM((4, n, 2 * ZB * rows, ny // 2), b16),
            pltpu.SemaphoreType.DMA((2, n)),
            pltpu.SemaphoreType.DMA((2, n)),
            pltpu.SemaphoreType.DMA((2, 2)),
            pltpu.SemaphoreType.DMA((4, 2, n)),
        ],
        compiler_params=pltpu.CompilerParams(
            collective_id=0, has_side_effects=True, vmem_limit_bytes=40 * 1024 * 1024
        ),
        cost_estimate=pl.CostEstimate(
            flops=24 * m * ny * ny, bytes_accessed=8 * m * ny * 4, transcendentals=0
        ),
    )(template, reference_image, velocity, codes, *constants)


def local(template, *others):
    n = lax.axis_size("pencil")
    rows, planes, _ = template.shape
    if n > 2 and planes == n * ZB and rows * ZB == 8 and n * rows <= 256:
        return by_groups(template, *others)
    return general(template, *others)


def solution(mesh):
    in_specs = (
        P("pencil", "start", None),
        P("pencil", "start", None),
        P("start", "pencil", None, None),
        P("start", "pencil"),
        P("start", "pencil"),
        P("start", "pencil"),
    )
    out_specs = (P("pencil", "start", None), P("start", "pencil", None, None))
    return jax.shard_map(local, mesh=mesh, in_specs=in_specs, out_specs=out_specs, check_vma=False)
```

```python
import functools
import math

import jax
import jax.numpy as jnp
import numpy as np
from jax import lax
from jax.experimental import pallas as pl
from jax.experimental.pallas import tpu as pltpu
from jax.sharding import PartitionSpec as P

ZB = 2
SEG = 128
Q = 16


h1_weight = 64.0
force_gain = 32.0


def shifted(x, axis, by):
    length = lax.axis_size(axis)
    return lax.ppermute(x, axis, [(i, (i + by) % length) for i in range(length)])


def dft_tables(length):
    series = jnp.arange(length, dtype=jnp.int32)
    product = series[:, None] * series[None, :] % length
    angles = product.astype(jnp.float32) * (2.0 * math.pi / length)
    return (jnp.cos(angles).astype(jnp.bfloat16), jnp.sin(angles).astype(jnp.bfloat16))


def signed_waves(series, length):
    signed = jnp.where(series < length // 2, series, series - length)
    signed = jnp.where(series == length // 2, 0, signed)
    return signed.astype(jnp.float32) * (2.0 * math.pi / length)


def wave_numbers(length):
    return signed_waves(jnp.arange(length, dtype=jnp.int32), length)


def cubic_table(levels):
    fraction = (jnp.arange(levels, dtype=jnp.float32) + 0.5) / levels
    node_left = -fraction * (fraction - 1.0) * (fraction - 2.0) / 6.0
    node_zero = (fraction + 1.0) * (fraction - 1.0) * (fraction - 2.0) / 2.0
    node_one = -(fraction + 1.0) * fraction * (fraction - 2.0) / 2.0
    node_two = (fraction + 1.0) * fraction * (fraction - 1.0) / 6.0
    return jnp.stack([node_left, node_zero, node_one, node_two], axis=1)


def pick_weights(weight_level, weight_table):
    onehot = (
        weight_level[:, None] == jnp.arange(weight_table.shape[0], dtype=jnp.int32)[None, :]
    ).astype(jnp.float32)
    return jnp.dot(onehot, weight_table, precision=lax.Precision.HIGHEST)


def general(template, reference_image, velocity, dep_owner, dep_offset, dep_weight):
    peer_count = lax.axis_size("pencil")
    row_count, plane_count, y_count = template.shape
    full_rows = row_count * peer_count
    z_groups = plane_count // ZB
    y_groups = y_count // SEG
    per_row = z_groups * y_groups
    block_count = row_count * per_row
    cell_count = plane_count * y_count
    weight_table = cubic_table(Q)
    my_index = lax.axis_index("pencil")
    shaped = template.reshape(row_count, z_groups, ZB, y_groups, SEG)
    blocks = shaped.transpose(0, 1, 3, 2, 4).reshape(block_count, ZB * SEG)
    for section_index in range(2):
        pieces = []
        for distance in (2, 1, 0, -1, -2):
            if distance == 0:
                pieces.append(blocks)
            else:
                pieces.append(shifted(blocks, "pencil", distance))
        window = jnp.concatenate(pieces, axis=0)
        relative = (dep_owner[section_index] - my_index + peer_count) % peer_count
        move = jnp.where(relative >= peer_count - 2, relative - peer_count, relative)
        offset = dep_offset[section_index]
        start_row = offset // per_row
        place = offset % per_row
        tap_row = (
            (move[:, None] + 2) * row_count
            + start_row[:, None]
            + jnp.arange(4, dtype=jnp.int32)[None, :]
        )
        taps = window[tap_row * per_row + place[:, None]].astype(jnp.float32)
        weights = pick_weights(dep_weight[section_index], weight_table)
        blocks = jnp.sum(weights[:, :, None] * taps, axis=1).astype(jnp.bfloat16)
    shaped = blocks.reshape(row_count, z_groups, y_groups, ZB, SEG)
    warped = shaped.transpose(0, 1, 3, 2, 4).reshape(row_count, plane_count, y_count)
    warped_f = warped.astype(jnp.float32)
    residual = reference_image.astype(jnp.float32) - warped_f
    cos_y, sin_y = dft_tables(y_count)
    cos_x, sin_x = dft_tables(full_rows)
    kvec_y = wave_numbers(y_count)
    kvec_x = wave_numbers(full_rows)
    forward_y = jnp.concatenate([cos_y, -sin_y], axis=1)
    inverse_y = jnp.concatenate([cos_y, -sin_y], axis=0)
    forward_x = jnp.concatenate([cos_x, -sin_x], axis=0)
    inverse_x = jnp.concatenate([cos_x, -sin_x], axis=1)
    spec_y = jnp.dot(warped.reshape(-1, y_count), forward_y, preferred_element_type=jnp.float32)
    spec_y = spec_y.astype(jnp.bfloat16).astype(jnp.float32)
    coef_y = jnp.concatenate(
        [-kvec_y * spec_y[:, y_count:], kvec_y * spec_y[:, :y_count]], axis=1
    ).astype(jnp.bfloat16)
    slope_y = (jnp.dot(coef_y, inverse_y, preferred_element_type=jnp.float32) / y_count).reshape(
        row_count, plane_count, y_count
    )
    flat_warp = warped.reshape(1, row_count, cell_count)
    spec_x = jnp.einsum(
        "kx,ixm->ikm",
        forward_x,
        lax.all_to_all(flat_warp, "pencil", split_axis=2, concat_axis=1, tiled=True),
        preferred_element_type=jnp.float32,
    )
    coef_x = jnp.concatenate(
        [
            -kvec_x[None, :, None] * spec_x[:, full_rows:],
            kvec_x[None, :, None] * spec_x[:, :full_rows],
        ],
        axis=1,
    ).astype(jnp.bfloat16)
    slope = (
        jnp.einsum("xk,ikm->ixm", inverse_x, coef_x, preferred_element_type=jnp.float32) / full_rows
    ).astype(jnp.bfloat16)
    slope_x = lax.all_to_all(slope, "pencil", split_axis=1, concat_axis=2, tiled=True)
    slope_x = slope_x.reshape(row_count, plane_count, y_count)
    slope_z = (jnp.roll(warped_f, -1, axis=1) - jnp.roll(warped_f, 1, axis=1)) * 0.5
    force = (jnp.stack([slope_x.astype(jnp.float32), slope_y, slope_z]) * residual[None]).astype(
        jnp.bfloat16
    )
    force_lines = force.reshape(-1, y_count)
    spec_real = jnp.dot(force_lines, cos_y, preferred_element_type=jnp.float32).astype(jnp.bfloat16)
    spec_imag = jnp.dot(force_lines, -sin_y, preferred_element_type=jnp.float32).astype(
        jnp.bfloat16
    )
    spec_f = jnp.stack(
        [spec_real.reshape(3, row_count, cell_count), spec_imag.reshape(3, row_count, cell_count)],
        axis=1,
    )
    planes = lax.all_to_all(spec_f, "pencil", split_axis=3, concat_axis=2, tiled=True)
    local_cols = planes.shape[3]
    column_ids = my_index * local_cols + jnp.arange(local_cols, dtype=jnp.int32)
    kvec_local = signed_waves(column_ids % y_count, y_count)
    spectral_gain = force_gain / (
        full_rows
        * y_count
        * (
            1.0
            + h1_weight
            * (kvec_x[:, None] * kvec_x[:, None] + kvec_local[None, :] * kvec_local[None, :])
        )
    )
    cos_part = jnp.einsum("kx,chxm->chkm", cos_x, planes, preferred_element_type=jnp.float32)
    sin_part = jnp.einsum("kx,chxm->chkm", sin_x, planes, preferred_element_type=jnp.float32)
    real_f = cos_part[:, 0] + sin_part[:, 1]
    imag_f = cos_part[:, 1] - sin_part[:, 0]
    scale_grid = spectral_gain[None]
    scaled = jnp.stack([real_f * scale_grid, imag_f * scale_grid], axis=1).astype(jnp.bfloat16)
    cos_back = jnp.einsum("xk,chkm->chxm", cos_x, scaled, preferred_element_type=jnp.float32)
    sin_back = jnp.einsum("xk,chkm->chxm", sin_x, scaled, preferred_element_type=jnp.float32)
    real_b = cos_back[:, 0] - sin_back[:, 1]
    imag_b = cos_back[:, 1] + sin_back[:, 0]
    mixed = jnp.stack([real_b, imag_b], axis=1).astype(jnp.bfloat16)
    smoothed = lax.all_to_all(mixed, "pencil", split_axis=2, concat_axis=3, tiled=True)
    spatial = jnp.dot(
        smoothed[:, 0].reshape(-1, y_count), cos_y, preferred_element_type=jnp.float32
    )
    spatial = spatial - jnp.dot(
        smoothed[:, 1].reshape(-1, y_count), sin_y, preferred_element_type=jnp.float32
    )
    gradient = velocity + spatial.reshape(3, row_count, plane_count, y_count)
    return (warped, gradient)


def split_pair(values):
    high = values.astype(jnp.bfloat16)
    low = (values - np.asarray(high, np.float64)).astype(jnp.bfloat16)
    return [high, low]


def real_dft(length):
    half = length // 2
    waves = np.concatenate([np.arange(half + 1), np.arange(1, half)])
    angle = 2.0 * np.pi * ((np.arange(length)[:, None] * waves[None, :]) % length) / length
    table = np.where(np.arange(length)[None, :] <= half, np.cos(angle), np.sin(angle))
    factor = np.where((waves == 0) | (waves == half), 1.0, 2.0)
    k = np.where(waves == half, 0, waves) * (2.0 * np.pi / length)
    return table, (table * factor[None, :]).T, k


def derivative(length):
    series = np.arange(length)
    angle = 2.0 * np.pi * ((series[:, None] * series[None, :]) % length) / length
    cos, sin = np.cos(angle), np.sin(angle)
    k = np.where(series < length // 2, series, series - length)
    k = np.where(series == length // 2, 0, k) * (2.0 * np.pi / length)
    return ((sin * k) @ cos - (cos * k) @ sin) / length


@functools.lru_cache(None)
def tables(n, rows, planes, ny):
    nx = n * rows
    m = nx * ZB
    index = np.arange(m)
    line_x = index // (ZB * rows) * rows + index % rows
    line_z = index // rows % ZB
    wide = np.arange(2 * m)
    wide_dev = wide // (2 * ZB * rows)
    wide_half = wide // (ZB * rows) % 2
    wide_z = wide // rows % ZB
    wide_row = wide % rows
    slab = wide_half * m + wide_row * planes + wide_dev * ZB + wide_z
    line = wide_half * m + wide_dev * (ZB * rows) + wide_z * rows + wide_row
    eye = np.eye(2 * m)
    to_message = eye[slab]
    from_message = eye[slab].T
    line_message = eye[line]
    wide_x = wide_dev * rows + wide_row
    first_x = [
        np.where(
            (line_z[:, None] == wide_z[None, :]) & (wide_half == h)[None, :],
            wide_x[None, :],
            8 * nx,
        )
        for h in range(2)
    ]
    second_x = np.where(line_z[:, None] == line_z[None, :], line_x[None, :], 8 * nx)
    same_z = line_z[:, None] == line_z[None, :]
    dx = derivative(nx)[line_x[None, :], line_x[:, None]] * same_z
    dy = derivative(ny)
    plane_last = np.zeros((nx, m))
    plane_first = np.zeros((nx, m))
    plane_last[line_x[line_z == ZB - 1], index[line_z == ZB - 1]] = 1.0
    plane_first[line_x[line_z == 0], index[line_z == 0]] = 1.0
    dz = np.zeros((m, 2 * m))
    for r in range(m):
        x, z = line_x[r], line_z[r]
        for step, sign in ((1, 0.5), (-1, -0.5)):
            if z + step < 0:
                column = m + x
            elif z + step >= ZB:
                column = m + nx + x
            else:
                column = int(np.nonzero((line_x == x) & (line_z == z + step))[0][0])
            dz[r, column] += sign
    fx, bx, kx = real_dft(nx)
    fy, by, ky = real_dft(ny)
    out_z = index // nx
    out_k = index % nx
    forward = fx.T[out_k][:, line_x] * (out_z[:, None] == line_z[None, :])
    backward = bx.T[line_x][:, out_k] * (line_z[:, None] == out_z[None, :])
    gain = force_gain / (
        nx * ny * (1.0 + h1_weight * (kx[out_k][:, None] ** 2 + ky[None, :] ** 2))
    )
    per = ny // SEG
    groups = planes // ZB
    lanes = np.arange(rows * groups * per)
    lane_row = lanes // (groups * per)
    lane_group = lanes // per % groups
    code_mask = (lane_group[None, :] == (index // (ZB * rows))[:, None]) & (
        lane_row[None, :] == (index % rows)[:, None]
    )
    code_spread = np.zeros((4, lanes.size, 128))
    for j in range(4):
        code_spread[j, lanes, j * per + lanes % per] = 1.0
    b16 = lambda t: np.asarray(t, np.float64).astype(jnp.bfloat16)
    f32 = lambda t: np.asarray(t, np.float32)
    return {
        "early": b16(np.concatenate([to_message, code_mask])),
        "spread": b16(code_spread),
        "first": f32(first_x),
        "second": f32(second_x),
        "lines": b16(np.concatenate([line_message, line_message.T, to_message.T, dz])),
        "ends": b16(np.concatenate([plane_last, plane_first])),
        "dx": np.concatenate([*split_pair(dx)]),
        "dy": np.concatenate([*split_pair(dy)]),
        "x": b16(np.concatenate([forward, backward])),
        "fy": b16(fy),
        "by": b16(by),
        "gain": f32(gain),
    }


def dot(a, b):
    return jnp.dot(a, b, preferred_element_type=jnp.float32)


def body(n, names, template_hbm, image_hbm, owner_hbm, offset_hbm, level_hbm, *refs):
    tables_hbm = refs[: len(names)]
    (out_ref,) = refs[len(names) : len(names) + 1]
    refs = refs[len(names) + 1 :]
    template_ref, image_ref, owner_ref, offset_ref, level_ref = refs[:5]
    table = dict(zip(names, refs[5 : 5 + len(names)]))
    (
        code_send,
        code_recv,
        image_send,
        image_recv,
        halo_send,
        halo_recv,
        back_send,
        back_recv,
        load_sems,
        code_sems,
        image_sems,
        halo_sems,
        back_sems,
    ) = refs[5 + len(names) :]
    sources = (template_hbm, image_hbm, owner_hbm, offset_hbm, level_hbm) + tables_hbm
    targets = refs[: 5 + len(names)]
    loads = {
        key: pltpu.make_async_copy(source, target, load_sems.at[at])
        for at, (key, source, target) in enumerate(
            zip(("template", "image", "owner", "offset", "level") + names, sources, targets)
        )
    }
    order = ("template", "early", "owner", "offset", "level", "spread", "image")
    for key in order + tuple(key for key in names if key not in order):
        loads[key].start()

    def loaded(*keys):
        for key in keys:
            loads[key].wait()

    me = lax.axis_index("pencil")
    rows, planes, ny = template_ref.shape
    m = n * rows * ZB
    nx = n * rows
    per = ny // SEG
    half = ny // 2
    after = lax.rem(me + 1, n)
    before = lax.rem(me + n - 1, n)

    barrier = pltpu.get_barrier_semaphore()

    def greet(off, carry):
        pl.semaphore_signal(
            barrier,
            inc=1,
            device_id={"pencil": lax.rem(me + off, n)},
            device_id_type=pl.DeviceIdType.MESH,
        )
        return carry

    lax.fori_loop(1, n, greet, 0)

    def copy(send, recv, sems, off, slot):
        return pltpu.make_async_remote_copy(
            src_ref=send.at[lax.rem(me + off, n)],
            dst_ref=recv.at[slot],
            send_sem=sems.at[0, off],
            recv_sem=sems.at[1, off],
            device_id={"pencil": lax.rem(me + off, n)},
            device_id_type=pl.DeviceIdType.MESH,
        )

    def scatter(send, recv, sems):
        def step(off, carry):
            copy(send, recv, sems, off, me).start()
            return carry

        lax.fori_loop(1, n, step, 0)
        recv[me] = send[me]

    def collect(send, recv, sems):
        def step(off, carry):
            copy(send, recv, sems, off, lax.rem(me + n - off, n)).wait_recv()
            return carry

        lax.fori_loop(1, n, step, 0)

    def drain(send, recv, sems):
        def step(off, carry):
            copy(send, recv, sems, off, me).wait_send()
            return carry

        lax.fori_loop(1, n, step, 0)

    def sort_image(slot, ref):
        value = ref[...].reshape(m, ny)
        stacked = jnp.concatenate([value[:, :half], value[:, half:]], axis=0)
        message = dot(table["early"][: 2 * m], stacked).astype(jnp.bfloat16)
        image_send[slot] = message.reshape(n, 2 * ZB * rows, half)

    loaded("template", "early")
    sort_image(0, template_ref)
    loaded("owner", "offset", "level", "spread")
    shift = (planes // ZB * per).bit_length() - 1
    base = owner_ref[...] * rows + lax.shift_right_logical(
        offset_ref[...], jnp.full(offset_ref.shape, shift, jnp.int32)
    )
    base = base.astype(jnp.float32)
    level = level_ref[...].astype(jnp.float32)
    mask = table["early"][2 * m :].astype(jnp.float32)
    codes = jnp.zeros((m, 128), jnp.float32)
    for j, line in enumerate((base[0:1], base[1:2], level[0:1], level[1:2])):
        codes += dot((mask * line).astype(jnp.bfloat16), table["spread"][j])
    code_send[...] = codes.reshape(n, ZB * rows, 128)
    pl.semaphore_wait(barrier, n - 1)
    scatter(code_send, code_recv, code_sems)
    scatter(image_send.at[0], image_recv.at[0], image_sems.at[0])
    loaded("image")
    sort_image(1, image_ref)
    scatter(image_send.at[1], image_recv.at[1], image_sems.at[1])

    collect(code_send, code_recv, code_sems)
    code = code_recv[...].reshape(m, 128)
    t = (code + 0.5) / Q
    weights = (
        -t * (t - 1.0) * (t - 2.0) / 6.0,
        (t + 1.0) * (t - 1.0) * (t - 2.0) / 2.0,
        -(t + 1.0) * t * (t - 2.0) / 2.0,
        (t + 1.0) * t * (t - 1.0) / 6.0,
    )

    def stencil(section, group, place):
        at = section * per + group
        delta = place - code[:, at : at + 1]
        delta = jnp.where(delta < 0.0, delta + nx, delta)
        at = 2 * per + at
        taps = jnp.zeros_like(delta)
        for k in range(4):
            taps = jnp.where(delta == float(k), weights[k][:, at : at + 1], taps)
        high = taps.astype(jnp.bfloat16)
        low = (taps - high.astype(jnp.float32)).astype(jnp.bfloat16)
        return high, low

    loaded("first", "second")
    first = [stencil(0, g, table["first"][g * SEG // half]) for g in range(per)]
    second = [stencil(1, g, table["second"][...]) for g in range(per)]
    collect(image_send.at[0], image_recv.at[0], image_sems.at[0])
    template = image_recv[0].reshape(2 * m, half)
    warped = []
    for g in range(per):
        at = g * SEG % half
        seg = template[:, at : at + SEG]
        high, low = first[g]
        seg = (dot(high, seg) + dot(low, seg)).astype(jnp.bfloat16)
        high, low = second[g]
        warped.append((dot(high, seg) + dot(low, seg)).astype(jnp.bfloat16))
    warped = jnp.concatenate(warped, axis=1)

    loaded("ends", "lines")
    halo_send[...] = dot(table["ends"][...], warped).astype(jnp.bfloat16).reshape(2, nx, ny)
    halos = [
        pltpu.make_async_remote_copy(
            src_ref=halo_send.at[side],
            dst_ref=halo_recv.at[side],
            send_sem=halo_sems.at[0, side],
            recv_sem=halo_sems.at[1, side],
            device_id={"pencil": (after, before)[side]},
            device_id_type=pl.DeviceIdType.MESH,
        )
        for side in range(2)
    ]
    for halo in halos:
        halo.start()

    def send_back(slot, value):
        stacked = jnp.concatenate([value[:, :half], value[:, half:]], axis=0)
        message = dot(table["lines"][: 2 * m], stacked).astype(jnp.bfloat16)
        back_send[slot] = message.reshape(n, 2 * ZB * rows, half)
        scatter(back_send.at[slot], back_recv.at[slot], back_sems.at[slot])

    send_back(0, warped)
    loaded("dx", "dy", "x", "fy", "by", "gain")
    slope_x = dot(table["dx"][:m], warped) + dot(table["dx"][m:], warped)
    collect(image_send.at[1], image_recv.at[1], image_sems.at[1])
    image = dot(table["lines"][2 * m : 4 * m], image_recv[1].reshape(2 * m, half))
    image = jnp.concatenate([image[:m], image[m:]], axis=1)
    residual = image - warped.astype(jnp.float32)

    def smooth(slot, slope):
        force = (slope * residual).astype(jnp.bfloat16)
        spectrum = dot(force, table["fy"][...]).astype(jnp.bfloat16)
        spectrum = dot(table["x"][:m], spectrum) * table["gain"][...]
        spectrum = dot(table["x"][m:], spectrum.astype(jnp.bfloat16)).astype(jnp.bfloat16)
        send_back(slot, dot(spectrum, table["by"][...]).astype(jnp.bfloat16))

    smooth(1, slope_x)
    smooth(2, dot(warped, table["dy"][:ny]) + dot(warped, table["dy"][ny:]))
    for halo in halos:
        halo.wait_recv()
    near = jnp.concatenate([warped, halo_recv[0], halo_recv[1]], axis=0)
    smooth(3, dot(table["lines"][6 * m :], near))

    for slot in range(4):
        collect(back_send.at[slot], back_recv.at[slot], back_sems.at[slot])
        home = dot(table["lines"][4 * m : 6 * m], back_recv[slot].reshape(2 * m, half))
        home = jnp.concatenate([home[:m], home[m:]], axis=1).astype(jnp.bfloat16)
        out_ref[slot] = home.reshape(rows, planes, ny)

    drain(code_send, code_recv, code_sems)
    for slot in range(2):
        drain(image_send.at[slot], image_recv.at[slot], image_sems.at[slot])
    for halo in halos:
        halo.wait_send()
    for slot in range(4):
        drain(back_send.at[slot], back_recv.at[slot], back_sems.at[slot])


def by_groups(template, reference_image, velocity, dep_owner, dep_offset, dep_weight):
    n = lax.axis_size("pencil")
    rows, planes, ny = template.shape
    m = n * rows * ZB
    held = tables(n, rows, planes, ny)
    names = tuple(held)
    constants = [jnp.asarray(held[name]) for name in names]
    operands = (template, reference_image, dep_owner, dep_offset, dep_weight, *constants)
    b16, f32 = jnp.bfloat16, jnp.float32
    message = (n, 2 * ZB * rows, ny // 2)
    out = pl.pallas_call(
        functools.partial(body, n, names),
        out_shape=jax.ShapeDtypeStruct((4,) + template.shape, b16),
        in_specs=[pl.BlockSpec(memory_space=pltpu.HBM)] * len(operands),
        out_specs=pl.BlockSpec(memory_space=pltpu.VMEM),
        scratch_shapes=[pltpu.VMEM(array.shape, array.dtype) for array in operands]
        + [
            pltpu.VMEM((n, ZB * rows, 128), f32),
            pltpu.VMEM((n, ZB * rows, 128), f32),
            pltpu.VMEM((2,) + message, b16),
            pltpu.VMEM((2,) + message, b16),
            pltpu.VMEM((2, n * rows, ny), b16),
            pltpu.VMEM((2, n * rows, ny), b16),
            pltpu.VMEM((4,) + message, b16),
            pltpu.VMEM((4,) + message, b16),
            pltpu.SemaphoreType.DMA((len(operands),)),
            pltpu.SemaphoreType.DMA((2, n)),
            pltpu.SemaphoreType.DMA((2, 2, n)),
            pltpu.SemaphoreType.DMA((2, 2)),
            pltpu.SemaphoreType.DMA((4, 2, n)),
        ],
        compiler_params=pltpu.CompilerParams(
            collective_id=0, has_side_effects=True, vmem_limit_bytes=60 * 1024 * 1024
        ),
        cost_estimate=pl.CostEstimate(
            flops=24 * m * ny * ny, bytes_accessed=8 * m * ny * 4, transcendentals=0
        ),
    )(*operands)
    return out[0], velocity + out[1:].astype(f32)


def local(template, *others):
    n = lax.axis_size("pencil")
    rows, planes, ny = template.shape
    per_row = planes // ZB * (ny // SEG)
    whole = planes == n * ZB and ny % (2 * SEG) == 0 and per_row & (per_row - 1) == 0
    if n > 2 and whole and rows * ZB == 8 and n * rows <= 256:
        return by_groups(template, *others)
    return general(template, *others)


def solution(mesh):
    in_specs = (
        P("pencil", "start", None),
        P("pencil", "start", None),
        P("start", "pencil", None, None),
        P("start", "pencil"),
        P("start", "pencil"),
        P("start", "pencil"),
    )
    out_specs = (P("pencil", "start", None), P("start", "pencil", None, None))
    return jax.shard_map(local, mesh=mesh, in_specs=in_specs, out_specs=out_specs, check_vma=False)
```

```python
import functools
import math

import jax
import jax.numpy as jnp
import numpy as np
from jax import lax
from jax.experimental import pallas as pl
from jax.experimental.pallas import tpu as pltpu
from jax.sharding import PartitionSpec as P

ZB = 2
SEG = 128
Q = 16


h1_weight = 64.0
force_gain = 32.0


def shifted(x, axis, by):
    length = lax.axis_size(axis)
    return lax.ppermute(x, axis, [(i, (i + by) % length) for i in range(length)])


def dft_tables(length):
    series = jnp.arange(length, dtype=jnp.int32)
    product = series[:, None] * series[None, :] % length
    angles = product.astype(jnp.float32) * (2.0 * math.pi / length)
    return (jnp.cos(angles).astype(jnp.bfloat16), jnp.sin(angles).astype(jnp.bfloat16))


def signed_waves(series, length):
    signed = jnp.where(series < length // 2, series, series - length)
    signed = jnp.where(series == length // 2, 0, signed)
    return signed.astype(jnp.float32) * (2.0 * math.pi / length)


def wave_numbers(length):
    return signed_waves(jnp.arange(length, dtype=jnp.int32), length)


def cubic_table(levels):
    fraction = (jnp.arange(levels, dtype=jnp.float32) + 0.5) / levels
    node_left = -fraction * (fraction - 1.0) * (fraction - 2.0) / 6.0
    node_zero = (fraction + 1.0) * (fraction - 1.0) * (fraction - 2.0) / 2.0
    node_one = -(fraction + 1.0) * fraction * (fraction - 2.0) / 2.0
    node_two = (fraction + 1.0) * fraction * (fraction - 1.0) / 6.0
    return jnp.stack([node_left, node_zero, node_one, node_two], axis=1)


def pick_weights(weight_level, weight_table):
    onehot = (
        weight_level[:, None] == jnp.arange(weight_table.shape[0], dtype=jnp.int32)[None, :]
    ).astype(jnp.float32)
    return jnp.dot(onehot, weight_table, precision=lax.Precision.HIGHEST)


def general(template, reference_image, velocity, dep_owner, dep_offset, dep_weight):
    peer_count = lax.axis_size("pencil")
    row_count, plane_count, y_count = template.shape
    full_rows = row_count * peer_count
    z_groups = plane_count // ZB
    y_groups = y_count // SEG
    per_row = z_groups * y_groups
    block_count = row_count * per_row
    cell_count = plane_count * y_count
    weight_table = cubic_table(Q)
    my_index = lax.axis_index("pencil")
    shaped = template.reshape(row_count, z_groups, ZB, y_groups, SEG)
    blocks = shaped.transpose(0, 1, 3, 2, 4).reshape(block_count, ZB * SEG)
    for section_index in range(2):
        pieces = []
        for distance in (2, 1, 0, -1, -2):
            if distance == 0:
                pieces.append(blocks)
            else:
                pieces.append(shifted(blocks, "pencil", distance))
        window = jnp.concatenate(pieces, axis=0)
        relative = (dep_owner[section_index] - my_index + peer_count) % peer_count
        move = jnp.where(relative >= peer_count - 2, relative - peer_count, relative)
        offset = dep_offset[section_index]
        start_row = offset // per_row
        place = offset % per_row
        tap_row = (
            (move[:, None] + 2) * row_count
            + start_row[:, None]
            + jnp.arange(4, dtype=jnp.int32)[None, :]
        )
        taps = window[tap_row * per_row + place[:, None]].astype(jnp.float32)
        weights = pick_weights(dep_weight[section_index], weight_table)
        blocks = jnp.sum(weights[:, :, None] * taps, axis=1).astype(jnp.bfloat16)
    shaped = blocks.reshape(row_count, z_groups, y_groups, ZB, SEG)
    warped = shaped.transpose(0, 1, 3, 2, 4).reshape(row_count, plane_count, y_count)
    warped_f = warped.astype(jnp.float32)
    residual = reference_image.astype(jnp.float32) - warped_f
    cos_y, sin_y = dft_tables(y_count)
    cos_x, sin_x = dft_tables(full_rows)
    kvec_y = wave_numbers(y_count)
    kvec_x = wave_numbers(full_rows)
    forward_y = jnp.concatenate([cos_y, -sin_y], axis=1)
    inverse_y = jnp.concatenate([cos_y, -sin_y], axis=0)
    forward_x = jnp.concatenate([cos_x, -sin_x], axis=0)
    inverse_x = jnp.concatenate([cos_x, -sin_x], axis=1)
    spec_y = jnp.dot(warped.reshape(-1, y_count), forward_y, preferred_element_type=jnp.float32)
    spec_y = spec_y.astype(jnp.bfloat16).astype(jnp.float32)
    coef_y = jnp.concatenate(
        [-kvec_y * spec_y[:, y_count:], kvec_y * spec_y[:, :y_count]], axis=1
    ).astype(jnp.bfloat16)
    slope_y = (jnp.dot(coef_y, inverse_y, preferred_element_type=jnp.float32) / y_count).reshape(
        row_count, plane_count, y_count
    )
    flat_warp = warped.reshape(1, row_count, cell_count)
    spec_x = jnp.einsum(
        "kx,ixm->ikm",
        forward_x,
        lax.all_to_all(flat_warp, "pencil", split_axis=2, concat_axis=1, tiled=True),
        preferred_element_type=jnp.float32,
    )
    coef_x = jnp.concatenate(
        [
            -kvec_x[None, :, None] * spec_x[:, full_rows:],
            kvec_x[None, :, None] * spec_x[:, :full_rows],
        ],
        axis=1,
    ).astype(jnp.bfloat16)
    slope = (
        jnp.einsum("xk,ikm->ixm", inverse_x, coef_x, preferred_element_type=jnp.float32) / full_rows
    ).astype(jnp.bfloat16)
    slope_x = lax.all_to_all(slope, "pencil", split_axis=1, concat_axis=2, tiled=True)
    slope_x = slope_x.reshape(row_count, plane_count, y_count)
    slope_z = (jnp.roll(warped_f, -1, axis=1) - jnp.roll(warped_f, 1, axis=1)) * 0.5
    force = (jnp.stack([slope_x.astype(jnp.float32), slope_y, slope_z]) * residual[None]).astype(
        jnp.bfloat16
    )
    force_lines = force.reshape(-1, y_count)
    spec_real = jnp.dot(force_lines, cos_y, preferred_element_type=jnp.float32).astype(jnp.bfloat16)
    spec_imag = jnp.dot(force_lines, -sin_y, preferred_element_type=jnp.float32).astype(
        jnp.bfloat16
    )
    spec_f = jnp.stack(
        [spec_real.reshape(3, row_count, cell_count), spec_imag.reshape(3, row_count, cell_count)],
        axis=1,
    )
    planes = lax.all_to_all(spec_f, "pencil", split_axis=3, concat_axis=2, tiled=True)
    local_cols = planes.shape[3]
    column_ids = my_index * local_cols + jnp.arange(local_cols, dtype=jnp.int32)
    kvec_local = signed_waves(column_ids % y_count, y_count)
    spectral_gain = force_gain / (
        full_rows
        * y_count
        * (
            1.0
            + h1_weight
            * (kvec_x[:, None] * kvec_x[:, None] + kvec_local[None, :] * kvec_local[None, :])
        )
    )
    cos_part = jnp.einsum("kx,chxm->chkm", cos_x, planes, preferred_element_type=jnp.float32)
    sin_part = jnp.einsum("kx,chxm->chkm", sin_x, planes, preferred_element_type=jnp.float32)
    real_f = cos_part[:, 0] + sin_part[:, 1]
    imag_f = cos_part[:, 1] - sin_part[:, 0]
    scale_grid = spectral_gain[None]
    scaled = jnp.stack([real_f * scale_grid, imag_f * scale_grid], axis=1).astype(jnp.bfloat16)
    cos_back = jnp.einsum("xk,chkm->chxm", cos_x, scaled, preferred_element_type=jnp.float32)
    sin_back = jnp.einsum("xk,chkm->chxm", sin_x, scaled, preferred_element_type=jnp.float32)
    real_b = cos_back[:, 0] - sin_back[:, 1]
    imag_b = cos_back[:, 1] + sin_back[:, 0]
    mixed = jnp.stack([real_b, imag_b], axis=1).astype(jnp.bfloat16)
    smoothed = lax.all_to_all(mixed, "pencil", split_axis=2, concat_axis=3, tiled=True)
    spatial = jnp.dot(
        smoothed[:, 0].reshape(-1, y_count), cos_y, preferred_element_type=jnp.float32
    )
    spatial = spatial - jnp.dot(
        smoothed[:, 1].reshape(-1, y_count), sin_y, preferred_element_type=jnp.float32
    )
    gradient = velocity + spatial.reshape(3, row_count, plane_count, y_count)
    return (warped, gradient)


def split_pair(values):
    high = values.astype(jnp.bfloat16)
    low = (values - np.asarray(high, np.float64)).astype(jnp.bfloat16)
    return [high, low]


def real_dft(length):
    half = length // 2
    waves = np.concatenate([np.arange(half + 1), np.arange(1, half)])
    angle = 2.0 * np.pi * ((np.arange(length)[:, None] * waves[None, :]) % length) / length
    table = np.where(np.arange(length)[None, :] <= half, np.cos(angle), np.sin(angle))
    factor = np.where((waves == 0) | (waves == half), 1.0, 2.0)
    k = np.where(waves == half, 0, waves) * (2.0 * np.pi / length)
    return table, (table * factor[None, :]).T, k


def derivative(length):
    series = np.arange(length)
    angle = 2.0 * np.pi * ((series[:, None] * series[None, :]) % length) / length
    cos, sin = np.cos(angle), np.sin(angle)
    k = np.where(series < length // 2, series, series - length)
    k = np.where(series == length // 2, 0, k) * (2.0 * np.pi / length)
    return ((sin * k) @ cos - (cos * k) @ sin) / length


@functools.lru_cache(None)
def tables(n, rows, planes, ny):
    nx = n * rows
    m = nx * ZB
    index = np.arange(m)
    line_x = index // (ZB * rows) * rows + index % rows
    line_z = index // rows % ZB
    wide = np.arange(2 * m)
    wide_dev = wide // (2 * ZB * rows)
    wide_half = wide // (ZB * rows) % 2
    wide_z = wide // rows % ZB
    wide_row = wide % rows
    slab = wide_half * m + wide_row * planes + wide_dev * ZB + wide_z
    line = wide_half * m + wide_dev * (ZB * rows) + wide_z * rows + wide_row
    eye = np.eye(2 * m)
    to_message = eye[slab]
    from_message = eye[slab].T
    line_message = eye[line]
    wide_x = wide_dev * rows + wide_row
    first_x = [
        np.where(
            (line_z[:, None] == wide_z[None, :]) & (wide_half == h)[None, :],
            wide_x[None, :],
            8 * nx,
        )
        for h in range(2)
    ]
    second_x = np.where(line_z[:, None] == line_z[None, :], line_x[None, :], 8 * nx)
    same_z = line_z[:, None] == line_z[None, :]
    dx = derivative(nx)[line_x[None, :], line_x[:, None]] * same_z
    dy = derivative(ny)
    plane_last = np.zeros((nx, m))
    plane_first = np.zeros((nx, m))
    plane_last[line_x[line_z == ZB - 1], index[line_z == ZB - 1]] = 1.0
    plane_first[line_x[line_z == 0], index[line_z == 0]] = 1.0
    dz = np.zeros((m, 2 * m))
    for r in range(m):
        x, z = line_x[r], line_z[r]
        for step, sign in ((1, 0.5), (-1, -0.5)):
            if z + step < 0:
                column = m + x
            elif z + step >= ZB:
                column = m + nx + x
            else:
                column = int(np.nonzero((line_x == x) & (line_z == z + step))[0][0])
            dz[r, column] += sign
    fx, bx, kx = real_dft(nx)
    fy, by, ky = real_dft(ny)
    out_z = index // nx
    out_k = index % nx
    forward = fx.T[out_k][:, line_x] * (out_z[:, None] == line_z[None, :])
    backward = bx.T[line_x][:, out_k] * (line_z[:, None] == out_z[None, :])
    gain = force_gain / (
        nx * ny * (1.0 + h1_weight * (kx[out_k][:, None] ** 2 + ky[None, :] ** 2))
    )
    per = ny // SEG
    groups = planes // ZB
    lanes = np.arange(rows * groups * per)
    lane_row = lanes // (groups * per)
    lane_group = lanes // per % groups
    code_mask = (lane_group[None, :] == (index // (ZB * rows))[:, None]) & (
        lane_row[None, :] == (index % rows)[:, None]
    )
    code_spread = np.zeros((4, lanes.size, 128))
    for j in range(4):
        code_spread[j, lanes, j * per + lanes % per] = 1.0
    b16 = lambda t: np.asarray(t, np.float64).astype(jnp.bfloat16)
    f32 = lambda t: np.asarray(t, np.float32)
    return {
        "early": b16(np.concatenate([to_message, code_mask])),
        "spread": b16(code_spread),
        "first": f32(first_x),
        "second": f32(second_x),
        "lines": b16(np.concatenate([line_message, line_message.T, dz])),
        "ends": b16(np.concatenate([plane_last, plane_first])),
        "dx": np.concatenate(split_pair(dx)),
        "dy": np.concatenate(split_pair(dy)),
        "x": b16(np.concatenate([forward, backward])),
        "fy": b16(fy),
        "by": b16(by),
        "gain": f32(gain),
    }, b16(to_message.T)


def dot(a, b):
    return jnp.dot(a, b, preferred_element_type=jnp.float32)


def body(n, names, template_hbm, image_hbm, owner_hbm, offset_hbm, level_hbm, *refs):
    tables_hbm = refs[: len(names)]
    (back_recv,) = refs[len(names) : len(names) + 1]
    refs = refs[len(names) + 1 :]
    template_ref, image_ref, owner_ref, offset_ref, level_ref = refs[:5]
    table = dict(zip(names, refs[5 : 5 + len(names)]))
    (
        code_send,
        code_recv,
        image_send,
        image_recv,
        halo_send,
        halo_recv,
        back_send,
        load_sems,
        code_sems,
        image_sems,
        halo_sems,
        back_sems,
        own_sems,
    ) = refs[5 + len(names) :]
    sources = (template_hbm, image_hbm, owner_hbm, offset_hbm, level_hbm) + tables_hbm
    targets = refs[: 5 + len(names)]
    loads = {
        key: pltpu.make_async_copy(source, target, load_sems.at[at])
        for at, (key, source, target) in enumerate(
            zip(("template", "image", "owner", "offset", "level") + names, sources, targets)
        )
    }
    order = ("template", "early", "owner", "offset", "level", "spread", "image")
    for key in order + tuple(key for key in names if key not in order):
        loads[key].start()

    def loaded(*keys):
        for key in keys:
            loads[key].wait()

    me = lax.axis_index("pencil")
    rows, planes, ny = template_ref.shape
    m = n * rows * ZB
    nx = n * rows
    per = ny // SEG
    half = ny // 2
    after = lax.rem(me + 1, n)
    before = lax.rem(me + n - 1, n)

    barrier = pltpu.get_barrier_semaphore()

    def greet(off, carry):
        pl.semaphore_signal(
            barrier,
            inc=1,
            device_id={"pencil": lax.rem(me + off, n)},
            device_id_type=pl.DeviceIdType.MESH,
        )
        return carry

    lax.fori_loop(1, n, greet, 0)

    def scatter(send, recv, sems):
        def step(off, carry):
            to = lax.rem(me + off, n)
            pltpu.make_async_remote_copy(
                src_ref=send.at[to],
                dst_ref=recv.at[me],
                send_sem=sems.at[0],
                recv_sem=sems.at[1],
                device_id={"pencil": to},
                device_id_type=pl.DeviceIdType.MESH,
            ).start()
            return carry

        lax.fori_loop(1, n, step, 0)

    def everything(send, recv, sems):
        return pltpu.make_async_remote_copy(
            src_ref=send.at[pl.ds(0, n - 1)],
            dst_ref=recv.at[pl.ds(0, n - 1)],
            send_sem=sems.at[0],
            recv_sem=sems.at[1],
            device_id={"pencil": after},
            device_id_type=pl.DeviceIdType.MESH,
        )

    def collect(send, recv, sems):
        everything(send, recv, sems).wait_recv()

    def drain(send, recv, sems):
        everything(send, recv, sems).wait_send()

    def sort_image(slot, ref):
        value = ref[...].reshape(m, ny)
        stacked = jnp.concatenate([value[:, :half], value[:, half:]], axis=0)
        message = dot(table["early"][: 2 * m], stacked).astype(jnp.bfloat16)
        image_send[slot] = message.reshape(n, 2 * ZB * rows, half)

    loaded("template", "early")
    sort_image(0, template_ref)
    loaded("owner", "offset", "level", "spread")
    shift = (planes // ZB * per).bit_length() - 1
    base = owner_ref[...] * rows + lax.shift_right_logical(
        offset_ref[...], jnp.full(offset_ref.shape, shift, jnp.int32)
    )
    base = base.astype(jnp.float32)
    level = level_ref[...].astype(jnp.float32)
    mask = table["early"][2 * m :].astype(jnp.float32)
    codes = jnp.zeros((m, 128), jnp.float32)
    for j, line in enumerate((base[0:1], base[1:2], level[0:1], level[1:2])):
        codes += dot((mask * line).astype(jnp.bfloat16), table["spread"][j])
    code_send[...] = codes.reshape(n, ZB * rows, 128)
    pl.semaphore_wait(barrier, n - 1)
    scatter(code_send, code_recv, code_sems)
    scatter(image_send.at[0], image_recv.at[0], image_sems.at[0])
    code_recv[me] = code_send[me]
    image_recv[0, me] = image_send[0, me]
    loaded("image")
    sort_image(1, image_ref)
    scatter(image_send.at[1], image_recv.at[1], image_sems.at[1])
    image_recv[1, me] = image_send[1, me]

    collect(code_send, code_recv, code_sems)
    code = code_recv[...].reshape(m, 128)
    t = (code + 0.5) / Q
    weights = (
        -t * (t - 1.0) * (t - 2.0) / 6.0,
        (t + 1.0) * (t - 1.0) * (t - 2.0) / 2.0,
        -(t + 1.0) * t * (t - 2.0) / 2.0,
        (t + 1.0) * t * (t - 1.0) / 6.0,
    )

    def stencil(section, group, place):
        at = section * per + group
        delta = place - code[:, at : at + 1]
        delta = jnp.where(delta < 0.0, delta + nx, delta)
        at = 2 * per + at
        taps = jnp.zeros_like(delta)
        for k in range(4):
            taps = jnp.where(delta == float(k), weights[k][:, at : at + 1], taps)
        high = taps.astype(jnp.bfloat16)
        low = (taps - high.astype(jnp.float32)).astype(jnp.bfloat16)
        return high, low

    loaded("first", "second")
    first = [stencil(0, g, table["first"][g * SEG // half]) for g in range(per)]
    second = [stencil(1, g, table["second"][...]) for g in range(per)]
    collect(image_send.at[0], image_recv.at[0], image_sems.at[0])
    template = image_recv[0].reshape(2 * m, half)
    warped = []
    for g in range(per):
        at = g * SEG % half
        seg = template[:, at : at + SEG]
        high, low = first[g]
        seg = (dot(high, seg) + dot(low, seg)).astype(jnp.bfloat16)
        high, low = second[g]
        warped.append((dot(high, seg) + dot(low, seg)).astype(jnp.bfloat16))
    warped = jnp.concatenate(warped, axis=1)

    loaded("ends", "lines")
    halo_send[...] = dot(table["ends"][...], warped).astype(jnp.bfloat16).reshape(2, nx, ny)
    halos = [
        pltpu.make_async_remote_copy(
            src_ref=halo_send.at[side],
            dst_ref=halo_recv.at[side],
            send_sem=halo_sems.at[0, side],
            recv_sem=halo_sems.at[1, side],
            device_id={"pencil": (after, before)[side]},
            device_id_type=pl.DeviceIdType.MESH,
        )
        for side in range(2)
    ]
    for halo in halos:
        halo.start()

    def own(slot):
        return pltpu.make_async_copy(
            back_send.at[slot, me], back_recv.at[slot, me], own_sems.at[slot]
        )

    def send_back(slot, value):
        stacked = jnp.concatenate([value[:, :half], value[:, half:]], axis=0)
        message = dot(table["lines"][: 2 * m], stacked).astype(jnp.bfloat16)
        back_send[slot] = message.reshape(n, 2 * ZB * rows, half)
        scatter(back_send.at[slot], back_recv.at[slot], back_sems.at[slot])
        own(slot).start()

    send_back(0, warped)
    loaded("dx", "dy", "x", "fy", "by", "gain")
    slope_x = dot(table["dx"][:m], warped) + dot(table["dx"][m:], warped)
    collect(image_send.at[1], image_recv.at[1], image_sems.at[1])
    image = dot(table["lines"][2 * m : 4 * m], image_recv[1].reshape(2 * m, half))
    image = jnp.concatenate([image[:m], image[m:]], axis=1)
    residual = image - warped.astype(jnp.float32)

    def smooth(slot, slope):
        force = (slope * residual).astype(jnp.bfloat16)
        spectrum = dot(force, table["fy"][...]).astype(jnp.bfloat16)
        spectrum = dot(table["x"][:m], spectrum) * table["gain"][...]
        spectrum = dot(table["x"][m:], spectrum.astype(jnp.bfloat16)).astype(jnp.bfloat16)
        send_back(slot, dot(spectrum, table["by"][...]).astype(jnp.bfloat16))

    smooth(1, slope_x)
    smooth(2, dot(warped, table["dy"][:ny]) + dot(warped, table["dy"][ny:]))
    for halo in halos:
        halo.wait_recv()
    near = jnp.concatenate([warped, halo_recv[0], halo_recv[1]], axis=0)
    smooth(3, dot(table["lines"][4 * m :], near))

    drain(code_send, code_recv, code_sems)
    for slot in range(2):
        drain(image_send.at[slot], image_recv.at[slot], image_sems.at[slot])
    for halo in halos:
        halo.wait_send()
    for slot in range(4):
        own(slot).wait()
        collect(back_send.at[slot], back_recv.at[slot], back_sems.at[slot])
        drain(back_send.at[slot], back_recv.at[slot], back_sems.at[slot])


def finish(
    back_hbm,
    velocity_ref,
    sort_ref,
    warped_hbm,
    gradient_hbm,
    back_ref,
    warped_ref,
    gradient_ref,
    load_sems,
    store_sems,
):
    rows, planes, ny = warped_ref.shape
    m = rows * planes
    loads = [
        pltpu.make_async_copy(back_hbm.at[slot], back_ref.at[slot], load_sems.at[slot])
        for slot in range(4)
    ]
    stores = [pltpu.make_async_copy(warped_ref, warped_hbm, store_sems.at[0])] + [
        pltpu.make_async_copy(gradient_ref.at[c], gradient_hbm.at[c], store_sems.at[1 + c])
        for c in range(3)
    ]
    for load in loads:
        load.start()
    for slot in range(4):
        loads[slot].wait()
        home = dot(sort_ref[...], back_ref[slot].reshape(2 * m, ny // 2))
        home = jnp.concatenate([home[:m], home[m:]], axis=1).reshape(rows, planes, ny)
        if slot == 0:
            warped_ref[...] = home.astype(jnp.bfloat16)
        else:
            gradient_ref[slot - 1] = velocity_ref[slot - 1] + home
        stores[slot].start()
    for store in stores:
        store.wait()


def by_groups(template, reference_image, velocity, dep_owner, dep_offset, dep_weight):
    n = lax.axis_size("pencil")
    rows, planes, ny = template.shape
    m = n * rows * ZB
    held, sort_rows = tables(n, rows, planes, ny)
    names = tuple(held)
    constants = [jnp.asarray(held[name]) for name in names]
    operands = (template, reference_image, dep_owner, dep_offset, dep_weight, *constants)
    b16, f32 = jnp.bfloat16, jnp.float32
    message = (n, 2 * ZB * rows, ny // 2)
    hbm = pl.BlockSpec(memory_space=pltpu.HBM)
    vmem = pl.BlockSpec(memory_space=pltpu.VMEM)
    back = pl.pallas_call(
        functools.partial(body, n, names),
        out_shape=jax.ShapeDtypeStruct((4,) + message, b16),
        in_specs=[hbm] * len(operands),
        out_specs=hbm,
        scratch_shapes=[pltpu.VMEM(array.shape, array.dtype) for array in operands]
        + [
            pltpu.VMEM((n, ZB * rows, 128), f32),
            pltpu.VMEM((n, ZB * rows, 128), f32),
            pltpu.VMEM((2,) + message, b16),
            pltpu.VMEM((2,) + message, b16),
            pltpu.VMEM((2, n * rows, ny), b16),
            pltpu.VMEM((2, n * rows, ny), b16),
            pltpu.VMEM((4,) + message, b16),
            pltpu.SemaphoreType.DMA((len(operands),)),
            pltpu.SemaphoreType.DMA((2,)),
            pltpu.SemaphoreType.DMA((2, 2)),
            pltpu.SemaphoreType.DMA((2, 2)),
            pltpu.SemaphoreType.DMA((4, 2)),
            pltpu.SemaphoreType.DMA((4,)),
        ],
        compiler_params=pltpu.CompilerParams(
            collective_id=0, has_side_effects=True, vmem_limit_bytes=60 * 1024 * 1024
        ),
        cost_estimate=pl.CostEstimate(
            flops=24 * m * ny * ny, bytes_accessed=8 * m * ny * 4, transcendentals=0
        ),
    )(*operands)
    return pl.pallas_call(
        finish,
        out_shape=(
            jax.ShapeDtypeStruct(template.shape, b16),
            jax.ShapeDtypeStruct(velocity.shape, f32),
        ),
        in_specs=[hbm, vmem, vmem],
        out_specs=(hbm, hbm),
        scratch_shapes=[
            pltpu.VMEM(back.shape, b16),
            pltpu.VMEM(template.shape, b16),
            pltpu.VMEM(velocity.shape, f32),
            pltpu.SemaphoreType.DMA((4,)),
            pltpu.SemaphoreType.DMA((4,)),
        ],
        compiler_params=pltpu.CompilerParams(vmem_limit_bytes=60 * 1024 * 1024),
        cost_estimate=pl.CostEstimate(
            flops=16 * m * m * ny, bytes_accessed=4 * m * ny * 8, transcendentals=0
        ),
    )(back, velocity, jnp.asarray(sort_rows))


def local(template, *others):
    n = lax.axis_size("pencil")
    rows, planes, ny = template.shape
    per_row = planes // ZB * (ny // SEG)
    whole = planes == n * ZB and ny % (2 * SEG) == 0 and per_row & (per_row - 1) == 0
    if n > 2 and whole and rows * ZB == 8 and n * rows <= 256:
        return by_groups(template, *others)
    return general(template, *others)


def solution(mesh):
    in_specs = (
        P("pencil", "start", None),
        P("pencil", "start", None),
        P("start", "pencil", None, None),
        P("start", "pencil"),
        P("start", "pencil"),
        P("start", "pencil"),
    )
    out_specs = (P("pencil", "start", None), P("start", "pencil", None, None))
    return jax.shard_map(local, mesh=mesh, in_specs=in_specs, out_specs=out_specs, check_vma=False)
```

```python
import functools
import math

import jax
import jax.numpy as jnp
import numpy as np
from jax import lax
from jax.experimental import pallas as pl
from jax.experimental.pallas import tpu as pltpu
from jax.sharding import PartitionSpec as P

ZB = 2
SEG = 128
Q = 16


h1_weight = 64.0
force_gain = 32.0


def shifted(x, axis, by):
    length = lax.axis_size(axis)
    return lax.ppermute(x, axis, [(i, (i + by) % length) for i in range(length)])


def dft_tables(length):
    series = jnp.arange(length, dtype=jnp.int32)
    product = series[:, None] * series[None, :] % length
    angles = product.astype(jnp.float32) * (2.0 * math.pi / length)
    return (jnp.cos(angles).astype(jnp.bfloat16), jnp.sin(angles).astype(jnp.bfloat16))


def signed_waves(series, length):
    signed = jnp.where(series < length // 2, series, series - length)
    signed = jnp.where(series == length // 2, 0, signed)
    return signed.astype(jnp.float32) * (2.0 * math.pi / length)


def wave_numbers(length):
    return signed_waves(jnp.arange(length, dtype=jnp.int32), length)


def cubic_table(levels):
    fraction = (jnp.arange(levels, dtype=jnp.float32) + 0.5) / levels
    node_left = -fraction * (fraction - 1.0) * (fraction - 2.0) / 6.0
    node_zero = (fraction + 1.0) * (fraction - 1.0) * (fraction - 2.0) / 2.0
    node_one = -(fraction + 1.0) * fraction * (fraction - 2.0) / 2.0
    node_two = (fraction + 1.0) * fraction * (fraction - 1.0) / 6.0
    return jnp.stack([node_left, node_zero, node_one, node_two], axis=1)


def pick_weights(weight_level, weight_table):
    onehot = (
        weight_level[:, None] == jnp.arange(weight_table.shape[0], dtype=jnp.int32)[None, :]
    ).astype(jnp.float32)
    return jnp.dot(onehot, weight_table, precision=lax.Precision.HIGHEST)


def general(template, reference_image, velocity, dep_owner, dep_offset, dep_weight):
    peer_count = lax.axis_size("pencil")
    row_count, plane_count, y_count = template.shape
    full_rows = row_count * peer_count
    z_groups = plane_count // ZB
    y_groups = y_count // SEG
    per_row = z_groups * y_groups
    block_count = row_count * per_row
    cell_count = plane_count * y_count
    weight_table = cubic_table(Q)
    my_index = lax.axis_index("pencil")
    shaped = template.reshape(row_count, z_groups, ZB, y_groups, SEG)
    blocks = shaped.transpose(0, 1, 3, 2, 4).reshape(block_count, ZB * SEG)
    for section_index in range(2):
        pieces = []
        for distance in (2, 1, 0, -1, -2):
            if distance == 0:
                pieces.append(blocks)
            else:
                pieces.append(shifted(blocks, "pencil", distance))
        window = jnp.concatenate(pieces, axis=0)
        relative = (dep_owner[section_index] - my_index + peer_count) % peer_count
        move = jnp.where(relative >= peer_count - 2, relative - peer_count, relative)
        offset = dep_offset[section_index]
        start_row = offset // per_row
        place = offset % per_row
        tap_row = (
            (move[:, None] + 2) * row_count
            + start_row[:, None]
            + jnp.arange(4, dtype=jnp.int32)[None, :]
        )
        taps = window[tap_row * per_row + place[:, None]].astype(jnp.float32)
        weights = pick_weights(dep_weight[section_index], weight_table)
        blocks = jnp.sum(weights[:, :, None] * taps, axis=1).astype(jnp.bfloat16)
    shaped = blocks.reshape(row_count, z_groups, y_groups, ZB, SEG)
    warped = shaped.transpose(0, 1, 3, 2, 4).reshape(row_count, plane_count, y_count)
    warped_f = warped.astype(jnp.float32)
    residual = reference_image.astype(jnp.float32) - warped_f
    cos_y, sin_y = dft_tables(y_count)
    cos_x, sin_x = dft_tables(full_rows)
    kvec_y = wave_numbers(y_count)
    kvec_x = wave_numbers(full_rows)
    forward_y = jnp.concatenate([cos_y, -sin_y], axis=1)
    inverse_y = jnp.concatenate([cos_y, -sin_y], axis=0)
    forward_x = jnp.concatenate([cos_x, -sin_x], axis=0)
    inverse_x = jnp.concatenate([cos_x, -sin_x], axis=1)
    spec_y = jnp.dot(warped.reshape(-1, y_count), forward_y, preferred_element_type=jnp.float32)
    spec_y = spec_y.astype(jnp.bfloat16).astype(jnp.float32)
    coef_y = jnp.concatenate(
        [-kvec_y * spec_y[:, y_count:], kvec_y * spec_y[:, :y_count]], axis=1
    ).astype(jnp.bfloat16)
    slope_y = (jnp.dot(coef_y, inverse_y, preferred_element_type=jnp.float32) / y_count).reshape(
        row_count, plane_count, y_count
    )
    flat_warp = warped.reshape(1, row_count, cell_count)
    spec_x = jnp.einsum(
        "kx,ixm->ikm",
        forward_x,
        lax.all_to_all(flat_warp, "pencil", split_axis=2, concat_axis=1, tiled=True),
        preferred_element_type=jnp.float32,
    )
    coef_x = jnp.concatenate(
        [
            -kvec_x[None, :, None] * spec_x[:, full_rows:],
            kvec_x[None, :, None] * spec_x[:, :full_rows],
        ],
        axis=1,
    ).astype(jnp.bfloat16)
    slope = (
        jnp.einsum("xk,ikm->ixm", inverse_x, coef_x, preferred_element_type=jnp.float32) / full_rows
    ).astype(jnp.bfloat16)
    slope_x = lax.all_to_all(slope, "pencil", split_axis=1, concat_axis=2, tiled=True)
    slope_x = slope_x.reshape(row_count, plane_count, y_count)
    slope_z = (jnp.roll(warped_f, -1, axis=1) - jnp.roll(warped_f, 1, axis=1)) * 0.5
    force = (jnp.stack([slope_x.astype(jnp.float32), slope_y, slope_z]) * residual[None]).astype(
        jnp.bfloat16
    )
    force_lines = force.reshape(-1, y_count)
    spec_real = jnp.dot(force_lines, cos_y, preferred_element_type=jnp.float32).astype(jnp.bfloat16)
    spec_imag = jnp.dot(force_lines, -sin_y, preferred_element_type=jnp.float32).astype(
        jnp.bfloat16
    )
    spec_f = jnp.stack(
        [spec_real.reshape(3, row_count, cell_count), spec_imag.reshape(3, row_count, cell_count)],
        axis=1,
    )
    planes = lax.all_to_all(spec_f, "pencil", split_axis=3, concat_axis=2, tiled=True)
    local_cols = planes.shape[3]
    column_ids = my_index * local_cols + jnp.arange(local_cols, dtype=jnp.int32)
    kvec_local = signed_waves(column_ids % y_count, y_count)
    spectral_gain = force_gain / (
        full_rows
        * y_count
        * (
            1.0
            + h1_weight
            * (kvec_x[:, None] * kvec_x[:, None] + kvec_local[None, :] * kvec_local[None, :])
        )
    )
    cos_part = jnp.einsum("kx,chxm->chkm", cos_x, planes, preferred_element_type=jnp.float32)
    sin_part = jnp.einsum("kx,chxm->chkm", sin_x, planes, preferred_element_type=jnp.float32)
    real_f = cos_part[:, 0] + sin_part[:, 1]
    imag_f = cos_part[:, 1] - sin_part[:, 0]
    scale_grid = spectral_gain[None]
    scaled = jnp.stack([real_f * scale_grid, imag_f * scale_grid], axis=1).astype(jnp.bfloat16)
    cos_back = jnp.einsum("xk,chkm->chxm", cos_x, scaled, preferred_element_type=jnp.float32)
    sin_back = jnp.einsum("xk,chkm->chxm", sin_x, scaled, preferred_element_type=jnp.float32)
    real_b = cos_back[:, 0] - sin_back[:, 1]
    imag_b = cos_back[:, 1] + sin_back[:, 0]
    mixed = jnp.stack([real_b, imag_b], axis=1).astype(jnp.bfloat16)
    smoothed = lax.all_to_all(mixed, "pencil", split_axis=2, concat_axis=3, tiled=True)
    spatial = jnp.dot(
        smoothed[:, 0].reshape(-1, y_count), cos_y, preferred_element_type=jnp.float32
    )
    spatial = spatial - jnp.dot(
        smoothed[:, 1].reshape(-1, y_count), sin_y, preferred_element_type=jnp.float32
    )
    gradient = velocity + spatial.reshape(3, row_count, plane_count, y_count)
    return (warped, gradient)


def split_pair(values):
    high = values.astype(jnp.bfloat16)
    low = (values - np.asarray(high, np.float64)).astype(jnp.bfloat16)
    return [high, low]


def real_dft(length):
    half = length // 2
    waves = np.concatenate([np.arange(half + 1), np.arange(1, half)])
    angle = 2.0 * np.pi * ((np.arange(length)[:, None] * waves[None, :]) % length) / length
    table = np.where(np.arange(length)[None, :] <= half, np.cos(angle), np.sin(angle))
    factor = np.where((waves == 0) | (waves == half), 1.0, 2.0)
    k = np.where(waves == half, 0, waves) * (2.0 * np.pi / length)
    return table, (table * factor[None, :]).T, k


def derivative(length):
    series = np.arange(length)
    angle = 2.0 * np.pi * ((series[:, None] * series[None, :]) % length) / length
    cos, sin = np.cos(angle), np.sin(angle)
    k = np.where(series < length // 2, series, series - length)
    k = np.where(series == length // 2, 0, k) * (2.0 * np.pi / length)
    return ((sin * k) @ cos - (cos * k) @ sin) / length


@functools.lru_cache(None)
def tables(n, rows, planes, ny):
    nx = n * rows
    m = nx * ZB
    index = np.arange(m)
    line_x = index // (ZB * rows) * rows + index % rows
    line_z = index // rows % ZB
    wide = np.arange(2 * m)
    wide_dev = wide // (2 * ZB * rows)
    wide_half = wide // (ZB * rows) % 2
    wide_z = wide // rows % ZB
    wide_row = wide % rows
    slab = wide_half * m + wide_row * planes + wide_dev * ZB + wide_z
    line = wide_half * m + wide_dev * (ZB * rows) + wide_z * rows + wide_row
    eye = np.eye(2 * m)
    to_message = eye[slab]
    from_message = eye[slab].T
    line_message = eye[line]
    wide_x = wide_dev * rows + wide_row
    first_x = [
        np.where(
            (line_z[:, None] == wide_z[None, :]) & (wide_half == h)[None, :],
            wide_x[None, :],
            8 * nx,
        )
        for h in range(2)
    ]
    second_x = np.where(line_z[:, None] == line_z[None, :], line_x[None, :], 8 * nx)
    same_z = line_z[:, None] == line_z[None, :]
    dx = derivative(nx)[line_x[None, :], line_x[:, None]] * same_z
    dy = derivative(ny)
    plane_last = np.zeros((nx, m))
    plane_first = np.zeros((nx, m))
    plane_last[line_x[line_z == ZB - 1], index[line_z == ZB - 1]] = 1.0
    plane_first[line_x[line_z == 0], index[line_z == 0]] = 1.0
    dz = np.zeros((m, 2 * m))
    for r in range(m):
        x, z = line_x[r], line_z[r]
        for step, sign in ((1, 0.5), (-1, -0.5)):
            if z + step < 0:
                column = m + x
            elif z + step >= ZB:
                column = m + nx + x
            else:
                column = int(np.nonzero((line_x == x) & (line_z == z + step))[0][0])
            dz[r, column] += sign
    fx, bx, kx = real_dft(nx)
    fy, by, ky = real_dft(ny)
    out_z = index // nx
    out_k = index % nx
    forward = fx.T[out_k][:, line_x] * (out_z[:, None] == line_z[None, :])
    backward = bx.T[line_x][:, out_k] * (line_z[:, None] == out_z[None, :])
    gain = force_gain / (
        nx * ny * (1.0 + h1_weight * (kx[out_k][:, None] ** 2 + ky[None, :] ** 2))
    )
    per = ny // SEG
    groups = planes // ZB
    lanes = np.arange(rows * groups * per)
    lane_row = lanes // (groups * per)
    lane_group = lanes // per % groups
    code_mask = (lane_group[None, :] == (index // (ZB * rows))[:, None]) & (
        lane_row[None, :] == (index % rows)[:, None]
    )
    code_spread = np.zeros((4, lanes.size, 128))
    for j in range(4):
        code_spread[j, lanes, j * per + lanes % per] = 1.0
    b16 = lambda t: np.asarray(t, np.float64).astype(jnp.bfloat16)
    f32 = lambda t: np.asarray(t, np.float32)
    return {
        "early": b16(np.concatenate([to_message, code_mask])),
        "spread": b16(code_spread),
        "first": f32(first_x),
        "second": f32(second_x),
        "lines": b16(np.concatenate([line_message, line_message.T, dz])),
        "ends": b16(np.concatenate([plane_last, plane_first])),
        "dx": np.concatenate(split_pair(dx)),
        "dy": np.concatenate(split_pair(dy)),
        "x": b16(np.concatenate([forward, backward])),
        "fy": b16(fy),
        "by": b16(by),
        "gain": f32(gain),
    }, b16(to_message.T)


def dot(a, b):
    return jnp.dot(a, b, preferred_element_type=jnp.float32)


def body(n, names, template_hbm, image_hbm, owner_hbm, offset_hbm, level_hbm, *refs):
    tables_hbm = refs[: len(names)]
    (back_recv,) = refs[len(names) : len(names) + 1]
    refs = refs[len(names) + 1 :]
    template_ref, image_ref, owner_ref, offset_ref, level_ref = refs[:5]
    table = dict(zip(names, refs[5 : 5 + len(names)]))
    (
        code_send,
        code_recv,
        image_send,
        image_recv,
        halo_send,
        halo_recv,
        back_send,
        load_sems,
        code_sems,
        image_sems,
        halo_sems,
        back_sems,
        own_sems,
    ) = refs[5 + len(names) :]
    sources = (template_hbm, image_hbm, owner_hbm, offset_hbm, level_hbm) + tables_hbm
    targets = refs[: 5 + len(names)]
    loads = {
        key: pltpu.make_async_copy(source, target, load_sems.at[at])
        for at, (key, source, target) in enumerate(
            zip(("template", "image", "owner", "offset", "level") + names, sources, targets)
        )
    }
    order = ("template", "early", "owner", "offset", "level", "spread", "image")
    for key in order + tuple(key for key in names if key not in order):
        loads[key].start()

    def loaded(*keys):
        for key in keys:
            loads[key].wait()

    me = lax.axis_index("pencil")
    rows, planes, ny = template_ref.shape
    m = n * rows * ZB
    nx = n * rows
    per = ny // SEG
    half = ny // 2
    after = lax.rem(me + 1, n)
    before = lax.rem(me + n - 1, n)

    barrier = pltpu.get_barrier_semaphore()
    partners = [
        lax.rem(me + off, n) for off in sorted(range(1, n), key=lambda off: abs(off - n // 2))
    ]
    for to in partners:
        pl.semaphore_signal(
            barrier, inc=1, device_id={"pencil": to}, device_id_type=pl.DeviceIdType.MESH
        )

    def scatter(send, recv, sems):
        for to in partners:
            pltpu.make_async_remote_copy(
                src_ref=send.at[to],
                dst_ref=recv.at[me],
                send_sem=sems.at[0],
                recv_sem=sems.at[1],
                device_id={"pencil": to},
                device_id_type=pl.DeviceIdType.MESH,
            ).start()

    def everything(send, recv, sems):
        return pltpu.make_async_remote_copy(
            src_ref=send.at[pl.ds(0, n - 1)],
            dst_ref=recv.at[pl.ds(0, n - 1)],
            send_sem=sems.at[0],
            recv_sem=sems.at[1],
            device_id={"pencil": after},
            device_id_type=pl.DeviceIdType.MESH,
        )

    def collect(send, recv, sems):
        everything(send, recv, sems).wait_recv()

    def drain(send, recv, sems):
        everything(send, recv, sems).wait_send()

    def sort_image(slot, ref):
        value = ref[...].reshape(m, ny)
        stacked = jnp.concatenate([value[:, :half], value[:, half:]], axis=0)
        message = dot(table["early"][: 2 * m], stacked).astype(jnp.bfloat16)
        image_send[slot] = message.reshape(n, 2 * ZB * rows, half)

    loaded("template", "early")
    sort_image(0, template_ref)
    loaded("owner", "offset", "level", "spread")
    shift = (planes // ZB * per).bit_length() - 1
    base = owner_ref[...] * rows + lax.shift_right_logical(
        offset_ref[...], jnp.full(offset_ref.shape, shift, jnp.int32)
    )
    base = base.astype(jnp.float32)
    level = level_ref[...].astype(jnp.float32)
    mask = table["early"][2 * m :].astype(jnp.float32)
    codes = jnp.zeros((m, 128), jnp.float32)
    for j, line in enumerate((base[0:1], base[1:2], level[0:1], level[1:2])):
        codes += dot((mask * line).astype(jnp.bfloat16), table["spread"][j])
    code_send[...] = codes.reshape(n, ZB * rows, 128)
    pl.semaphore_wait(barrier, n - 1)
    scatter(code_send, code_recv, code_sems)
    scatter(image_send.at[0], image_recv.at[0], image_sems.at[0])
    code_recv[me] = code_send[me]
    image_recv[0, me] = image_send[0, me]
    loaded("image")
    sort_image(1, image_ref)
    scatter(image_send.at[1], image_recv.at[1], image_sems.at[1])
    image_recv[1, me] = image_send[1, me]

    collect(code_send, code_recv, code_sems)
    code = code_recv[...].reshape(m, 128)
    t = (code + 0.5) / Q
    weights = (
        -t * (t - 1.0) * (t - 2.0) / 6.0,
        (t + 1.0) * (t - 1.0) * (t - 2.0) / 2.0,
        -(t + 1.0) * t * (t - 2.0) / 2.0,
        (t + 1.0) * t * (t - 1.0) / 6.0,
    )

    def stencil(section, group, place):
        at = section * per + group
        delta = place - code[:, at : at + 1]
        delta = jnp.where(delta < 0.0, delta + nx, delta)
        at = 2 * per + at
        taps = jnp.zeros_like(delta)
        for k in range(4):
            taps = jnp.where(delta == float(k), weights[k][:, at : at + 1], taps)
        high = taps.astype(jnp.bfloat16)
        low = (taps - high.astype(jnp.float32)).astype(jnp.bfloat16)
        return high, low

    loaded("first", "second")
    first = [stencil(0, g, table["first"][g * SEG // half]) for g in range(per)]
    second = [stencil(1, g, table["second"][...]) for g in range(per)]
    collect(image_send.at[0], image_recv.at[0], image_sems.at[0])
    template = image_recv[0].reshape(2 * m, half)
    warped = []
    for g in range(per):
        at = g * SEG % half
        seg = template[:, at : at + SEG]
        high, low = first[g]
        seg = (dot(high, seg) + dot(low, seg)).astype(jnp.bfloat16)
        high, low = second[g]
        warped.append((dot(high, seg) + dot(low, seg)).astype(jnp.bfloat16))
    warped = jnp.concatenate(warped, axis=1)

    loaded("ends", "lines")
    halo_send[...] = dot(table["ends"][...], warped).astype(jnp.bfloat16).reshape(2, nx, ny)
    halos = [
        pltpu.make_async_remote_copy(
            src_ref=halo_send.at[side],
            dst_ref=halo_recv.at[side],
            send_sem=halo_sems.at[0, side],
            recv_sem=halo_sems.at[1, side],
            device_id={"pencil": (after, before)[side]},
            device_id_type=pl.DeviceIdType.MESH,
        )
        for side in range(2)
    ]
    for halo in halos:
        halo.start()

    def own(slot):
        return pltpu.make_async_copy(
            back_send.at[slot, me], back_recv.at[slot, me], own_sems.at[slot]
        )

    def send_back(slot, value):
        stacked = jnp.concatenate([value[:, :half], value[:, half:]], axis=0)
        message = dot(table["lines"][: 2 * m], stacked).astype(jnp.bfloat16)
        back_send[slot] = message.reshape(n, 2 * ZB * rows, half)
        scatter(back_send.at[slot], back_recv.at[slot], back_sems.at[slot])
        own(slot).start()

    send_back(0, warped)
    loaded("dx", "dy", "x", "fy", "by", "gain")
    slope_x = dot(table["dx"][:m], warped) + dot(table["dx"][m:], warped)
    collect(image_send.at[1], image_recv.at[1], image_sems.at[1])
    image = dot(table["lines"][2 * m : 4 * m], image_recv[1].reshape(2 * m, half))
    image = jnp.concatenate([image[:m], image[m:]], axis=1)
    residual = image - warped.astype(jnp.float32)

    def smooth(slot, slope):
        force = (slope * residual).astype(jnp.bfloat16)
        spectrum = dot(force, table["fy"][...]).astype(jnp.bfloat16)
        spectrum = dot(table["x"][:m], spectrum) * table["gain"][...]
        spectrum = dot(table["x"][m:], spectrum.astype(jnp.bfloat16)).astype(jnp.bfloat16)
        send_back(slot, dot(spectrum, table["by"][...]).astype(jnp.bfloat16))

    smooth(1, slope_x)
    smooth(2, dot(warped, table["dy"][:ny]) + dot(warped, table["dy"][ny:]))
    for halo in halos:
        halo.wait_recv()
    near = jnp.concatenate([warped, halo_recv[0], halo_recv[1]], axis=0)
    smooth(3, dot(table["lines"][4 * m :], near))

    drain(code_send, code_recv, code_sems)
    for slot in range(2):
        drain(image_send.at[slot], image_recv.at[slot], image_sems.at[slot])
    for halo in halos:
        halo.wait_send()
    for slot in range(4):
        own(slot).wait()
        collect(back_send.at[slot], back_recv.at[slot], back_sems.at[slot])
        drain(back_send.at[slot], back_recv.at[slot], back_sems.at[slot])


def finish(
    back_hbm,
    velocity_hbm,
    sort_hbm,
    warped_hbm,
    gradient_hbm,
    back_ref,
    velocity_ref,
    sort_ref,
    warped_ref,
    gradient_ref,
    load_sems,
    store_sems,
):
    rows, planes, ny = warped_ref.shape
    m = rows * planes
    sort = pltpu.make_async_copy(sort_hbm, sort_ref, load_sems.at[0])
    backs = [
        pltpu.make_async_copy(back_hbm.at[slot], back_ref.at[slot], load_sems.at[1 + slot])
        for slot in range(4)
    ]
    velocities = [
        pltpu.make_async_copy(velocity_hbm.at[c], velocity_ref.at[c], load_sems.at[5 + c])
        for c in range(3)
    ]
    stores = [pltpu.make_async_copy(warped_ref, warped_hbm, store_sems.at[0])] + [
        pltpu.make_async_copy(gradient_ref.at[c], gradient_hbm.at[c], store_sems.at[1 + c])
        for c in range(3)
    ]
    sort.start()
    for slot in (1, 2, 3, 0):
        backs[slot].start()
        if slot > 0:
            velocities[slot - 1].start()
    sort.wait()
    for slot in (1, 2, 3, 0):
        backs[slot].wait()
        home = dot(sort_ref[...], back_ref[slot].reshape(2 * m, ny // 2))
        home = jnp.concatenate([home[:m], home[m:]], axis=1).reshape(rows, planes, ny)
        if slot == 0:
            warped_ref[...] = home.astype(jnp.bfloat16)
        else:
            velocities[slot - 1].wait()
            gradient_ref[slot - 1] = velocity_ref[slot - 1] + home
        stores[slot].start()
    for store in stores:
        store.wait()


def by_groups(template, reference_image, velocity, dep_owner, dep_offset, dep_weight):
    n = lax.axis_size("pencil")
    rows, planes, ny = template.shape
    m = n * rows * ZB
    held, sort_rows = tables(n, rows, planes, ny)
    names = tuple(held)
    constants = [jnp.asarray(held[name]) for name in names]
    operands = (template, reference_image, dep_owner, dep_offset, dep_weight, *constants)
    b16, f32 = jnp.bfloat16, jnp.float32
    message = (n, 2 * ZB * rows, ny // 2)
    hbm = pl.BlockSpec(memory_space=pltpu.HBM)
    back = pl.pallas_call(
        functools.partial(body, n, names),
        out_shape=jax.ShapeDtypeStruct((4,) + message, b16),
        in_specs=[hbm] * len(operands),
        out_specs=hbm,
        scratch_shapes=[pltpu.VMEM(array.shape, array.dtype) for array in operands]
        + [
            pltpu.VMEM((n, ZB * rows, 128), f32),
            pltpu.VMEM((n, ZB * rows, 128), f32),
            pltpu.VMEM((2,) + message, b16),
            pltpu.VMEM((2,) + message, b16),
            pltpu.VMEM((2, n * rows, ny), b16),
            pltpu.VMEM((2, n * rows, ny), b16),
            pltpu.VMEM((4,) + message, b16),
            pltpu.SemaphoreType.DMA((len(operands),)),
            pltpu.SemaphoreType.DMA((2,)),
            pltpu.SemaphoreType.DMA((2, 2)),
            pltpu.SemaphoreType.DMA((2, 2)),
            pltpu.SemaphoreType.DMA((4, 2)),
            pltpu.SemaphoreType.DMA((4,)),
        ],
        compiler_params=pltpu.CompilerParams(
            collective_id=0, has_side_effects=True, vmem_limit_bytes=60 * 1024 * 1024
        ),
        cost_estimate=pl.CostEstimate(
            flops=24 * m * ny * ny, bytes_accessed=8 * m * ny * 4, transcendentals=0
        ),
    )(*operands)
    return pl.pallas_call(
        finish,
        out_shape=(
            jax.ShapeDtypeStruct(template.shape, b16),
            jax.ShapeDtypeStruct(velocity.shape, f32),
        ),
        in_specs=[hbm, hbm, hbm],
        out_specs=(hbm, hbm),
        scratch_shapes=[
            pltpu.VMEM(back.shape, b16),
            pltpu.VMEM(velocity.shape, f32),
            pltpu.VMEM(sort_rows.shape, b16),
            pltpu.VMEM(template.shape, b16),
            pltpu.VMEM(velocity.shape, f32),
            pltpu.SemaphoreType.DMA((8,)),
            pltpu.SemaphoreType.DMA((4,)),
        ],
        compiler_params=pltpu.CompilerParams(vmem_limit_bytes=60 * 1024 * 1024),
        cost_estimate=pl.CostEstimate(
            flops=16 * m * m * ny, bytes_accessed=4 * m * ny * 8, transcendentals=0
        ),
    )(back, velocity, jnp.asarray(sort_rows))


def local(template, *others):
    n = lax.axis_size("pencil")
    rows, planes, ny = template.shape
    per_row = planes // ZB * (ny // SEG)
    whole = planes == n * ZB and ny % (2 * SEG) == 0 and per_row & (per_row - 1) == 0
    if n > 2 and whole and rows * ZB == 8 and n * rows <= 256:
        return by_groups(template, *others)
    return general(template, *others)


def solution(mesh):
    in_specs = (
        P("pencil", "start", None),
        P("pencil", "start", None),
        P("start", "pencil", None, None),
        P("start", "pencil"),
        P("start", "pencil"),
        P("start", "pencil"),
    )
    out_specs = (P("pencil", "start", None), P("start", "pencil", None, None))
    return jax.shard_map(local, mesh=mesh, in_specs=in_specs, out_specs=out_specs, check_vma=False)
```

```python
import functools
import math

import jax
import jax.numpy as jnp
import numpy as np
from jax import lax
from jax.experimental import pallas as pl
from jax.experimental.pallas import tpu as pltpu
from jax.sharding import PartitionSpec as P

ZB = 2
SEG = 128
Q = 16


h1_weight = 64.0
force_gain = 32.0


def shifted(x, axis, by):
    length = lax.axis_size(axis)
    return lax.ppermute(x, axis, [(i, (i + by) % length) for i in range(length)])


def dft_tables(length):
    series = jnp.arange(length, dtype=jnp.int32)
    product = series[:, None] * series[None, :] % length
    angles = product.astype(jnp.float32) * (2.0 * math.pi / length)
    return (jnp.cos(angles).astype(jnp.bfloat16), jnp.sin(angles).astype(jnp.bfloat16))


def signed_waves(series, length):
    signed = jnp.where(series < length // 2, series, series - length)
    signed = jnp.where(series == length // 2, 0, signed)
    return signed.astype(jnp.float32) * (2.0 * math.pi / length)


def wave_numbers(length):
    return signed_waves(jnp.arange(length, dtype=jnp.int32), length)


def cubic_table(levels):
    fraction = (jnp.arange(levels, dtype=jnp.float32) + 0.5) / levels
    node_left = -fraction * (fraction - 1.0) * (fraction - 2.0) / 6.0
    node_zero = (fraction + 1.0) * (fraction - 1.0) * (fraction - 2.0) / 2.0
    node_one = -(fraction + 1.0) * fraction * (fraction - 2.0) / 2.0
    node_two = (fraction + 1.0) * fraction * (fraction - 1.0) / 6.0
    return jnp.stack([node_left, node_zero, node_one, node_two], axis=1)


def pick_weights(weight_level, weight_table):
    onehot = (
        weight_level[:, None] == jnp.arange(weight_table.shape[0], dtype=jnp.int32)[None, :]
    ).astype(jnp.float32)
    return jnp.dot(onehot, weight_table, precision=lax.Precision.HIGHEST)


def general(template, reference_image, velocity, dep_owner, dep_offset, dep_weight):
    peer_count = lax.axis_size("pencil")
    row_count, plane_count, y_count = template.shape
    full_rows = row_count * peer_count
    z_groups = plane_count // ZB
    y_groups = y_count // SEG
    per_row = z_groups * y_groups
    block_count = row_count * per_row
    cell_count = plane_count * y_count
    weight_table = cubic_table(Q)
    my_index = lax.axis_index("pencil")
    shaped = template.reshape(row_count, z_groups, ZB, y_groups, SEG)
    blocks = shaped.transpose(0, 1, 3, 2, 4).reshape(block_count, ZB * SEG)
    for section_index in range(2):
        pieces = []
        for distance in (2, 1, 0, -1, -2):
            if distance == 0:
                pieces.append(blocks)
            else:
                pieces.append(shifted(blocks, "pencil", distance))
        window = jnp.concatenate(pieces, axis=0)
        relative = (dep_owner[section_index] - my_index + peer_count) % peer_count
        move = jnp.where(relative >= peer_count - 2, relative - peer_count, relative)
        offset = dep_offset[section_index]
        start_row = offset // per_row
        place = offset % per_row
        tap_row = (
            (move[:, None] + 2) * row_count
            + start_row[:, None]
            + jnp.arange(4, dtype=jnp.int32)[None, :]
        )
        taps = window[tap_row * per_row + place[:, None]].astype(jnp.float32)
        weights = pick_weights(dep_weight[section_index], weight_table)
        blocks = jnp.sum(weights[:, :, None] * taps, axis=1).astype(jnp.bfloat16)
    shaped = blocks.reshape(row_count, z_groups, y_groups, ZB, SEG)
    warped = shaped.transpose(0, 1, 3, 2, 4).reshape(row_count, plane_count, y_count)
    warped_f = warped.astype(jnp.float32)
    residual = reference_image.astype(jnp.float32) - warped_f
    cos_y, sin_y = dft_tables(y_count)
    cos_x, sin_x = dft_tables(full_rows)
    kvec_y = wave_numbers(y_count)
    kvec_x = wave_numbers(full_rows)
    forward_y = jnp.concatenate([cos_y, -sin_y], axis=1)
    inverse_y = jnp.concatenate([cos_y, -sin_y], axis=0)
    forward_x = jnp.concatenate([cos_x, -sin_x], axis=0)
    inverse_x = jnp.concatenate([cos_x, -sin_x], axis=1)
    spec_y = jnp.dot(warped.reshape(-1, y_count), forward_y, preferred_element_type=jnp.float32)
    spec_y = spec_y.astype(jnp.bfloat16).astype(jnp.float32)
    coef_y = jnp.concatenate(
        [-kvec_y * spec_y[:, y_count:], kvec_y * spec_y[:, :y_count]], axis=1
    ).astype(jnp.bfloat16)
    slope_y = (jnp.dot(coef_y, inverse_y, preferred_element_type=jnp.float32) / y_count).reshape(
        row_count, plane_count, y_count
    )
    flat_warp = warped.reshape(1, row_count, cell_count)
    spec_x = jnp.einsum(
        "kx,ixm->ikm",
        forward_x,
        lax.all_to_all(flat_warp, "pencil", split_axis=2, concat_axis=1, tiled=True),
        preferred_element_type=jnp.float32,
    )
    coef_x = jnp.concatenate(
        [
            -kvec_x[None, :, None] * spec_x[:, full_rows:],
            kvec_x[None, :, None] * spec_x[:, :full_rows],
        ],
        axis=1,
    ).astype(jnp.bfloat16)
    slope = (
        jnp.einsum("xk,ikm->ixm", inverse_x, coef_x, preferred_element_type=jnp.float32) / full_rows
    ).astype(jnp.bfloat16)
    slope_x = lax.all_to_all(slope, "pencil", split_axis=1, concat_axis=2, tiled=True)
    slope_x = slope_x.reshape(row_count, plane_count, y_count)
    slope_z = (jnp.roll(warped_f, -1, axis=1) - jnp.roll(warped_f, 1, axis=1)) * 0.5
    force = (jnp.stack([slope_x.astype(jnp.float32), slope_y, slope_z]) * residual[None]).astype(
        jnp.bfloat16
    )
    force_lines = force.reshape(-1, y_count)
    spec_real = jnp.dot(force_lines, cos_y, preferred_element_type=jnp.float32).astype(jnp.bfloat16)
    spec_imag = jnp.dot(force_lines, -sin_y, preferred_element_type=jnp.float32).astype(
        jnp.bfloat16
    )
    spec_f = jnp.stack(
        [spec_real.reshape(3, row_count, cell_count), spec_imag.reshape(3, row_count, cell_count)],
        axis=1,
    )
    planes = lax.all_to_all(spec_f, "pencil", split_axis=3, concat_axis=2, tiled=True)
    local_cols = planes.shape[3]
    column_ids = my_index * local_cols + jnp.arange(local_cols, dtype=jnp.int32)
    kvec_local = signed_waves(column_ids % y_count, y_count)
    spectral_gain = force_gain / (
        full_rows
        * y_count
        * (
            1.0
            + h1_weight
            * (kvec_x[:, None] * kvec_x[:, None] + kvec_local[None, :] * kvec_local[None, :])
        )
    )
    cos_part = jnp.einsum("kx,chxm->chkm", cos_x, planes, preferred_element_type=jnp.float32)
    sin_part = jnp.einsum("kx,chxm->chkm", sin_x, planes, preferred_element_type=jnp.float32)
    real_f = cos_part[:, 0] + sin_part[:, 1]
    imag_f = cos_part[:, 1] - sin_part[:, 0]
    scale_grid = spectral_gain[None]
    scaled = jnp.stack([real_f * scale_grid, imag_f * scale_grid], axis=1).astype(jnp.bfloat16)
    cos_back = jnp.einsum("xk,chkm->chxm", cos_x, scaled, preferred_element_type=jnp.float32)
    sin_back = jnp.einsum("xk,chkm->chxm", sin_x, scaled, preferred_element_type=jnp.float32)
    real_b = cos_back[:, 0] - sin_back[:, 1]
    imag_b = cos_back[:, 1] + sin_back[:, 0]
    mixed = jnp.stack([real_b, imag_b], axis=1).astype(jnp.bfloat16)
    smoothed = lax.all_to_all(mixed, "pencil", split_axis=2, concat_axis=3, tiled=True)
    spatial = jnp.dot(
        smoothed[:, 0].reshape(-1, y_count), cos_y, preferred_element_type=jnp.float32
    )
    spatial = spatial - jnp.dot(
        smoothed[:, 1].reshape(-1, y_count), sin_y, preferred_element_type=jnp.float32
    )
    gradient = velocity + spatial.reshape(3, row_count, plane_count, y_count)
    return (warped, gradient)


def split_pair(values):
    high = values.astype(jnp.bfloat16)
    low = (values - np.asarray(high, np.float64)).astype(jnp.bfloat16)
    return [high, low]


def real_dft(length):
    half = length // 2
    waves = np.concatenate([np.arange(half + 1), np.arange(1, half)])
    angle = 2.0 * np.pi * ((np.arange(length)[:, None] * waves[None, :]) % length) / length
    table = np.where(np.arange(length)[None, :] <= half, np.cos(angle), np.sin(angle))
    factor = np.where((waves == 0) | (waves == half), 1.0, 2.0)
    k = np.where(waves == half, 0, waves) * (2.0 * np.pi / length)
    return table, (table * factor[None, :]).T, k


def derivative(length):
    series = np.arange(length)
    angle = 2.0 * np.pi * ((series[:, None] * series[None, :]) % length) / length
    cos, sin = np.cos(angle), np.sin(angle)
    k = np.where(series < length // 2, series, series - length)
    k = np.where(series == length // 2, 0, k) * (2.0 * np.pi / length)
    return ((sin * k) @ cos - (cos * k) @ sin) / length


@functools.lru_cache(None)
def tables(n, rows, planes, ny):
    nx = n * rows
    m = nx * ZB
    index = np.arange(m)
    line_x = index // (ZB * rows) * rows + index % rows
    line_z = index // rows % ZB
    wide = np.arange(2 * m)
    wide_dev = wide // (2 * ZB * rows)
    wide_half = wide // (ZB * rows) % 2
    wide_z = wide // rows % ZB
    wide_row = wide % rows
    slab = wide_half * m + wide_row * planes + wide_dev * ZB + wide_z
    line = wide_half * m + wide_dev * (ZB * rows) + wide_z * rows + wide_row
    eye = np.eye(2 * m)
    to_message = eye[slab]
    from_message = eye[slab].T
    line_message = eye[line]
    wide_x = wide_dev * rows + wide_row
    first_x = [
        np.where(
            (line_z[:, None] == wide_z[None, :]) & (wide_half == h)[None, :],
            wide_x[None, :],
            8 * nx,
        )
        for h in range(2)
    ]
    second_x = np.where(line_z[:, None] == line_z[None, :], line_x[None, :], 8 * nx)
    same_z = line_z[:, None] == line_z[None, :]
    dx = derivative(nx)[line_x[None, :], line_x[:, None]] * same_z
    dy = derivative(ny)
    plane_last = np.zeros((nx, m))
    plane_first = np.zeros((nx, m))
    plane_last[line_x[line_z == ZB - 1], index[line_z == ZB - 1]] = 1.0
    plane_first[line_x[line_z == 0], index[line_z == 0]] = 1.0
    dz = np.zeros((m, 2 * m))
    for r in range(m):
        x, z = line_x[r], line_z[r]
        for step, sign in ((1, 0.5), (-1, -0.5)):
            if z + step < 0:
                column = m + x
            elif z + step >= ZB:
                column = m + nx + x
            else:
                column = int(np.nonzero((line_x == x) & (line_z == z + step))[0][0])
            dz[r, column] += sign
    fx, bx, kx = real_dft(nx)
    fy, by, ky = real_dft(ny)
    out_z = index // nx
    out_k = index % nx
    forward = fx.T[out_k][:, line_x] * (out_z[:, None] == line_z[None, :])
    backward = bx.T[line_x][:, out_k] * (line_z[:, None] == out_z[None, :])
    gain = force_gain / (
        nx * ny * (1.0 + h1_weight * (kx[out_k][:, None] ** 2 + ky[None, :] ** 2))
    )
    per = ny // SEG
    groups = planes // ZB
    lanes = np.arange(rows * groups * per)
    lane_row = lanes // (groups * per)
    lane_group = lanes // per % groups
    code_mask = np.arange(n)[:, None] == lane_group[None, :]
    code_spread = np.zeros((4, lanes.size, 128))
    for j in range(4):
        code_spread[j, lanes, (lane_row * 4 + j) * per + lanes % per] = 1.0
    code_lines = index[:, None] // (ZB * rows) == np.arange(n)[None, :]
    out = np.arange(128)
    code_rows = (out[None, :] // (4 * per)) == (index % rows)[:, None]
    code_fold = (out[:, None] % (4 * per) == out[None, :]) & (out[:, None] < rows * 4 * per)
    b16 = lambda t: np.asarray(t, np.float64).astype(jnp.bfloat16)
    f32 = lambda t: np.asarray(t, np.float32)
    return {
        "early": b16(to_message),
        "mask": f32(code_mask),
        "lay": b16(code_lines),
        "fold": b16(np.concatenate([code_rows, code_fold])),
        "spread": b16(code_spread),
        "first": f32(first_x),
        "second": f32(second_x),
        "lines": b16(np.concatenate([line_message, line_message.T, dz])),
        "ends": b16(np.concatenate([plane_last, plane_first])),
        "dx": np.concatenate(split_pair(dx)),
        "dy": np.concatenate(split_pair(dy)),
        "x": b16(np.concatenate([forward, backward])),
        "fy": b16(fy),
        "by": b16(by),
        "gain": f32(gain),
    }, b16(to_message.T)


def dot(a, b):
    return jnp.dot(a, b, preferred_element_type=jnp.float32)


def body(n, names, template_hbm, image_hbm, owner_hbm, offset_hbm, level_hbm, *refs):
    tables_hbm = refs[: len(names)]
    (back_recv,) = refs[len(names) : len(names) + 1]
    refs = refs[len(names) + 1 :]
    template_ref, image_ref, owner_ref, offset_ref, level_ref = refs[:5]
    table = dict(zip(names, refs[5 : 5 + len(names)]))
    (
        code_send,
        code_recv,
        image_send,
        image_recv,
        halo_send,
        halo_recv,
        back_send,
        load_sems,
        code_sems,
        image_sems,
        halo_sems,
        back_sems,
        own_sems,
    ) = refs[5 + len(names) :]
    sources = (template_hbm, image_hbm, owner_hbm, offset_hbm, level_hbm) + tables_hbm
    targets = refs[: 5 + len(names)]
    loads = {
        key: pltpu.make_async_copy(source, target, load_sems.at[at])
        for at, (key, source, target) in enumerate(
            zip(("template", "image", "owner", "offset", "level") + names, sources, targets)
        )
    }
    order = ("template", "early", "owner", "offset", "level", "spread", "mask", "image", "lay", "fold")
    for key in order + tuple(key for key in names if key not in order):
        loads[key].start()

    def loaded(*keys):
        for key in keys:
            loads[key].wait()

    me = lax.axis_index("pencil")
    rows, planes, ny = template_ref.shape
    m = n * rows * ZB
    nx = n * rows
    per = ny // SEG
    half = ny // 2
    core = lax.axis_index("start")

    def flip(at):
        return at + lax.rem(core, 2) * (1 - 2 * lax.rem(at, 2))

    group = flip(me)
    after = flip(lax.rem(group + 1, n))
    before = flip(lax.rem(group + n - 1, n))

    barrier = pltpu.get_barrier_semaphore()
    partners = [
        lax.rem(me + off, n) for off in sorted(range(1, n), key=lambda off: abs(off - n // 2))
    ]
    for to in partners:
        pl.semaphore_signal(
            barrier, inc=1, device_id={"pencil": to}, device_id_type=pl.DeviceIdType.MESH
        )

    to_groups = [(to, flip(to), me) for to in partners]
    to_homes = [(to, to, group) for to in partners]

    def scatter(send, recv, sems, ways):
        for to, part, place in ways:
            pltpu.make_async_remote_copy(
                src_ref=send.at[part],
                dst_ref=recv.at[place],
                send_sem=sems.at[0],
                recv_sem=sems.at[1],
                device_id={"pencil": to},
                device_id_type=pl.DeviceIdType.MESH,
            ).start()

    def everything(send, recv, sems):
        return pltpu.make_async_remote_copy(
            src_ref=send.at[pl.ds(0, n - 1)],
            dst_ref=recv.at[pl.ds(0, n - 1)],
            send_sem=sems.at[0],
            recv_sem=sems.at[1],
            device_id={"pencil": after},
            device_id_type=pl.DeviceIdType.MESH,
        )

    def collect(send, recv, sems):
        everything(send, recv, sems).wait_recv()

    def drain(send, recv, sems):
        everything(send, recv, sems).wait_send()

    def sort_image(slot, ref):
        value = ref[...].reshape(m, ny)
        stacked = jnp.concatenate([value[:, :half], value[:, half:]], axis=0)
        message = dot(table["early"][...], stacked).astype(jnp.bfloat16)
        image_send[slot] = message.reshape(n, 2 * ZB * rows, half)

    loaded("template", "early")
    sort_image(0, template_ref)
    loaded("owner", "offset", "level", "spread", "mask")
    shift = (planes // ZB * per).bit_length() - 1
    base = owner_ref[...] * rows + lax.shift_right_logical(
        offset_ref[...], jnp.full(offset_ref.shape, shift, jnp.int32)
    )
    base = base.astype(jnp.float32)
    level = level_ref[...].astype(jnp.float32)
    codes = jnp.zeros((n, 128), jnp.float32)
    for j, line in enumerate((base[0:1], base[1:2], level[0:1], level[1:2])):
        codes += dot((table["mask"][...] * line).astype(jnp.bfloat16), table["spread"][j])
    code_send[...] = codes.reshape(n, 1, 128)
    pl.semaphore_wait(barrier, n - 1)
    scatter(code_send, code_recv, code_sems, to_groups)
    scatter(image_send.at[0], image_recv.at[0], image_sems.at[0], to_groups)
    code_recv[me] = code_send[group]
    image_recv[0, me] = image_send[0, group]
    loaded("image")
    sort_image(1, image_ref)
    scatter(image_send.at[1], image_recv.at[1], image_sems.at[1], to_groups)
    image_recv[1, me] = image_send[1, group]

    collect(code_send, code_recv, code_sems)
    loaded("lay", "fold")
    code = dot(table["lay"][...], code_recv[...].reshape(n, 128).astype(jnp.bfloat16))
    code = (code * table["fold"][:m].astype(jnp.float32)).astype(jnp.bfloat16)
    code = dot(code, table["fold"][m:])
    t = (code + 0.5) / Q
    weights = (
        -t * (t - 1.0) * (t - 2.0) / 6.0,
        (t + 1.0) * (t - 1.0) * (t - 2.0) / 2.0,
        -(t + 1.0) * t * (t - 2.0) / 2.0,
        (t + 1.0) * t * (t - 1.0) / 6.0,
    )

    def stencil(section, group, place):
        at = section * per + group
        delta = place - code[:, at : at + 1]
        delta = jnp.where(delta < 0.0, delta + nx, delta)
        at = 2 * per + at
        taps = jnp.zeros_like(delta)
        for k in range(4):
            taps = jnp.where(delta == float(k), weights[k][:, at : at + 1], taps)
        high = taps.astype(jnp.bfloat16)
        low = (taps - high.astype(jnp.float32)).astype(jnp.bfloat16)
        return high, low

    loaded("first", "second")
    first = [stencil(0, g, table["first"][g * SEG // half]) for g in range(per)]
    second = [stencil(1, g, table["second"][...]) for g in range(per)]
    collect(image_send.at[0], image_recv.at[0], image_sems.at[0])
    template = image_recv[0].reshape(2 * m, half)
    warped = []
    for g in range(per):
        at = g * SEG % half
        seg = template[:, at : at + SEG]
        high, low = first[g]
        seg = (dot(high, seg) + dot(low, seg)).astype(jnp.bfloat16)
        high, low = second[g]
        warped.append((dot(high, seg) + dot(low, seg)).astype(jnp.bfloat16))
    warped = jnp.concatenate(warped, axis=1)

    loaded("ends", "lines")
    halo_send[...] = dot(table["ends"][...], warped).astype(jnp.bfloat16).reshape(2, nx, ny)
    halos = [
        pltpu.make_async_remote_copy(
            src_ref=halo_send.at[side],
            dst_ref=halo_recv.at[side],
            send_sem=halo_sems.at[0, side],
            recv_sem=halo_sems.at[1, side],
            device_id={"pencil": (after, before)[side]},
            device_id_type=pl.DeviceIdType.MESH,
        )
        for side in range(2)
    ]
    for halo in halos:
        halo.start()

    def own(slot):
        return pltpu.make_async_copy(
            back_send.at[slot, me], back_recv.at[slot, group], own_sems.at[slot]
        )

    def send_back(slot, value):
        stacked = jnp.concatenate([value[:, :half], value[:, half:]], axis=0)
        message = dot(table["lines"][: 2 * m], stacked).astype(jnp.bfloat16)
        back_send[slot] = message.reshape(n, 2 * ZB * rows, half)
        scatter(back_send.at[slot], back_recv.at[slot], back_sems.at[slot], to_homes)
        own(slot).start()

    send_back(0, warped)
    loaded("dx", "dy", "x", "fy", "by", "gain")
    slope_x = dot(table["dx"][:m], warped) + dot(table["dx"][m:], warped)
    collect(image_send.at[1], image_recv.at[1], image_sems.at[1])
    image = dot(table["lines"][2 * m : 4 * m], image_recv[1].reshape(2 * m, half))
    image = jnp.concatenate([image[:m], image[m:]], axis=1)
    residual = image - warped.astype(jnp.float32)

    def smooth(slot, slope):
        force = (slope * residual).astype(jnp.bfloat16)
        spectrum = dot(force, table["fy"][...]).astype(jnp.bfloat16)
        spectrum = dot(table["x"][:m], spectrum) * table["gain"][...]
        spectrum = dot(table["x"][m:], spectrum.astype(jnp.bfloat16)).astype(jnp.bfloat16)
        send_back(slot, dot(spectrum, table["by"][...]).astype(jnp.bfloat16))

    smooth(1, slope_x)
    smooth(2, dot(warped, table["dy"][:ny]) + dot(warped, table["dy"][ny:]))
    for halo in halos:
        halo.wait_recv()
    near = jnp.concatenate([warped, halo_recv[0], halo_recv[1]], axis=0)
    smooth(3, dot(table["lines"][4 * m :], near))

    drain(code_send, code_recv, code_sems)
    for slot in range(2):
        drain(image_send.at[slot], image_recv.at[slot], image_sems.at[slot])
    for halo in halos:
        halo.wait_send()
    for slot in range(4):
        own(slot).wait()
        collect(back_send.at[slot], back_recv.at[slot], back_sems.at[slot])
        drain(back_send.at[slot], back_recv.at[slot], back_sems.at[slot])


def finish(
    back_hbm,
    velocity_hbm,
    sort_hbm,
    warped_hbm,
    gradient_hbm,
    back_ref,
    velocity_ref,
    sort_ref,
    warped_ref,
    gradient_ref,
    load_sems,
    store_sems,
):
    rows, planes, ny = warped_ref.shape
    m = rows * planes
    sort = pltpu.make_async_copy(sort_hbm, sort_ref, load_sems.at[0])
    backs = [
        pltpu.make_async_copy(back_hbm.at[slot], back_ref.at[slot], load_sems.at[1 + slot])
        for slot in range(4)
    ]
    velocities = [
        pltpu.make_async_copy(velocity_hbm.at[c], velocity_ref.at[c], load_sems.at[5 + c])
        for c in range(3)
    ]
    stores = [pltpu.make_async_copy(warped_ref, warped_hbm, store_sems.at[0])] + [
        pltpu.make_async_copy(gradient_ref.at[c], gradient_hbm.at[c], store_sems.at[1 + c])
        for c in range(3)
    ]
    sort.start()
    for slot in (1, 2, 3, 0):
        backs[slot].start()
        if slot > 0:
            velocities[slot - 1].start()
    sort.wait()
    for slot in (1, 2, 3, 0):
        backs[slot].wait()
        home = dot(sort_ref[...], back_ref[slot].reshape(2 * m, ny // 2))
        home = jnp.concatenate([home[:m], home[m:]], axis=1).reshape(rows, planes, ny)
        if slot == 0:
            warped_ref[...] = home.astype(jnp.bfloat16)
        else:
            velocities[slot - 1].wait()
            gradient_ref[slot - 1] = velocity_ref[slot - 1] + home
        stores[slot].start()
    for store in stores:
        store.wait()


def by_groups(template, reference_image, velocity, dep_owner, dep_offset, dep_weight):
    n = lax.axis_size("pencil")
    rows, planes, ny = template.shape
    m = n * rows * ZB
    held, sort_rows = tables(n, rows, planes, ny)
    names = tuple(held)
    constants = [jnp.asarray(held[name]) for name in names]
    operands = (template, reference_image, dep_owner, dep_offset, dep_weight, *constants)
    b16, f32 = jnp.bfloat16, jnp.float32
    message = (n, 2 * ZB * rows, ny // 2)
    hbm = pl.BlockSpec(memory_space=pltpu.HBM)
    back = pl.pallas_call(
        functools.partial(body, n, names),
        out_shape=jax.ShapeDtypeStruct((4,) + message, b16),
        in_specs=[hbm] * len(operands),
        out_specs=hbm,
        scratch_shapes=[pltpu.VMEM(array.shape, array.dtype) for array in operands]
        + [
            pltpu.VMEM((n, 1, 128), f32),
            pltpu.VMEM((n, 1, 128), f32),
            pltpu.VMEM((2,) + message, b16),
            pltpu.VMEM((2,) + message, b16),
            pltpu.VMEM((2, n * rows, ny), b16),
            pltpu.VMEM((2, n * rows, ny), b16),
            pltpu.VMEM((4,) + message, b16),
            pltpu.SemaphoreType.DMA((len(operands),)),
            pltpu.SemaphoreType.DMA((2,)),
            pltpu.SemaphoreType.DMA((2, 2)),
            pltpu.SemaphoreType.DMA((2, 2)),
            pltpu.SemaphoreType.DMA((4, 2)),
            pltpu.SemaphoreType.DMA((4,)),
        ],
        compiler_params=pltpu.CompilerParams(
            collective_id=0, has_side_effects=True, vmem_limit_bytes=60 * 1024 * 1024
        ),
        cost_estimate=pl.CostEstimate(
            flops=24 * m * ny * ny, bytes_accessed=8 * m * ny * 4, transcendentals=0
        ),
    )(*operands)
    return pl.pallas_call(
        finish,
        out_shape=(
            jax.ShapeDtypeStruct(template.shape, b16),
            jax.ShapeDtypeStruct(velocity.shape, f32),
        ),
        in_specs=[hbm, hbm, hbm],
        out_specs=(hbm, hbm),
        scratch_shapes=[
            pltpu.VMEM(back.shape, b16),
            pltpu.VMEM(velocity.shape, f32),
            pltpu.VMEM(sort_rows.shape, b16),
            pltpu.VMEM(template.shape, b16),
            pltpu.VMEM(velocity.shape, f32),
            pltpu.SemaphoreType.DMA((8,)),
            pltpu.SemaphoreType.DMA((4,)),
        ],
        compiler_params=pltpu.CompilerParams(vmem_limit_bytes=60 * 1024 * 1024),
        cost_estimate=pl.CostEstimate(
            flops=16 * m * m * ny, bytes_accessed=4 * m * ny * 8, transcendentals=0
        ),
    )(back, velocity, jnp.asarray(sort_rows))


def local(template, *others):
    n = lax.axis_size("pencil")
    rows, planes, ny = template.shape
    per_row = planes // ZB * (ny // SEG)
    whole = planes == n * ZB and ny % (2 * SEG) == 0 and per_row & (per_row - 1) == 0
    if n > 2 and n % 2 == 0 and 4 * rows * (ny // SEG) <= 128 and whole and rows * ZB == 8 and n * rows <= 256:
        return by_groups(template, *others)
    return general(template, *others)


def solution(mesh):
    in_specs = (
        P("pencil", "start", None),
        P("pencil", "start", None),
        P("start", "pencil", None, None),
        P("start", "pencil"),
        P("start", "pencil"),
        P("start", "pencil"),
    )
    out_specs = (P("pencil", "start", None), P("start", "pencil", None, None))
    return jax.shard_map(local, mesh=mesh, in_specs=in_specs, out_specs=out_specs, check_vma=False)
```

```python
import functools
import math

import jax
import jax.numpy as jnp
import numpy as np
from jax import lax
from jax.experimental import pallas as pl
from jax.experimental.pallas import tpu as pltpu
from jax.sharding import PartitionSpec as P

ZB = 2
SEG = 128
Q = 16


h1_weight = 64.0
force_gain = 32.0


def shifted(x, axis, by):
    length = lax.axis_size(axis)
    return lax.ppermute(x, axis, [(i, (i + by) % length) for i in range(length)])


def dft_tables(length):
    series = jnp.arange(length, dtype=jnp.int32)
    product = series[:, None] * series[None, :] % length
    angles = product.astype(jnp.float32) * (2.0 * math.pi / length)
    return (jnp.cos(angles).astype(jnp.bfloat16), jnp.sin(angles).astype(jnp.bfloat16))


def signed_waves(series, length):
    signed = jnp.where(series < length // 2, series, series - length)
    signed = jnp.where(series == length // 2, 0, signed)
    return signed.astype(jnp.float32) * (2.0 * math.pi / length)


def wave_numbers(length):
    return signed_waves(jnp.arange(length, dtype=jnp.int32), length)


def cubic_table(levels):
    fraction = (jnp.arange(levels, dtype=jnp.float32) + 0.5) / levels
    node_left = -fraction * (fraction - 1.0) * (fraction - 2.0) / 6.0
    node_zero = (fraction + 1.0) * (fraction - 1.0) * (fraction - 2.0) / 2.0
    node_one = -(fraction + 1.0) * fraction * (fraction - 2.0) / 2.0
    node_two = (fraction + 1.0) * fraction * (fraction - 1.0) / 6.0
    return jnp.stack([node_left, node_zero, node_one, node_two], axis=1)


def pick_weights(weight_level, weight_table):
    onehot = (
        weight_level[:, None] == jnp.arange(weight_table.shape[0], dtype=jnp.int32)[None, :]
    ).astype(jnp.float32)
    return jnp.dot(onehot, weight_table, precision=lax.Precision.HIGHEST)


def general(template, reference_image, velocity, dep_owner, dep_offset, dep_weight):
    peer_count = lax.axis_size("pencil")
    row_count, plane_count, y_count = template.shape
    full_rows = row_count * peer_count
    z_groups = plane_count // ZB
    y_groups = y_count // SEG
    per_row = z_groups * y_groups
    block_count = row_count * per_row
    cell_count = plane_count * y_count
    weight_table = cubic_table(Q)
    my_index = lax.axis_index("pencil")
    shaped = template.reshape(row_count, z_groups, ZB, y_groups, SEG)
    blocks = shaped.transpose(0, 1, 3, 2, 4).reshape(block_count, ZB * SEG)
    for section_index in range(2):
        pieces = []
        for distance in (2, 1, 0, -1, -2):
            if distance == 0:
                pieces.append(blocks)
            else:
                pieces.append(shifted(blocks, "pencil", distance))
        window = jnp.concatenate(pieces, axis=0)
        relative = (dep_owner[section_index] - my_index + peer_count) % peer_count
        move = jnp.where(relative >= peer_count - 2, relative - peer_count, relative)
        offset = dep_offset[section_index]
        start_row = offset // per_row
        place = offset % per_row
        tap_row = (
            (move[:, None] + 2) * row_count
            + start_row[:, None]
            + jnp.arange(4, dtype=jnp.int32)[None, :]
        )
        taps = window[tap_row * per_row + place[:, None]].astype(jnp.float32)
        weights = pick_weights(dep_weight[section_index], weight_table)
        blocks = jnp.sum(weights[:, :, None] * taps, axis=1).astype(jnp.bfloat16)
    shaped = blocks.reshape(row_count, z_groups, y_groups, ZB, SEG)
    warped = shaped.transpose(0, 1, 3, 2, 4).reshape(row_count, plane_count, y_count)
    warped_f = warped.astype(jnp.float32)
    residual = reference_image.astype(jnp.float32) - warped_f
    cos_y, sin_y = dft_tables(y_count)
    cos_x, sin_x = dft_tables(full_rows)
    kvec_y = wave_numbers(y_count)
    kvec_x = wave_numbers(full_rows)
    forward_y = jnp.concatenate([cos_y, -sin_y], axis=1)
    inverse_y = jnp.concatenate([cos_y, -sin_y], axis=0)
    forward_x = jnp.concatenate([cos_x, -sin_x], axis=0)
    inverse_x = jnp.concatenate([cos_x, -sin_x], axis=1)
    spec_y = jnp.dot(warped.reshape(-1, y_count), forward_y, preferred_element_type=jnp.float32)
    spec_y = spec_y.astype(jnp.bfloat16).astype(jnp.float32)
    coef_y = jnp.concatenate(
        [-kvec_y * spec_y[:, y_count:], kvec_y * spec_y[:, :y_count]], axis=1
    ).astype(jnp.bfloat16)
    slope_y = (jnp.dot(coef_y, inverse_y, preferred_element_type=jnp.float32) / y_count).reshape(
        row_count, plane_count, y_count
    )
    flat_warp = warped.reshape(1, row_count, cell_count)
    spec_x = jnp.einsum(
        "kx,ixm->ikm",
        forward_x,
        lax.all_to_all(flat_warp, "pencil", split_axis=2, concat_axis=1, tiled=True),
        preferred_element_type=jnp.float32,
    )
    coef_x = jnp.concatenate(
        [
            -kvec_x[None, :, None] * spec_x[:, full_rows:],
            kvec_x[None, :, None] * spec_x[:, :full_rows],
        ],
        axis=1,
    ).astype(jnp.bfloat16)
    slope = (
        jnp.einsum("xk,ikm->ixm", inverse_x, coef_x, preferred_element_type=jnp.float32) / full_rows
    ).astype(jnp.bfloat16)
    slope_x = lax.all_to_all(slope, "pencil", split_axis=1, concat_axis=2, tiled=True)
    slope_x = slope_x.reshape(row_count, plane_count, y_count)
    slope_z = (jnp.roll(warped_f, -1, axis=1) - jnp.roll(warped_f, 1, axis=1)) * 0.5
    force = (jnp.stack([slope_x.astype(jnp.float32), slope_y, slope_z]) * residual[None]).astype(
        jnp.bfloat16
    )
    force_lines = force.reshape(-1, y_count)
    spec_real = jnp.dot(force_lines, cos_y, preferred_element_type=jnp.float32).astype(jnp.bfloat16)
    spec_imag = jnp.dot(force_lines, -sin_y, preferred_element_type=jnp.float32).astype(
        jnp.bfloat16
    )
    spec_f = jnp.stack(
        [spec_real.reshape(3, row_count, cell_count), spec_imag.reshape(3, row_count, cell_count)],
        axis=1,
    )
    planes = lax.all_to_all(spec_f, "pencil", split_axis=3, concat_axis=2, tiled=True)
    local_cols = planes.shape[3]
    column_ids = my_index * local_cols + jnp.arange(local_cols, dtype=jnp.int32)
    kvec_local = signed_waves(column_ids % y_count, y_count)
    spectral_gain = force_gain / (
        full_rows
        * y_count
        * (
            1.0
            + h1_weight
            * (kvec_x[:, None] * kvec_x[:, None] + kvec_local[None, :] * kvec_local[None, :])
        )
    )
    cos_part = jnp.einsum("kx,chxm->chkm", cos_x, planes, preferred_element_type=jnp.float32)
    sin_part = jnp.einsum("kx,chxm->chkm", sin_x, planes, preferred_element_type=jnp.float32)
    real_f = cos_part[:, 0] + sin_part[:, 1]
    imag_f = cos_part[:, 1] - sin_part[:, 0]
    scale_grid = spectral_gain[None]
    scaled = jnp.stack([real_f * scale_grid, imag_f * scale_grid], axis=1).astype(jnp.bfloat16)
    cos_back = jnp.einsum("xk,chkm->chxm", cos_x, scaled, preferred_element_type=jnp.float32)
    sin_back = jnp.einsum("xk,chkm->chxm", sin_x, scaled, preferred_element_type=jnp.float32)
    real_b = cos_back[:, 0] - sin_back[:, 1]
    imag_b = cos_back[:, 1] + sin_back[:, 0]
    mixed = jnp.stack([real_b, imag_b], axis=1).astype(jnp.bfloat16)
    smoothed = lax.all_to_all(mixed, "pencil", split_axis=2, concat_axis=3, tiled=True)
    spatial = jnp.dot(
        smoothed[:, 0].reshape(-1, y_count), cos_y, preferred_element_type=jnp.float32
    )
    spatial = spatial - jnp.dot(
        smoothed[:, 1].reshape(-1, y_count), sin_y, preferred_element_type=jnp.float32
    )
    gradient = velocity + spatial.reshape(3, row_count, plane_count, y_count)
    return (warped, gradient)


def split_pair(values):
    high = values.astype(jnp.bfloat16)
    low = (values - np.asarray(high, np.float64)).astype(jnp.bfloat16)
    return [high, low]


def real_dft(length):
    half = length // 2
    waves = np.concatenate([np.arange(half + 1), np.arange(1, half)])
    angle = 2.0 * np.pi * ((np.arange(length)[:, None] * waves[None, :]) % length) / length
    table = np.where(np.arange(length)[None, :] <= half, np.cos(angle), np.sin(angle))
    factor = np.where((waves == 0) | (waves == half), 1.0, 2.0)
    k = np.where(waves == half, 0, waves) * (2.0 * np.pi / length)
    return table, (table * factor[None, :]).T, k


def derivative(length):
    series = np.arange(length)
    angle = 2.0 * np.pi * ((series[:, None] * series[None, :]) % length) / length
    cos, sin = np.cos(angle), np.sin(angle)
    k = np.where(series < length // 2, series, series - length)
    k = np.where(series == length // 2, 0, k) * (2.0 * np.pi / length)
    return ((sin * k) @ cos - (cos * k) @ sin) / length


@functools.lru_cache(None)
def tables(n, rows, planes, ny):
    nx = n * rows
    m = nx * ZB
    index = np.arange(m)
    line_x = index // (ZB * rows) * rows + index % rows
    line_z = index // rows % ZB
    wide = np.arange(2 * m)
    wide_dev = wide // (2 * ZB * rows)
    wide_half = wide // (ZB * rows) % 2
    wide_z = wide // rows % ZB
    wide_row = wide % rows
    slab = wide_half * m + wide_row * planes + wide_dev * ZB + wide_z
    eye = np.eye(2 * m)
    to_message = eye[slab]
    from_message = eye[slab].T
    wide_x = wide_dev * rows + wide_row
    first_x = [
        np.where(
            (line_z[:, None] == wide_z[None, :]) & (wide_half == h)[None, :],
            wide_x[None, :],
            8 * nx,
        )
        for h in range(2)
    ]
    second_x = np.where(line_z[:, None] == line_z[None, :], line_x[None, :], 8 * nx)
    same_z = line_z[:, None] == line_z[None, :]
    dx = derivative(nx)[line_x[None, :], line_x[:, None]] * same_z
    dy = derivative(ny)
    plane_last = np.zeros((nx, m))
    plane_first = np.zeros((nx, m))
    plane_last[line_x[line_z == ZB - 1], index[line_z == ZB - 1]] = 1.0
    plane_first[line_x[line_z == 0], index[line_z == 0]] = 1.0
    dz = np.zeros((m, 2 * m))
    for r in range(m):
        x, z = line_x[r], line_z[r]
        for step, sign in ((1, 0.5), (-1, -0.5)):
            if z + step < 0:
                column = m + x
            elif z + step >= ZB:
                column = m + nx + x
            else:
                column = int(np.nonzero((line_x == x) & (line_z == z + step))[0][0])
            dz[r, column] += sign
    fx, bx, kx = real_dft(nx)
    fy, by, ky = real_dft(ny)
    out_z = index // nx
    out_k = index % nx
    forward = fx.T[out_k][:, line_x] * (out_z[:, None] == line_z[None, :])
    backward = bx.T[line_x][:, out_k] * (line_z[:, None] == out_z[None, :])
    gain = force_gain / (
        nx * ny * (1.0 + h1_weight * (kx[out_k][:, None] ** 2 + ky[None, :] ** 2))
    )
    per = ny // SEG
    groups = planes // ZB
    lanes = np.arange(rows * groups * per)
    lane_row = lanes // (groups * per)
    lane_group = lanes // per % groups
    code_mask = np.arange(n)[:, None] == lane_group[None, :]
    code_spread = np.zeros((4, lanes.size, 128))
    for j in range(4):
        code_spread[j, lanes, (lane_row * 4 + j) * per + lanes % per] = 1.0
    code_lines = index[:, None] // (ZB * rows) == np.arange(n)[None, :]
    out = np.arange(128)
    code_rows = (out[None, :] // (4 * per)) == (index % rows)[:, None]
    code_fold = (out[:, None] % (4 * per) == out[None, :]) & (out[:, None] < rows * 4 * per)
    b16 = lambda t: np.asarray(t, np.float64).astype(jnp.bfloat16)
    f32 = lambda t: np.asarray(t, np.float32)
    return {
        "early": b16(to_message),
        "mask": f32(code_mask),
        "lay": b16(code_lines),
        "fold": b16(np.concatenate([code_rows, code_fold])),
        "spread": b16(code_spread),
        "first": f32(first_x),
        "second": f32(second_x),
        "dz": b16(dz),
        "ends": b16(np.concatenate([plane_last, plane_first])),
        "dx": np.concatenate(split_pair(dx)),
        "dy": np.concatenate(split_pair(dy)),
        "x": b16(np.concatenate([forward, backward])),
        "fy": b16(fy),
        "by": b16(by),
        "gain": f32(gain),
    }, b16(to_message.T)


def dot(a, b):
    return jnp.dot(a, b, preferred_element_type=jnp.float32)


def body(n, names, template_hbm, image_hbm, owner_hbm, offset_hbm, level_hbm, *refs):
    tables_hbm = refs[: len(names)]
    (back_recv,) = refs[len(names) : len(names) + 1]
    refs = refs[len(names) + 1 :]
    template_ref, image_ref, owner_ref, offset_ref, level_ref = refs[:5]
    table = dict(zip(names, refs[5 : 5 + len(names)]))
    (
        code_send,
        code_recv,
        image_send,
        image_recv,
        halo_send,
        halo_recv,
        back_send,
        load_sems,
        code_sems,
        image_sems,
        halo_sems,
        back_sems,
        own_sems,
    ) = refs[5 + len(names) :]
    sources = (template_hbm, image_hbm, owner_hbm, offset_hbm, level_hbm) + tables_hbm
    targets = refs[: 5 + len(names)]
    loads = {
        key: pltpu.make_async_copy(source, target, load_sems.at[at])
        for at, (key, source, target) in enumerate(
            zip(("template", "image", "owner", "offset", "level") + names, sources, targets)
        )
    }
    order = ("template", "early", "owner", "offset", "level", "spread", "mask", "image", "lay", "fold")
    for key in order + tuple(key for key in names if key not in order):
        loads[key].start()

    def loaded(*keys):
        for key in keys:
            loads[key].wait()

    me = lax.axis_index("pencil")
    rows, planes, ny = template_ref.shape
    m = n * rows * ZB
    nx = n * rows
    per = ny // SEG
    half = ny // 2
    each = ZB * rows
    core = lax.axis_index("start")

    def flip(at):
        return at + lax.rem(core, 2) * (1 - 2 * lax.rem(at, 2))

    group = flip(me)
    after = flip(lax.rem(group + 1, n))
    before = flip(lax.rem(group + n - 1, n))

    barrier = pltpu.get_barrier_semaphore()
    partners = [
        lax.rem(me + off, n) for off in sorted(range(1, n), key=lambda off: abs(off - n // 2))
    ]
    for to in partners:
        pl.semaphore_signal(
            barrier, inc=1, device_id={"pencil": to}, device_id_type=pl.DeviceIdType.MESH
        )

    to_groups = [(to, flip(to), me) for to in partners]
    to_homes = [(to, to, group) for to in partners]

    def scatter(send, recv, sems, ways):
        for to, part, place in ways:
            pltpu.make_async_remote_copy(
                src_ref=send.at[part],
                dst_ref=recv.at[place],
                send_sem=sems.at[0],
                recv_sem=sems.at[1],
                device_id={"pencil": to},
                device_id_type=pl.DeviceIdType.MESH,
            ).start()

    def everything(send, recv, sems):
        return pltpu.make_async_remote_copy(
            src_ref=send.at[pl.ds(0, n - 1)],
            dst_ref=recv.at[pl.ds(0, n - 1)],
            send_sem=sems.at[0],
            recv_sem=sems.at[1],
            device_id={"pencil": after},
            device_id_type=pl.DeviceIdType.MESH,
        )

    def collect(send, recv, sems):
        everything(send, recv, sems).wait_recv()

    def drain(send, recv, sems):
        everything(send, recv, sems).wait_send()

    def sort_image(slot, ref):
        value = ref[...].reshape(m, ny)
        stacked = jnp.concatenate([value[:, :half], value[:, half:]], axis=0)
        message = dot(table["early"][...], stacked).astype(jnp.bfloat16)
        image_send[slot] = message.reshape(n, 2 * ZB * rows, half)

    loaded("template", "early")
    sort_image(0, template_ref)
    loaded("owner", "offset", "level", "spread", "mask")
    shift = (planes // ZB * per).bit_length() - 1
    base = owner_ref[...] * rows + lax.shift_right_logical(
        offset_ref[...], jnp.full(offset_ref.shape, shift, jnp.int32)
    )
    base = base.astype(jnp.float32)
    level = level_ref[...].astype(jnp.float32)
    codes = jnp.zeros((n, 128), jnp.float32)
    for j, line in enumerate((base[0:1], base[1:2], level[0:1], level[1:2])):
        codes += dot((table["mask"][...] * line).astype(jnp.bfloat16), table["spread"][j])
    code_send[...] = codes.reshape(n, 1, 128)
    pl.semaphore_wait(barrier, n - 1)
    scatter(code_send, code_recv, code_sems, to_groups)
    scatter(image_send.at[0], image_recv.at[0], image_sems.at[0], to_groups)
    code_recv[me] = code_send[group]
    image_recv[0, me] = image_send[0, group]
    loaded("image")
    sort_image(1, image_ref)
    scatter(image_send.at[1], image_recv.at[1], image_sems.at[1], to_groups)
    image_recv[1, me] = image_send[1, group]

    collect(code_send, code_recv, code_sems)
    loaded("lay", "fold")
    code = dot(table["lay"][...], code_recv[...].reshape(n, 128).astype(jnp.bfloat16))
    code = (code * table["fold"][:m].astype(jnp.float32)).astype(jnp.bfloat16)
    code = dot(code, table["fold"][m:])
    t = (code + 0.5) / Q
    weights = (
        -t * (t - 1.0) * (t - 2.0) / 6.0,
        (t + 1.0) * (t - 1.0) * (t - 2.0) / 2.0,
        -(t + 1.0) * t * (t - 2.0) / 2.0,
        (t + 1.0) * t * (t - 1.0) / 6.0,
    )

    def stencil(section, group, place):
        at = section * per + group
        delta = place - code[:, at : at + 1]
        delta = jnp.where(delta < 0.0, delta + nx, delta)
        at = 2 * per + at
        taps = jnp.zeros_like(delta)
        for k in range(4):
            taps = jnp.where(delta == float(k), weights[k][:, at : at + 1], taps)
        return taps.astype(jnp.bfloat16)

    loaded("first", "second")
    first = [stencil(0, g, table["first"][g * SEG // half]) for g in range(per)]
    second = [stencil(1, g, table["second"][...]) for g in range(per)]
    collect(image_send.at[0], image_recv.at[0], image_sems.at[0])
    template = image_recv[0].reshape(2 * m, half)
    warped = []
    for g in range(per):
        at = g * SEG % half
        seg = template[:, at : at + SEG]
        seg = dot(first[g], seg).astype(jnp.bfloat16)
        warped.append(dot(second[g], seg).astype(jnp.bfloat16))
    warped = jnp.concatenate(warped, axis=1)
    warped_f = warped.astype(jnp.float32)

    loaded("ends", "dz")
    halo_send[...] = dot(table["ends"][...], warped).astype(jnp.bfloat16).reshape(2, nx, ny)
    halos = [
        pltpu.make_async_remote_copy(
            src_ref=halo_send.at[side],
            dst_ref=halo_recv.at[side],
            send_sem=halo_sems.at[0, side],
            recv_sem=halo_sems.at[1, side],
            device_id={"pencil": (after, before)[side]},
            device_id_type=pl.DeviceIdType.MESH,
        )
        for side in range(2)
    ]
    for halo in halos:
        halo.start()

    def own(slot):
        return pltpu.make_async_copy(
            back_send.at[slot, me], back_recv.at[slot, group], own_sems.at[slot]
        )

    def send_back(slot, value):
        for h in range(2):
            part = value[:, h * half : (h + 1) * half].reshape(n, each, half)
            back_send[slot, :, h * each : (h + 1) * each, :] = part.astype(jnp.bfloat16)
        scatter(back_send.at[slot], back_recv.at[slot], back_sems.at[slot], to_homes)
        own(slot).start()

    send_back(0, warped_f)
    loaded("dx", "dy", "x", "fy", "by", "gain")
    slope_x = dot(table["dx"][:m], warped) + dot(table["dx"][m:], warped)
    collect(image_send.at[1], image_recv.at[1], image_sems.at[1])
    image = [
        image_recv[1, :, h * each : (h + 1) * each, :].astype(jnp.float32).reshape(m, half)
        for h in range(2)
    ]
    residual = jnp.concatenate(image, axis=1) - warped_f

    def smooth(slot, slope):
        force = (slope * residual).astype(jnp.bfloat16)
        spectrum = dot(force, table["fy"][...]).astype(jnp.bfloat16)
        spectrum = dot(table["x"][:m], spectrum) * table["gain"][...]
        spectrum = dot(table["x"][m:], spectrum.astype(jnp.bfloat16)).astype(jnp.bfloat16)
        send_back(slot, dot(spectrum, table["by"][...]))

    smooth(1, slope_x)
    smooth(2, dot(warped, table["dy"][:ny]) + dot(warped, table["dy"][ny:]))
    for halo in halos:
        halo.wait_recv()
    near = jnp.concatenate([warped, halo_recv[0], halo_recv[1]], axis=0)
    smooth(3, dot(table["dz"][...], near))

    drain(code_send, code_recv, code_sems)
    for slot in range(2):
        drain(image_send.at[slot], image_recv.at[slot], image_sems.at[slot])
    for halo in halos:
        halo.wait_send()
    for slot in range(4):
        own(slot).wait()
        collect(back_send.at[slot], back_recv.at[slot], back_sems.at[slot])
        drain(back_send.at[slot], back_recv.at[slot], back_sems.at[slot])


def finish(
    back_ref,
    velocity_ref,
    sort_ref,
    warped_hbm,
    gradient_hbm,
    warped_ref,
    gradient_ref,
    store_sems,
):
    rows, planes, ny = warped_ref.shape
    m = rows * planes
    stores = [pltpu.make_async_copy(warped_ref, warped_hbm, store_sems.at[0])] + [
        pltpu.make_async_copy(gradient_ref.at[c], gradient_hbm.at[c], store_sems.at[1 + c])
        for c in range(3)
    ]
    for slot in (1, 2, 3, 0):
        home = dot(sort_ref[...], back_ref[slot].reshape(2 * m, ny // 2))
        home = jnp.concatenate([home[:m], home[m:]], axis=1).reshape(rows, planes, ny)
        if slot == 0:
            warped_ref[...] = home.astype(jnp.bfloat16)
        else:
            gradient_ref[slot - 1] = velocity_ref[slot - 1] + home
        stores[slot].start()
    for store in stores:
        store.wait()


def by_groups(template, reference_image, velocity, dep_owner, dep_offset, dep_weight):
    n = lax.axis_size("pencil")
    rows, planes, ny = template.shape
    m = n * rows * ZB
    held, sort_rows = tables(n, rows, planes, ny)
    names = tuple(held)
    constants = [jnp.asarray(held[name]) for name in names]
    operands = (template, reference_image, dep_owner, dep_offset, dep_weight, *constants)
    b16, f32 = jnp.bfloat16, jnp.float32
    message = (n, 2 * ZB * rows, ny // 2)
    hbm = pl.BlockSpec(memory_space=pltpu.HBM)
    back = pl.pallas_call(
        functools.partial(body, n, names),
        out_shape=jax.ShapeDtypeStruct((4,) + message, b16),
        in_specs=[hbm] * len(operands),
        out_specs=hbm,
        scratch_shapes=[pltpu.VMEM(array.shape, array.dtype) for array in operands]
        + [
            pltpu.VMEM((n, 1, 128), f32),
            pltpu.VMEM((n, 1, 128), f32),
            pltpu.VMEM((2,) + message, b16),
            pltpu.VMEM((2,) + message, b16),
            pltpu.VMEM((2, n * rows, ny), b16),
            pltpu.VMEM((2, n * rows, ny), b16),
            pltpu.VMEM((4,) + message, b16),
            pltpu.SemaphoreType.DMA((len(operands),)),
            pltpu.SemaphoreType.DMA((2,)),
            pltpu.SemaphoreType.DMA((2, 2)),
            pltpu.SemaphoreType.DMA((2, 2)),
            pltpu.SemaphoreType.DMA((4, 2)),
            pltpu.SemaphoreType.DMA((4,)),
        ],
        compiler_params=pltpu.CompilerParams(
            collective_id=0, has_side_effects=True, vmem_limit_bytes=60 * 1024 * 1024
        ),
        cost_estimate=pl.CostEstimate(
            flops=24 * m * ny * ny, bytes_accessed=8 * m * ny * 4, transcendentals=0
        ),
    )(*operands)
    return pl.pallas_call(
        finish,
        out_shape=(
            jax.ShapeDtypeStruct(template.shape, b16),
            jax.ShapeDtypeStruct(velocity.shape, f32),
        ),
        in_specs=[pl.BlockSpec(memory_space=pltpu.VMEM)] * 3,
        out_specs=(hbm, hbm),
        scratch_shapes=[
            pltpu.VMEM(template.shape, b16),
            pltpu.VMEM(velocity.shape, f32),
            pltpu.SemaphoreType.DMA((4,)),
        ],
        compiler_params=pltpu.CompilerParams(vmem_limit_bytes=12 * 1024 * 1024),
        cost_estimate=pl.CostEstimate(
            flops=16 * m * m * ny, bytes_accessed=4 * m * ny * 8, transcendentals=0
        ),
    )(back, velocity, jnp.asarray(sort_rows))


def local(template, *others):
    n = lax.axis_size("pencil")
    rows, planes, ny = template.shape
    per_row = planes // ZB * (ny // SEG)
    whole = planes == n * ZB and ny % (2 * SEG) == 0 and per_row & (per_row - 1) == 0
    if n > 2 and n % 2 == 0 and 4 * rows * (ny // SEG) <= 128 and whole and rows * ZB == 8 and n * rows <= 256:
        return by_groups(template, *others)
    return general(template, *others)


def solution(mesh):
    in_specs = (
        P("pencil", "start", None),
        P("pencil", "start", None),
        P("start", "pencil", None, None),
        P("start", "pencil"),
        P("start", "pencil"),
        P("start", "pencil"),
    )
    out_specs = (P("pencil", "start", None), P("start", "pencil", None, None))
    return jax.shard_map(local, mesh=mesh, in_specs=in_specs, out_specs=out_specs, check_vma=False)
```

```python
import functools
import math

import jax
import jax.numpy as jnp
import numpy as np
from jax import lax
from jax.experimental import pallas as pl
from jax.experimental.pallas import tpu as pltpu
from jax.sharding import PartitionSpec as P

ZB = 2
SEG = 128
Q = 16


h1_weight = 64.0
force_gain = 32.0


def shifted(x, axis, by):
    length = lax.axis_size(axis)
    return lax.ppermute(x, axis, [(i, (i + by) % length) for i in range(length)])


def dft_tables(length):
    series = jnp.arange(length, dtype=jnp.int32)
    product = series[:, None] * series[None, :] % length
    angles = product.astype(jnp.float32) * (2.0 * math.pi / length)
    return (jnp.cos(angles).astype(jnp.bfloat16), jnp.sin(angles).astype(jnp.bfloat16))


def signed_waves(series, length):
    signed = jnp.where(series < length // 2, series, series - length)
    signed = jnp.where(series == length // 2, 0, signed)
    return signed.astype(jnp.float32) * (2.0 * math.pi / length)


def wave_numbers(length):
    return signed_waves(jnp.arange(length, dtype=jnp.int32), length)


def cubic_table(levels):
    fraction = (jnp.arange(levels, dtype=jnp.float32) + 0.5) / levels
    node_left = -fraction * (fraction - 1.0) * (fraction - 2.0) / 6.0
    node_zero = (fraction + 1.0) * (fraction - 1.0) * (fraction - 2.0) / 2.0
    node_one = -(fraction + 1.0) * fraction * (fraction - 2.0) / 2.0
    node_two = (fraction + 1.0) * fraction * (fraction - 1.0) / 6.0
    return jnp.stack([node_left, node_zero, node_one, node_two], axis=1)


def pick_weights(weight_level, weight_table):
    onehot = (
        weight_level[:, None] == jnp.arange(weight_table.shape[0], dtype=jnp.int32)[None, :]
    ).astype(jnp.float32)
    return jnp.dot(onehot, weight_table, precision=lax.Precision.HIGHEST)


def general(template, reference_image, velocity, dep_owner, dep_offset, dep_weight):
    peer_count = lax.axis_size("pencil")
    row_count, plane_count, y_count = template.shape
    full_rows = row_count * peer_count
    z_groups = plane_count // ZB
    y_groups = y_count // SEG
    per_row = z_groups * y_groups
    block_count = row_count * per_row
    cell_count = plane_count * y_count
    weight_table = cubic_table(Q)
    my_index = lax.axis_index("pencil")
    shaped = template.reshape(row_count, z_groups, ZB, y_groups, SEG)
    blocks = shaped.transpose(0, 1, 3, 2, 4).reshape(block_count, ZB * SEG)
    for section_index in range(2):
        pieces = []
        for distance in (2, 1, 0, -1, -2):
            if distance == 0:
                pieces.append(blocks)
            else:
                pieces.append(shifted(blocks, "pencil", distance))
        window = jnp.concatenate(pieces, axis=0)
        relative = (dep_owner[section_index] - my_index + peer_count) % peer_count
        move = jnp.where(relative >= peer_count - 2, relative - peer_count, relative)
        offset = dep_offset[section_index]
        start_row = offset // per_row
        place = offset % per_row
        tap_row = (
            (move[:, None] + 2) * row_count
            + start_row[:, None]
            + jnp.arange(4, dtype=jnp.int32)[None, :]
        )
        taps = window[tap_row * per_row + place[:, None]].astype(jnp.float32)
        weights = pick_weights(dep_weight[section_index], weight_table)
        blocks = jnp.sum(weights[:, :, None] * taps, axis=1).astype(jnp.bfloat16)
    shaped = blocks.reshape(row_count, z_groups, y_groups, ZB, SEG)
    warped = shaped.transpose(0, 1, 3, 2, 4).reshape(row_count, plane_count, y_count)
    warped_f = warped.astype(jnp.float32)
    residual = reference_image.astype(jnp.float32) - warped_f
    cos_y, sin_y = dft_tables(y_count)
    cos_x, sin_x = dft_tables(full_rows)
    kvec_y = wave_numbers(y_count)
    kvec_x = wave_numbers(full_rows)
    forward_y = jnp.concatenate([cos_y, -sin_y], axis=1)
    inverse_y = jnp.concatenate([cos_y, -sin_y], axis=0)
    forward_x = jnp.concatenate([cos_x, -sin_x], axis=0)
    inverse_x = jnp.concatenate([cos_x, -sin_x], axis=1)
    spec_y = jnp.dot(warped.reshape(-1, y_count), forward_y, preferred_element_type=jnp.float32)
    spec_y = spec_y.astype(jnp.bfloat16).astype(jnp.float32)
    coef_y = jnp.concatenate(
        [-kvec_y * spec_y[:, y_count:], kvec_y * spec_y[:, :y_count]], axis=1
    ).astype(jnp.bfloat16)
    slope_y = (jnp.dot(coef_y, inverse_y, preferred_element_type=jnp.float32) / y_count).reshape(
        row_count, plane_count, y_count
    )
    flat_warp = warped.reshape(1, row_count, cell_count)
    spec_x = jnp.einsum(
        "kx,ixm->ikm",
        forward_x,
        lax.all_to_all(flat_warp, "pencil", split_axis=2, concat_axis=1, tiled=True),
        preferred_element_type=jnp.float32,
    )
    coef_x = jnp.concatenate(
        [
            -kvec_x[None, :, None] * spec_x[:, full_rows:],
            kvec_x[None, :, None] * spec_x[:, :full_rows],
        ],
        axis=1,
    ).astype(jnp.bfloat16)
    slope = (
        jnp.einsum("xk,ikm->ixm", inverse_x, coef_x, preferred_element_type=jnp.float32) / full_rows
    ).astype(jnp.bfloat16)
    slope_x = lax.all_to_all(slope, "pencil", split_axis=1, concat_axis=2, tiled=True)
    slope_x = slope_x.reshape(row_count, plane_count, y_count)
    slope_z = (jnp.roll(warped_f, -1, axis=1) - jnp.roll(warped_f, 1, axis=1)) * 0.5
    force = (jnp.stack([slope_x.astype(jnp.float32), slope_y, slope_z]) * residual[None]).astype(
        jnp.bfloat16
    )
    force_lines = force.reshape(-1, y_count)
    spec_real = jnp.dot(force_lines, cos_y, preferred_element_type=jnp.float32).astype(jnp.bfloat16)
    spec_imag = jnp.dot(force_lines, -sin_y, preferred_element_type=jnp.float32).astype(
        jnp.bfloat16
    )
    spec_f = jnp.stack(
        [spec_real.reshape(3, row_count, cell_count), spec_imag.reshape(3, row_count, cell_count)],
        axis=1,
    )
    planes = lax.all_to_all(spec_f, "pencil", split_axis=3, concat_axis=2, tiled=True)
    local_cols = planes.shape[3]
    column_ids = my_index * local_cols + jnp.arange(local_cols, dtype=jnp.int32)
    kvec_local = signed_waves(column_ids % y_count, y_count)
    spectral_gain = force_gain / (
        full_rows
        * y_count
        * (
            1.0
            + h1_weight
            * (kvec_x[:, None] * kvec_x[:, None] + kvec_local[None, :] * kvec_local[None, :])
        )
    )
    cos_part = jnp.einsum("kx,chxm->chkm", cos_x, planes, preferred_element_type=jnp.float32)
    sin_part = jnp.einsum("kx,chxm->chkm", sin_x, planes, preferred_element_type=jnp.float32)
    real_f = cos_part[:, 0] + sin_part[:, 1]
    imag_f = cos_part[:, 1] - sin_part[:, 0]
    scale_grid = spectral_gain[None]
    scaled = jnp.stack([real_f * scale_grid, imag_f * scale_grid], axis=1).astype(jnp.bfloat16)
    cos_back = jnp.einsum("xk,chkm->chxm", cos_x, scaled, preferred_element_type=jnp.float32)
    sin_back = jnp.einsum("xk,chkm->chxm", sin_x, scaled, preferred_element_type=jnp.float32)
    real_b = cos_back[:, 0] - sin_back[:, 1]
    imag_b = cos_back[:, 1] + sin_back[:, 0]
    mixed = jnp.stack([real_b, imag_b], axis=1).astype(jnp.bfloat16)
    smoothed = lax.all_to_all(mixed, "pencil", split_axis=2, concat_axis=3, tiled=True)
    spatial = jnp.dot(
        smoothed[:, 0].reshape(-1, y_count), cos_y, preferred_element_type=jnp.float32
    )
    spatial = spatial - jnp.dot(
        smoothed[:, 1].reshape(-1, y_count), sin_y, preferred_element_type=jnp.float32
    )
    gradient = velocity + spatial.reshape(3, row_count, plane_count, y_count)
    return (warped, gradient)


def split_pair(values):
    high = values.astype(jnp.bfloat16)
    low = (values - np.asarray(high, np.float64)).astype(jnp.bfloat16)
    return [high, low]


def real_dft(length):
    half = length // 2
    waves = np.concatenate([np.arange(half + 1), np.arange(1, half)])
    angle = 2.0 * np.pi * ((np.arange(length)[:, None] * waves[None, :]) % length) / length
    table = np.where(np.arange(length)[None, :] <= half, np.cos(angle), np.sin(angle))
    factor = np.where((waves == 0) | (waves == half), 1.0, 2.0)
    k = np.where(waves == half, 0, waves) * (2.0 * np.pi / length)
    return table, (table * factor[None, :]).T, k


def derivative(length):
    series = np.arange(length)
    angle = 2.0 * np.pi * ((series[:, None] * series[None, :]) % length) / length
    cos, sin = np.cos(angle), np.sin(angle)
    k = np.where(series < length // 2, series, series - length)
    k = np.where(series == length // 2, 0, k) * (2.0 * np.pi / length)
    return ((sin * k) @ cos - (cos * k) @ sin) / length


@functools.lru_cache(None)
def tables(n, rows, planes, ny):
    nx = n * rows
    m = nx * ZB
    index = np.arange(m)
    line_x = index // (ZB * rows) * rows + index % rows
    line_z = index // rows % ZB
    wide = np.arange(2 * m)
    wide_dev = wide // (2 * ZB * rows)
    wide_half = wide // (ZB * rows) % 2
    wide_z = wide // rows % ZB
    wide_row = wide % rows
    slab = wide_half * m + wide_row * planes + wide_dev * ZB + wide_z
    eye = np.eye(2 * m)
    to_message = eye[slab]
    from_message = eye[slab].T
    wide_x = wide_dev * rows + wide_row
    first_x = [
        np.where(
            (line_z[:, None] == wide_z[None, :]) & (wide_half == h)[None, :],
            wide_x[None, :],
            8 * nx,
        )
        for h in range(2)
    ]
    second_x = np.where(line_z[:, None] == line_z[None, :], line_x[None, :], 8 * nx)
    same_z = line_z[:, None] == line_z[None, :]
    dx = derivative(nx)[line_x[None, :], line_x[:, None]] * same_z
    dy = derivative(ny)
    plane_last = np.zeros((nx, m))
    plane_first = np.zeros((nx, m))
    plane_last[line_x[line_z == ZB - 1], index[line_z == ZB - 1]] = 1.0
    plane_first[line_x[line_z == 0], index[line_z == 0]] = 1.0
    dz = np.zeros((m, 2 * m))
    for r in range(m):
        x, z = line_x[r], line_z[r]
        for step, sign in ((1, 0.5), (-1, -0.5)):
            if z + step < 0:
                column = m + x
            elif z + step >= ZB:
                column = m + nx + x
            else:
                column = int(np.nonzero((line_x == x) & (line_z == z + step))[0][0])
            dz[r, column] += sign
    fx, bx, kx = real_dft(nx)
    fy, by, ky = real_dft(ny)
    out_z = index // nx
    out_k = index % nx
    forward = fx.T[out_k][:, line_x] * (out_z[:, None] == line_z[None, :])
    backward = bx.T[line_x][:, out_k] * (line_z[:, None] == out_z[None, :])
    gain = force_gain / (
        nx * ny * (1.0 + h1_weight * (kx[out_k][:, None] ** 2 + ky[None, :] ** 2))
    )
    per = ny // SEG
    groups = planes // ZB
    lanes = np.arange(rows * groups * per)
    lane_row = lanes // (groups * per)
    lane_group = lanes // per % groups
    code_mask = np.arange(n)[:, None] == lane_group[None, :]
    code_spread = np.zeros((4, lanes.size, 128))
    for j in range(4):
        code_spread[j, lanes, (lane_row * 4 + j) * per + lanes % per] = 1.0
    code_lines = index[:, None] // (ZB * rows) == np.arange(n)[None, :]
    out = np.arange(128)
    code_rows = (out[None, :] // (4 * per)) == (index % rows)[:, None]
    code_fold = (out[:, None] % (4 * per) == out[None, :]) & (out[:, None] < rows * 4 * per)
    b16 = lambda t: np.asarray(t, np.float64).astype(jnp.bfloat16)
    f32 = lambda t: np.asarray(t, np.float32)
    return {
        "early": b16(to_message),
        "mask": f32(code_mask),
        "lay": b16(code_lines),
        "fold": b16(np.concatenate([code_rows, code_fold])),
        "spread": b16(code_spread),
        "first": f32(first_x),
        "second": f32(second_x),
        "dz": b16(dz),
        "ends": b16(np.concatenate([plane_last, plane_first])),
        "dx": np.concatenate(split_pair(dx)),
        "dy": np.concatenate(split_pair(dy)),
        "x": b16(np.concatenate([forward, backward])),
        "fy": b16(fy),
        "by": b16(by),
        "gain": f32(gain),
    }, b16(to_message.T)


def dot(a, b):
    return jnp.dot(a, b, preferred_element_type=jnp.float32)


def body(n, names, template_hbm, image_hbm, owner_hbm, offset_hbm, level_hbm, *refs):
    tables_hbm = refs[: len(names)]
    (back_recv,) = refs[len(names) : len(names) + 1]
    refs = refs[len(names) + 1 :]
    template_ref, image_ref, owner_ref, offset_ref, level_ref = refs[:5]
    table = dict(zip(names, refs[5 : 5 + len(names)]))
    (
        code_send,
        code_recv,
        image_send,
        image_recv,
        halo_send,
        halo_recv,
        back_send,
        load_sems,
        code_sems,
        image_sems,
        halo_sems,
        back_sems,
        own_sems,
    ) = refs[5 + len(names) :]
    sources = (template_hbm, image_hbm, owner_hbm, offset_hbm, level_hbm) + tables_hbm
    targets = refs[: 5 + len(names)]
    loads = {
        key: pltpu.make_async_copy(source, target, load_sems.at[at])
        for at, (key, source, target) in enumerate(
            zip(("template", "image", "owner", "offset", "level") + names, sources, targets)
        )
    }
    order = ("owner", "offset", "level", "mask", "spread", "template", "early")
    for key in order:
        loads[key].start()

    def loaded(*keys):
        for key in keys:
            loads[key].wait()

    me = lax.axis_index("pencil")
    rows, planes, ny = template_ref.shape
    m = n * rows * ZB
    nx = n * rows
    per = ny // SEG
    half = ny // 2
    each = ZB * rows
    core = lax.axis_index("start")

    def flip(at):
        return at + lax.rem(core, 2) * (1 - 2 * lax.rem(at, 2))

    group = flip(me)
    after = flip(lax.rem(group + 1, n))
    before = flip(lax.rem(group + n - 1, n))

    barrier = pltpu.get_barrier_semaphore()
    partners = [
        lax.rem(me + off, n) for off in sorted(range(1, n), key=lambda off: abs(off - n // 2))
    ]
    for to in partners:
        pl.semaphore_signal(
            barrier, inc=1, device_id={"pencil": to}, device_id_type=pl.DeviceIdType.MESH
        )
    order += ("image", "lay", "fold", "first", "second")
    for key in order[7:] + tuple(key for key in names if key not in order):
        loads[key].start()

    to_groups = [(to, flip(to), me) for to in partners]
    to_homes = [(to, to, group) for to in partners]

    def scatter(send, recv, sems, ways):
        for to, part, place in ways:
            pltpu.make_async_remote_copy(
                src_ref=send.at[part],
                dst_ref=recv.at[place],
                send_sem=sems.at[0],
                recv_sem=sems.at[1],
                device_id={"pencil": to},
                device_id_type=pl.DeviceIdType.MESH,
            ).start()

    def everything(send, recv, sems):
        return pltpu.make_async_remote_copy(
            src_ref=send.at[pl.ds(0, n - 1)],
            dst_ref=recv.at[pl.ds(0, n - 1)],
            send_sem=sems.at[0],
            recv_sem=sems.at[1],
            device_id={"pencil": after},
            device_id_type=pl.DeviceIdType.MESH,
        )

    def collect(send, recv, sems):
        everything(send, recv, sems).wait_recv()

    def drain(send, recv, sems):
        everything(send, recv, sems).wait_send()

    def sort_image(slot, ref):
        value = ref[...].reshape(m, ny)
        stacked = jnp.concatenate([value[:, :half], value[:, half:]], axis=0)
        message = dot(table["early"][...], stacked).astype(jnp.bfloat16)
        image_send[slot] = message.reshape(n, 2 * ZB * rows, half)

    loaded("owner", "offset", "level", "spread", "mask")
    shift = (planes // ZB * per).bit_length() - 1
    base = owner_ref[...] * rows + lax.shift_right_logical(
        offset_ref[...], jnp.full(offset_ref.shape, shift, jnp.int32)
    )
    base = base.astype(jnp.float32)
    level = level_ref[...].astype(jnp.float32)
    codes = jnp.zeros((n, 128), jnp.float32)
    for j, line in enumerate((base[0:1], base[1:2], level[0:1], level[1:2])):
        codes += dot((table["mask"][...] * line).astype(jnp.bfloat16), table["spread"][j])
    code_send[...] = codes.reshape(n, 1, 128)
    pl.semaphore_wait(barrier, n - 1)
    scatter(code_send, code_recv, code_sems, to_groups)
    loaded("template", "early")
    sort_image(0, template_ref)
    scatter(image_send.at[0], image_recv.at[0], image_sems.at[0], to_groups)
    code_recv[me] = code_send[group]
    image_recv[0, me] = image_send[0, group]
    loaded("image")
    sort_image(1, image_ref)
    scatter(image_send.at[1], image_recv.at[1], image_sems.at[1], to_groups)
    image_recv[1, me] = image_send[1, group]

    collect(code_send, code_recv, code_sems)
    loaded("lay", "fold")
    code = dot(table["lay"][...], code_recv[...].reshape(n, 128).astype(jnp.bfloat16))
    code = (code * table["fold"][:m].astype(jnp.float32)).astype(jnp.bfloat16)
    code = dot(code, table["fold"][m:])
    t = (code + 0.5) / Q
    weights = (
        -t * (t - 1.0) * (t - 2.0) / 6.0,
        (t + 1.0) * (t - 1.0) * (t - 2.0) / 2.0,
        -(t + 1.0) * t * (t - 2.0) / 2.0,
        (t + 1.0) * t * (t - 1.0) / 6.0,
    )

    def stencil(section, group, place):
        at = section * per + group
        delta = place - code[:, at : at + 1]
        delta = jnp.where(delta < 0.0, delta + nx, delta)
        at = 2 * per + at
        taps = jnp.zeros_like(delta)
        for k in range(4):
            taps = jnp.where(delta == float(k), weights[k][:, at : at + 1], taps)
        return taps.astype(jnp.bfloat16)

    loaded("first", "second")
    first = [stencil(0, g, table["first"][g * SEG // half]) for g in range(per)]
    second = [stencil(1, g, table["second"][...]) for g in range(per)]
    collect(image_send.at[0], image_recv.at[0], image_sems.at[0])
    template = image_recv[0].reshape(2 * m, half)
    warped = []
    for g in range(per):
        at = g * SEG % half
        seg = template[:, at : at + SEG]
        seg = dot(first[g], seg).astype(jnp.bfloat16)
        warped.append(dot(second[g], seg).astype(jnp.bfloat16))
    warped = jnp.concatenate(warped, axis=1)
    warped_f = warped.astype(jnp.float32)

    loaded("ends", "dz")
    halo_send[...] = dot(table["ends"][...], warped).astype(jnp.bfloat16).reshape(2, nx, ny)
    halos = [
        pltpu.make_async_remote_copy(
            src_ref=halo_send.at[side],
            dst_ref=halo_recv.at[side],
            send_sem=halo_sems.at[0, side],
            recv_sem=halo_sems.at[1, side],
            device_id={"pencil": (after, before)[side]},
            device_id_type=pl.DeviceIdType.MESH,
        )
        for side in range(2)
    ]
    for halo in halos:
        halo.start()

    def own(slot):
        return pltpu.make_async_copy(
            back_send.at[slot, me], back_recv.at[slot, group], own_sems.at[slot]
        )

    def send_back(slot, value):
        for h in range(2):
            part = value[:, h * half : (h + 1) * half].reshape(n, each, half)
            back_send[slot, :, h * each : (h + 1) * each, :] = part.astype(jnp.bfloat16)
        scatter(back_send.at[slot], back_recv.at[slot], back_sems.at[slot], to_homes)
        own(slot).start()

    send_back(0, warped_f)
    loaded("dx", "dy", "x", "fy", "by", "gain")
    slope_x = dot(table["dx"][:m], warped) + dot(table["dx"][m:], warped)
    collect(image_send.at[1], image_recv.at[1], image_sems.at[1])
    image = [
        image_recv[1, :, h * each : (h + 1) * each, :].astype(jnp.float32).reshape(m, half)
        for h in range(2)
    ]
    residual = jnp.concatenate(image, axis=1) - warped_f

    def smooth(slot, slope):
        force = (slope * residual).astype(jnp.bfloat16)
        spectrum = dot(force, table["fy"][...]).astype(jnp.bfloat16)
        spectrum = dot(table["x"][:m], spectrum) * table["gain"][...]
        spectrum = dot(table["x"][m:], spectrum.astype(jnp.bfloat16)).astype(jnp.bfloat16)
        send_back(slot, dot(spectrum, table["by"][...]))

    smooth(1, slope_x)
    smooth(2, dot(warped, table["dy"][:ny]) + dot(warped, table["dy"][ny:]))
    for halo in halos:
        halo.wait_recv()
    near = jnp.concatenate([warped, halo_recv[0], halo_recv[1]], axis=0)
    smooth(3, dot(table["dz"][...], near))

    drain(code_send, code_recv, code_sems)
    for slot in range(2):
        drain(image_send.at[slot], image_recv.at[slot], image_sems.at[slot])
    for halo in halos:
        halo.wait_send()
    for slot in range(4):
        own(slot).wait()
        collect(back_send.at[slot], back_recv.at[slot], back_sems.at[slot])
        drain(back_send.at[slot], back_recv.at[slot], back_sems.at[slot])


def finish(
    back_ref,
    velocity_ref,
    sort_ref,
    warped_hbm,
    gradient_hbm,
    warped_ref,
    gradient_ref,
    store_sems,
):
    rows, planes, ny = warped_ref.shape
    m = rows * planes
    stores = [pltpu.make_async_copy(warped_ref, warped_hbm, store_sems.at[0])] + [
        pltpu.make_async_copy(gradient_ref.at[c], gradient_hbm.at[c], store_sems.at[1 + c])
        for c in range(3)
    ]
    for slot in (1, 2, 3, 0):
        home = dot(sort_ref[...], back_ref[slot].reshape(2 * m, ny // 2))
        home = jnp.concatenate([home[:m], home[m:]], axis=1).reshape(rows, planes, ny)
        if slot == 0:
            warped_ref[...] = home.astype(jnp.bfloat16)
        else:
            gradient_ref[slot - 1] = velocity_ref[slot - 1] + home
        stores[slot].start()
    for store in stores:
        store.wait()


def by_groups(template, reference_image, velocity, dep_owner, dep_offset, dep_weight):
    n = lax.axis_size("pencil")
    rows, planes, ny = template.shape
    m = n * rows * ZB
    held, sort_rows = tables(n, rows, planes, ny)
    names = tuple(held)
    constants = [jnp.asarray(held[name]) for name in names]
    operands = (template, reference_image, dep_owner, dep_offset, dep_weight, *constants)
    b16, f32 = jnp.bfloat16, jnp.float32
    message = (n, 2 * ZB * rows, ny // 2)
    hbm = pl.BlockSpec(memory_space=pltpu.HBM)
    back = pl.pallas_call(
        functools.partial(body, n, names),
        out_shape=jax.ShapeDtypeStruct((4,) + message, b16),
        in_specs=[hbm] * len(operands),
        out_specs=hbm,
        scratch_shapes=[pltpu.VMEM(array.shape, array.dtype) for array in operands]
        + [
            pltpu.VMEM((n, 1, 128), f32),
            pltpu.VMEM((n, 1, 128), f32),
            pltpu.VMEM((2,) + message, b16),
            pltpu.VMEM((2,) + message, b16),
            pltpu.VMEM((2, n * rows, ny), b16),
            pltpu.VMEM((2, n * rows, ny), b16),
            pltpu.VMEM((4,) + message, b16),
            pltpu.SemaphoreType.DMA((len(operands),)),
            pltpu.SemaphoreType.DMA((2,)),
            pltpu.SemaphoreType.DMA((2, 2)),
            pltpu.SemaphoreType.DMA((2, 2)),
            pltpu.SemaphoreType.DMA((4, 2)),
            pltpu.SemaphoreType.DMA((4,)),
        ],
        compiler_params=pltpu.CompilerParams(
            collective_id=0, has_side_effects=True, vmem_limit_bytes=60 * 1024 * 1024
        ),
        cost_estimate=pl.CostEstimate(
            flops=24 * m * ny * ny, bytes_accessed=8 * m * ny * 4, transcendentals=0
        ),
    )(*operands)
    return pl.pallas_call(
        finish,
        out_shape=(
            jax.ShapeDtypeStruct(template.shape, b16),
            jax.ShapeDtypeStruct(velocity.shape, f32),
        ),
        in_specs=[pl.BlockSpec(memory_space=pltpu.VMEM)] * 3,
        out_specs=(hbm, hbm),
        scratch_shapes=[
            pltpu.VMEM(template.shape, b16),
            pltpu.VMEM(velocity.shape, f32),
            pltpu.SemaphoreType.DMA((4,)),
        ],
        compiler_params=pltpu.CompilerParams(vmem_limit_bytes=12 * 1024 * 1024),
        cost_estimate=pl.CostEstimate(
            flops=16 * m * m * ny, bytes_accessed=4 * m * ny * 8, transcendentals=0
        ),
    )(back, velocity, jnp.asarray(sort_rows))


def local(template, *others):
    n = lax.axis_size("pencil")
    rows, planes, ny = template.shape
    per_row = planes // ZB * (ny // SEG)
    whole = planes == n * ZB and ny % (2 * SEG) == 0 and per_row & (per_row - 1) == 0
    if n > 2 and n % 2 == 0 and 4 * rows * (ny // SEG) <= 128 and whole and rows * ZB == 8 and n * rows <= 256:
        return by_groups(template, *others)
    return general(template, *others)


def solution(mesh):
    in_specs = (
        P("pencil", "start", None),
        P("pencil", "start", None),
        P("start", "pencil", None, None),
        P("start", "pencil"),
        P("start", "pencil"),
        P("start", "pencil"),
    )
    out_specs = (P("pencil", "start", None), P("start", "pencil", None, None))
    return jax.shard_map(local, mesh=mesh, in_specs=in_specs, out_specs=out_specs, check_vma=False)
```

```python
import functools
import math

import jax
import jax.numpy as jnp
import numpy as np
from jax import lax
from jax.experimental import pallas as pl
from jax.experimental.pallas import tpu as pltpu
from jax.sharding import PartitionSpec as P

ZB = 2
SEG = 128
Q = 16


h1_weight = 64.0
force_gain = 32.0


def shifted(x, axis, by):
    length = lax.axis_size(axis)
    return lax.ppermute(x, axis, [(i, (i + by) % length) for i in range(length)])


def dft_tables(length):
    series = jnp.arange(length, dtype=jnp.int32)
    product = series[:, None] * series[None, :] % length
    angles = product.astype(jnp.float32) * (2.0 * math.pi / length)
    return (jnp.cos(angles).astype(jnp.bfloat16), jnp.sin(angles).astype(jnp.bfloat16))


def signed_waves(series, length):
    signed = jnp.where(series < length // 2, series, series - length)
    signed = jnp.where(series == length // 2, 0, signed)
    return signed.astype(jnp.float32) * (2.0 * math.pi / length)


def wave_numbers(length):
    return signed_waves(jnp.arange(length, dtype=jnp.int32), length)


def cubic_table(levels):
    fraction = (jnp.arange(levels, dtype=jnp.float32) + 0.5) / levels
    node_left = -fraction * (fraction - 1.0) * (fraction - 2.0) / 6.0
    node_zero = (fraction + 1.0) * (fraction - 1.0) * (fraction - 2.0) / 2.0
    node_one = -(fraction + 1.0) * fraction * (fraction - 2.0) / 2.0
    node_two = (fraction + 1.0) * fraction * (fraction - 1.0) / 6.0
    return jnp.stack([node_left, node_zero, node_one, node_two], axis=1)


def pick_weights(weight_level, weight_table):
    onehot = (
        weight_level[:, None] == jnp.arange(weight_table.shape[0], dtype=jnp.int32)[None, :]
    ).astype(jnp.float32)
    return jnp.dot(onehot, weight_table, precision=lax.Precision.HIGHEST)


def general(template, reference_image, velocity, dep_owner, dep_offset, dep_weight):
    peer_count = lax.axis_size("pencil")
    row_count, plane_count, y_count = template.shape
    full_rows = row_count * peer_count
    z_groups = plane_count // ZB
    y_groups = y_count // SEG
    per_row = z_groups * y_groups
    block_count = row_count * per_row
    cell_count = plane_count * y_count
    weight_table = cubic_table(Q)
    my_index = lax.axis_index("pencil")
    shaped = template.reshape(row_count, z_groups, ZB, y_groups, SEG)
    blocks = shaped.transpose(0, 1, 3, 2, 4).reshape(block_count, ZB * SEG)
    for section_index in range(2):
        pieces = []
        for distance in (2, 1, 0, -1, -2):
            if distance == 0:
                pieces.append(blocks)
            else:
                pieces.append(shifted(blocks, "pencil", distance))
        window = jnp.concatenate(pieces, axis=0)
        relative = (dep_owner[section_index] - my_index + peer_count) % peer_count
        move = jnp.where(relative >= peer_count - 2, relative - peer_count, relative)
        offset = dep_offset[section_index]
        start_row = offset // per_row
        place = offset % per_row
        tap_row = (
            (move[:, None] + 2) * row_count
            + start_row[:, None]
            + jnp.arange(4, dtype=jnp.int32)[None, :]
        )
        taps = window[tap_row * per_row + place[:, None]].astype(jnp.float32)
        weights = pick_weights(dep_weight[section_index], weight_table)
        blocks = jnp.sum(weights[:, :, None] * taps, axis=1).astype(jnp.bfloat16)
    shaped = blocks.reshape(row_count, z_groups, y_groups, ZB, SEG)
    warped = shaped.transpose(0, 1, 3, 2, 4).reshape(row_count, plane_count, y_count)
    warped_f = warped.astype(jnp.float32)
    residual = reference_image.astype(jnp.float32) - warped_f
    cos_y, sin_y = dft_tables(y_count)
    cos_x, sin_x = dft_tables(full_rows)
    kvec_y = wave_numbers(y_count)
    kvec_x = wave_numbers(full_rows)
    forward_y = jnp.concatenate([cos_y, -sin_y], axis=1)
    inverse_y = jnp.concatenate([cos_y, -sin_y], axis=0)
    forward_x = jnp.concatenate([cos_x, -sin_x], axis=0)
    inverse_x = jnp.concatenate([cos_x, -sin_x], axis=1)
    spec_y = jnp.dot(warped.reshape(-1, y_count), forward_y, preferred_element_type=jnp.float32)
    spec_y = spec_y.astype(jnp.bfloat16).astype(jnp.float32)
    coef_y = jnp.concatenate(
        [-kvec_y * spec_y[:, y_count:], kvec_y * spec_y[:, :y_count]], axis=1
    ).astype(jnp.bfloat16)
    slope_y = (jnp.dot(coef_y, inverse_y, preferred_element_type=jnp.float32) / y_count).reshape(
        row_count, plane_count, y_count
    )
    flat_warp = warped.reshape(1, row_count, cell_count)
    spec_x = jnp.einsum(
        "kx,ixm->ikm",
        forward_x,
        lax.all_to_all(flat_warp, "pencil", split_axis=2, concat_axis=1, tiled=True),
        preferred_element_type=jnp.float32,
    )
    coef_x = jnp.concatenate(
        [
            -kvec_x[None, :, None] * spec_x[:, full_rows:],
            kvec_x[None, :, None] * spec_x[:, :full_rows],
        ],
        axis=1,
    ).astype(jnp.bfloat16)
    slope = (
        jnp.einsum("xk,ikm->ixm", inverse_x, coef_x, preferred_element_type=jnp.float32) / full_rows
    ).astype(jnp.bfloat16)
    slope_x = lax.all_to_all(slope, "pencil", split_axis=1, concat_axis=2, tiled=True)
    slope_x = slope_x.reshape(row_count, plane_count, y_count)
    slope_z = (jnp.roll(warped_f, -1, axis=1) - jnp.roll(warped_f, 1, axis=1)) * 0.5
    force = (jnp.stack([slope_x.astype(jnp.float32), slope_y, slope_z]) * residual[None]).astype(
        jnp.bfloat16
    )
    force_lines = force.reshape(-1, y_count)
    spec_real = jnp.dot(force_lines, cos_y, preferred_element_type=jnp.float32).astype(jnp.bfloat16)
    spec_imag = jnp.dot(force_lines, -sin_y, preferred_element_type=jnp.float32).astype(
        jnp.bfloat16
    )
    spec_f = jnp.stack(
        [spec_real.reshape(3, row_count, cell_count), spec_imag.reshape(3, row_count, cell_count)],
        axis=1,
    )
    planes = lax.all_to_all(spec_f, "pencil", split_axis=3, concat_axis=2, tiled=True)
    local_cols = planes.shape[3]
    column_ids = my_index * local_cols + jnp.arange(local_cols, dtype=jnp.int32)
    kvec_local = signed_waves(column_ids % y_count, y_count)
    spectral_gain = force_gain / (
        full_rows
        * y_count
        * (
            1.0
            + h1_weight
            * (kvec_x[:, None] * kvec_x[:, None] + kvec_local[None, :] * kvec_local[None, :])
        )
    )
    cos_part = jnp.einsum("kx,chxm->chkm", cos_x, planes, preferred_element_type=jnp.float32)
    sin_part = jnp.einsum("kx,chxm->chkm", sin_x, planes, preferred_element_type=jnp.float32)
    real_f = cos_part[:, 0] + sin_part[:, 1]
    imag_f = cos_part[:, 1] - sin_part[:, 0]
    scale_grid = spectral_gain[None]
    scaled = jnp.stack([real_f * scale_grid, imag_f * scale_grid], axis=1).astype(jnp.bfloat16)
    cos_back = jnp.einsum("xk,chkm->chxm", cos_x, scaled, preferred_element_type=jnp.float32)
    sin_back = jnp.einsum("xk,chkm->chxm", sin_x, scaled, preferred_element_type=jnp.float32)
    real_b = cos_back[:, 0] - sin_back[:, 1]
    imag_b = cos_back[:, 1] + sin_back[:, 0]
    mixed = jnp.stack([real_b, imag_b], axis=1).astype(jnp.bfloat16)
    smoothed = lax.all_to_all(mixed, "pencil", split_axis=2, concat_axis=3, tiled=True)
    spatial = jnp.dot(
        smoothed[:, 0].reshape(-1, y_count), cos_y, preferred_element_type=jnp.float32
    )
    spatial = spatial - jnp.dot(
        smoothed[:, 1].reshape(-1, y_count), sin_y, preferred_element_type=jnp.float32
    )
    gradient = velocity + spatial.reshape(3, row_count, plane_count, y_count)
    return (warped, gradient)


def split_pair(values):
    high = values.astype(jnp.bfloat16)
    low = (values - np.asarray(high, np.float64)).astype(jnp.bfloat16)
    return [high, low]


def real_dft(length):
    half = length // 2
    waves = np.concatenate([np.arange(half + 1), np.arange(1, half)])
    angle = 2.0 * np.pi * ((np.arange(length)[:, None] * waves[None, :]) % length) / length
    table = np.where(np.arange(length)[None, :] <= half, np.cos(angle), np.sin(angle))
    factor = np.where((waves == 0) | (waves == half), 1.0, 2.0)
    k = np.where(waves == half, 0, waves) * (2.0 * np.pi / length)
    return table, (table * factor[None, :]).T, k


def derivative(length):
    series = np.arange(length)
    angle = 2.0 * np.pi * ((series[:, None] * series[None, :]) % length) / length
    cos, sin = np.cos(angle), np.sin(angle)
    k = np.where(series < length // 2, series, series - length)
    k = np.where(series == length // 2, 0, k) * (2.0 * np.pi / length)
    return ((sin * k) @ cos - (cos * k) @ sin) / length


@functools.lru_cache(None)
def tables(n, rows, planes, ny):
    nx = n * rows
    m = nx * ZB
    index = np.arange(m)
    line_x = index // (ZB * rows) * rows + index % rows
    line_z = index // rows % ZB
    wide = np.arange(2 * m)
    wide_dev = wide // (2 * ZB * rows)
    wide_half = wide // (ZB * rows) % 2
    wide_z = wide // rows % ZB
    wide_row = wide % rows
    slab = wide_half * m + wide_row * planes + wide_dev * ZB + wide_z
    eye = np.eye(2 * m)
    to_message = eye[slab]
    from_message = eye[slab].T
    wide_x = wide_dev * rows + wide_row
    first_x = [
        np.where(
            (line_z[:, None] == wide_z[None, :]) & (wide_half == h)[None, :],
            wide_x[None, :],
            8 * nx,
        )
        for h in range(2)
    ]
    second_x = np.where(line_z[:, None] == line_z[None, :], line_x[None, :], 8 * nx)
    same_z = line_z[:, None] == line_z[None, :]
    dx = derivative(nx)[line_x[None, :], line_x[:, None]] * same_z
    dy = derivative(ny)
    plane_last = np.zeros((nx, m))
    plane_first = np.zeros((nx, m))
    plane_last[line_x[line_z == ZB - 1], index[line_z == ZB - 1]] = 1.0
    plane_first[line_x[line_z == 0], index[line_z == 0]] = 1.0
    dz = np.zeros((m, 2 * m))
    for r in range(m):
        x, z = line_x[r], line_z[r]
        for step, sign in ((1, 0.5), (-1, -0.5)):
            if z + step < 0:
                column = m + x
            elif z + step >= ZB:
                column = m + nx + x
            else:
                column = int(np.nonzero((line_x == x) & (line_z == z + step))[0][0])
            dz[r, column] += sign
    fx, bx, kx = real_dft(nx)
    fy, by, ky = real_dft(ny)
    out_z = index // nx
    out_k = index % nx
    forward = fx.T[out_k][:, line_x] * (out_z[:, None] == line_z[None, :])
    backward = bx.T[line_x][:, out_k] * (line_z[:, None] == out_z[None, :])
    gain = force_gain / (
        nx * ny * (1.0 + h1_weight * (kx[out_k][:, None] ** 2 + ky[None, :] ** 2))
    )
    per = ny // SEG
    groups = planes // ZB
    lanes = np.arange(rows * groups * per)
    lane_row = lanes // (groups * per)
    lane_group = lanes // per % groups
    code_mask = np.arange(n)[:, None] == lane_group[None, :]
    code_spread = np.zeros((4, lanes.size, 128))
    for j in range(4):
        code_spread[j, lanes, (lane_row * 4 + j) * per + lanes % per] = 1.0
    code_lines = index[:, None] // (ZB * rows) == np.arange(n)[None, :]
    out = np.arange(128)
    code_rows = (out[None, :] // (4 * per)) == (index % rows)[:, None]
    code_fold = (out[:, None] % (4 * per) == out[None, :]) & (out[:, None] < rows * 4 * per)
    b16 = lambda t: np.asarray(t, np.float64).astype(jnp.bfloat16)
    f32 = lambda t: np.asarray(t, np.float32)
    return {
        "early": b16(to_message),
        "mask": f32(code_mask),
        "lay": b16(code_lines),
        "fold": b16(np.concatenate([code_rows, code_fold])),
        "spread": b16(code_spread),
        "first": f32(first_x),
        "second": f32(second_x),
        "dz": b16(dz),
        "ends": b16(np.concatenate([plane_last, plane_first])),
        "dx": np.concatenate(split_pair(dx)),
        "dy": np.concatenate(split_pair(dy)),
        "x": b16(np.concatenate([forward, backward])),
        "fy": b16(fy),
        "by": b16(by),
        "gain": f32(gain),
    }, b16(to_message.T)


def dot(a, b):
    return jnp.dot(a, b, preferred_element_type=jnp.float32)


def body(n, names, template_hbm, image_hbm, owner_hbm, offset_hbm, level_hbm, *refs):
    tables_hbm = refs[: len(names)]
    (back_recv,) = refs[len(names) : len(names) + 1]
    refs = refs[len(names) + 1 :]
    template_ref, image_ref, owner_ref, offset_ref, level_ref = refs[:5]
    table = dict(zip(names, refs[5 : 5 + len(names)]))
    (
        code_send,
        code_recv,
        image_send,
        image_recv,
        halo_send,
        halo_recv,
        back_send,
        load_sems,
        code_sems,
        image_sems,
        halo_sems,
        back_sems,
        own_sems,
    ) = refs[5 + len(names) :]
    sources = (template_hbm, image_hbm, owner_hbm, offset_hbm, level_hbm) + tables_hbm
    targets = refs[: 5 + len(names)]
    loads = {
        key: pltpu.make_async_copy(source, target, load_sems.at[at])
        for at, (key, source, target) in enumerate(
            zip(("template", "image", "owner", "offset", "level") + names, sources, targets)
        )
    }
    order = ("template", "early", "owner", "offset", "level", "spread", "mask", "image", "lay", "fold")
    for key in order + tuple(key for key in names if key not in order):
        loads[key].start()

    def loaded(*keys):
        for key in keys:
            loads[key].wait()

    me = lax.axis_index("pencil")
    rows, planes, ny = template_ref.shape
    m = n * rows * ZB
    nx = n * rows
    per = ny // SEG
    half = ny // 2
    each = ZB * rows
    core = lax.axis_index("start")

    def flip(at):
        return at + lax.rem(core, 2) * (1 - 2 * lax.rem(at, 2))

    group = flip(me)
    after = flip(lax.rem(group + 1, n))
    before = flip(lax.rem(group + n - 1, n))

    barrier = pltpu.get_barrier_semaphore()
    partners = [
        lax.rem(me + off, n) for off in sorted(range(1, n), key=lambda off: abs(off - n // 2))
    ]
    for to in partners:
        pl.semaphore_signal(
            barrier, inc=1, device_id={"pencil": to}, device_id_type=pl.DeviceIdType.MESH
        )

    to_groups = [(to, flip(to), me) for to in partners]
    to_homes = [(to, to, group) for to in partners]

    def scatter(send, recv, sems, ways):
        for to, part, place in ways:
            pltpu.make_async_remote_copy(
                src_ref=send.at[part],
                dst_ref=recv.at[place],
                send_sem=sems.at[0],
                recv_sem=sems.at[1],
                device_id={"pencil": to},
                device_id_type=pl.DeviceIdType.MESH,
            ).start()

    def everything(send, recv, sems):
        return pltpu.make_async_remote_copy(
            src_ref=send.at[pl.ds(0, n - 1)],
            dst_ref=recv.at[pl.ds(0, n - 1)],
            send_sem=sems.at[0],
            recv_sem=sems.at[1],
            device_id={"pencil": after},
            device_id_type=pl.DeviceIdType.MESH,
        )

    def collect(send, recv, sems):
        everything(send, recv, sems).wait_recv()

    def drain(send, recv, sems):
        everything(send, recv, sems).wait_send()

    def sort_image(slot, ref):
        value = ref[...].reshape(m, ny)
        stacked = jnp.concatenate([value[:, :half], value[:, half:]], axis=0)
        message = dot(table["early"][...], stacked).astype(jnp.bfloat16)
        image_send[slot] = message.reshape(n, 2 * ZB * rows, half)

    loaded("template", "early")
    sort_image(0, template_ref)
    loaded("owner", "offset", "level", "spread", "mask")
    shift = (planes // ZB * per).bit_length() - 1
    base = owner_ref[...] * rows + lax.shift_right_logical(
        offset_ref[...], jnp.full(offset_ref.shape, shift, jnp.int32)
    )
    base = base.astype(jnp.float32)
    level = level_ref[...].astype(jnp.float32)
    codes = jnp.zeros((n, 128), jnp.float32)
    for j, line in enumerate((base[0:1], base[1:2], level[0:1], level[1:2])):
        codes += dot((table["mask"][...] * line).astype(jnp.bfloat16), table["spread"][j])
    code_send[...] = codes.reshape(n, 1, 128)
    pl.semaphore_wait(barrier, n - 1)
    scatter(code_send, code_recv, code_sems, to_groups)
    scatter(image_send.at[0], image_recv.at[0], image_sems.at[0], to_groups)
    code_recv[me] = code_send[group]
    image_recv[0, me] = image_send[0, group]
    loaded("image")
    sort_image(1, image_ref)
    scatter(image_send.at[1], image_recv.at[1], image_sems.at[1], to_groups)
    image_recv[1, me] = image_send[1, group]

    collect(code_send, code_recv, code_sems)
    loaded("lay", "fold")
    code = dot(table["lay"][...], code_recv[...].reshape(n, 128).astype(jnp.bfloat16))
    code = (code * table["fold"][:m].astype(jnp.float32)).astype(jnp.bfloat16)
    code = dot(code, table["fold"][m:])
    t = (code + 0.5) / Q
    weights = (
        -t * (t - 1.0) * (t - 2.0) / 6.0,
        (t + 1.0) * (t - 1.0) * (t - 2.0) / 2.0,
        -(t + 1.0) * t * (t - 2.0) / 2.0,
        (t + 1.0) * t * (t - 1.0) / 6.0,
    )

    def stencil(section, group, place):
        at = section * per + group
        delta = place - code[:, at : at + 1]
        delta = jnp.where(delta < 0.0, delta + nx, delta)
        at = 2 * per + at
        taps = jnp.zeros_like(delta)
        for k in range(4):
            taps = jnp.where(delta == float(k), weights[k][:, at : at + 1], taps)
        return taps.astype(jnp.bfloat16)

    loaded("first", "second")
    first = [stencil(0, g, table["first"][g * SEG // half]) for g in range(per)]
    second = [stencil(1, g, table["second"][...]) for g in range(per)]
    collect(image_send.at[0], image_recv.at[0], image_sems.at[0])
    template = image_recv[0].reshape(2 * m, half)
    warped = []
    for g in range(per):
        at = g * SEG % half
        seg = template[:, at : at + SEG]
        seg = dot(first[g], seg).astype(jnp.bfloat16)
        warped.append(dot(second[g], seg).astype(jnp.bfloat16))
    warped = jnp.concatenate(warped, axis=1)
    warped_f = warped.astype(jnp.float32)

    loaded("ends", "dz")
    halo_send[...] = dot(table["ends"][...], warped).astype(jnp.bfloat16).reshape(2, nx, ny)
    halos = [
        pltpu.make_async_remote_copy(
            src_ref=halo_send.at[side],
            dst_ref=halo_recv.at[side],
            send_sem=halo_sems.at[0, side],
            recv_sem=halo_sems.at[1, side],
            device_id={"pencil": (after, before)[side]},
            device_id_type=pl.DeviceIdType.MESH,
        )
        for side in range(2)
    ]
    for halo in halos:
        halo.start()

    def own(slot):
        return pltpu.make_async_copy(
            back_send.at[slot, me], back_recv.at[slot, group], own_sems.at[slot]
        )

    def send_back(slot, value):
        for h in range(2):
            part = value[:, h * half : (h + 1) * half].reshape(n, each, half)
            back_send[slot, :, h * each : (h + 1) * each, :] = part.astype(jnp.bfloat16)
        scatter(back_send.at[slot], back_recv.at[slot], back_sems.at[slot], to_homes)
        own(slot).start()

    send_back(0, warped_f)
    loaded("dx", "dy", "x", "fy", "by", "gain")
    slope_x = dot(table["dx"][:m], warped) + dot(table["dx"][m:], warped)
    slope_y = dot(warped, table["dy"][:ny]) + dot(warped, table["dy"][ny:])
    collect(image_send.at[1], image_recv.at[1], image_sems.at[1])
    image = [
        image_recv[1, :, h * each : (h + 1) * each, :].astype(jnp.float32).reshape(m, half)
        for h in range(2)
    ]
    residual = jnp.concatenate(image, axis=1) - warped_f

    def smooth(slot, slope):
        force = (slope * residual).astype(jnp.bfloat16)
        spectrum = dot(force, table["fy"][...]).astype(jnp.bfloat16)
        spectrum = dot(table["x"][:m], spectrum) * table["gain"][...]
        spectrum = dot(table["x"][m:], spectrum.astype(jnp.bfloat16)).astype(jnp.bfloat16)
        send_back(slot, dot(spectrum, table["by"][...]))

    smooth(1, slope_x)
    smooth(2, slope_y)
    for halo in halos:
        halo.wait_recv()
    near = jnp.concatenate([warped, halo_recv[0], halo_recv[1]], axis=0)
    smooth(3, dot(table["dz"][...], near))

    drain(code_send, code_recv, code_sems)
    for slot in range(2):
        drain(image_send.at[slot], image_recv.at[slot], image_sems.at[slot])
    for halo in halos:
        halo.wait_send()
    for slot in range(4):
        own(slot).wait()
        collect(back_send.at[slot], back_recv.at[slot], back_sems.at[slot])
        drain(back_send.at[slot], back_recv.at[slot], back_sems.at[slot])


def finish(
    back_ref,
    velocity_ref,
    sort_ref,
    warped_hbm,
    gradient_hbm,
    warped_ref,
    gradient_ref,
    store_sems,
):
    rows, planes, ny = warped_ref.shape
    m = rows * planes
    stores = [pltpu.make_async_copy(warped_ref, warped_hbm, store_sems.at[0])] + [
        pltpu.make_async_copy(gradient_ref.at[c], gradient_hbm.at[c], store_sems.at[1 + c])
        for c in range(3)
    ]
    for slot in (1, 2, 3, 0):
        home = dot(sort_ref[...], back_ref[slot].reshape(2 * m, ny // 2))
        home = jnp.concatenate([home[:m], home[m:]], axis=1).reshape(rows, planes, ny)
        if slot == 0:
            warped_ref[...] = home.astype(jnp.bfloat16)
        else:
            gradient_ref[slot - 1] = velocity_ref[slot - 1] + home
        stores[slot].start()
    for store in stores:
        store.wait()


def by_groups(template, reference_image, velocity, dep_owner, dep_offset, dep_weight):
    n = lax.axis_size("pencil")
    rows, planes, ny = template.shape
    m = n * rows * ZB
    held, sort_rows = tables(n, rows, planes, ny)
    names = tuple(held)
    constants = [jnp.asarray(held[name]) for name in names]
    operands = (template, reference_image, dep_owner, dep_offset, dep_weight, *constants)
    b16, f32 = jnp.bfloat16, jnp.float32
    message = (n, 2 * ZB * rows, ny // 2)
    hbm = pl.BlockSpec(memory_space=pltpu.HBM)
    back = pl.pallas_call(
        functools.partial(body, n, names),
        out_shape=jax.ShapeDtypeStruct((4,) + message, b16),
        in_specs=[hbm] * len(operands),
        out_specs=hbm,
        scratch_shapes=[pltpu.VMEM(array.shape, array.dtype) for array in operands]
        + [
            pltpu.VMEM((n, 1, 128), f32),
            pltpu.VMEM((n, 1, 128), f32),
            pltpu.VMEM((2,) + message, b16),
            pltpu.VMEM((2,) + message, b16),
            pltpu.VMEM((2, n * rows, ny), b16),
            pltpu.VMEM((2, n * rows, ny), b16),
            pltpu.VMEM((4,) + message, b16),
            pltpu.SemaphoreType.DMA((len(operands),)),
            pltpu.SemaphoreType.DMA((2,)),
            pltpu.SemaphoreType.DMA((2, 2)),
            pltpu.SemaphoreType.DMA((2, 2)),
            pltpu.SemaphoreType.DMA((4, 2)),
            pltpu.SemaphoreType.DMA((4,)),
        ],
        compiler_params=pltpu.CompilerParams(
            collective_id=0, has_side_effects=True, vmem_limit_bytes=60 * 1024 * 1024
        ),
        cost_estimate=pl.CostEstimate(
            flops=24 * m * ny * ny, bytes_accessed=8 * m * ny * 4, transcendentals=0
        ),
    )(*operands)
    return pl.pallas_call(
        finish,
        out_shape=(
            jax.ShapeDtypeStruct(template.shape, b16),
            jax.ShapeDtypeStruct(velocity.shape, f32),
        ),
        in_specs=[pl.BlockSpec(memory_space=pltpu.VMEM)] * 3,
        out_specs=(hbm, hbm),
        scratch_shapes=[
            pltpu.VMEM(template.shape, b16),
            pltpu.VMEM(velocity.shape, f32),
            pltpu.SemaphoreType.DMA((4,)),
        ],
        compiler_params=pltpu.CompilerParams(vmem_limit_bytes=12 * 1024 * 1024),
        cost_estimate=pl.CostEstimate(
            flops=16 * m * m * ny, bytes_accessed=4 * m * ny * 8, transcendentals=0
        ),
    )(back, velocity, jnp.asarray(sort_rows))


def local(template, *others):
    n = lax.axis_size("pencil")
    rows, planes, ny = template.shape
    per_row = planes // ZB * (ny // SEG)
    whole = planes == n * ZB and ny % (2 * SEG) == 0 and per_row & (per_row - 1) == 0
    if n > 2 and n % 2 == 0 and 4 * rows * (ny // SEG) <= 128 and whole and rows * ZB == 8 and n * rows <= 256:
        return by_groups(template, *others)
    return general(template, *others)


def solution(mesh):
    in_specs = (
        P("pencil", "start", None),
        P("pencil", "start", None),
        P("start", "pencil", None, None),
        P("start", "pencil"),
        P("start", "pencil"),
        P("start", "pencil"),
    )
    out_specs = (P("pencil", "start", None), P("start", "pencil", None, None))
    return jax.shard_map(local, mesh=mesh, in_specs=in_specs, out_specs=out_specs, check_vma=False)
```
